128 devices in a mesh: img: 16 (over z, x_lo, core), seq: 4 (over y), col: 2 (over x_hi).
Axes of the slice: x: 4 (x_hi: 2, x_lo: 2; x = x_hi * 2 + x_lo), y: 4, z: 4, core: 2. Of those that a mesh axis runs over, the one named last changes fastest.
Arguments:
- images: bfloat16 [16, 112, 56, 512], P('img', 'seq', 'col'), may hold values from -6 to 6
- out_grad: bfloat16 [16, 112, 56, 512], P('img', 'seq', 'col'), may hold values from -6 to 6
- region_ids: int32 [112, 56], P(None, 'col'), may hold values from 0 to 3
- rel_index: int32 [49, 49], replicated, may hold values from 0 to 168
- qkv_weight: float32 [2, 512, 1536], P(None, ('img', 'col')), may hold values from -0.25 to 0.25
- qkv_first: float32 [2, 512, 1536], P(None, ('img', 'col')), may hold values from -160 to 160
- qkv_second: float32 [2, 512, 1536], P(None, ('img', 'col')), may hold values from 64.22528 to 256.90112
- proj_weight: float32 [2, 512, 512], P(None, ('img', 'col')), may hold values from -0.75 to 0.75
- proj_first: float32 [2, 512, 512], P(None, ('img', 'col')), may hold values from -112 to 112
- proj_second: float32 [2, 512, 512], P(None, ('img', 'col')), may hold values from 25.088 to 100.352
- expand_weight: float32 [2, 512, 2048], P(None, ('img', 'col')), may hold values from -0.25 to 0.25
- expand_first: float32 [2, 512, 2048], P(None, ('img', 'col')), may hold values from -80 to 80
- expand_second: float32 [2, 512, 2048], P(None, ('img', 'col')), may hold values from 16.05632 to 64.22528
- contract_weight: float32 [2, 2048, 512], P(None, ('img', 'col')), may hold values from -0.125 to 0.125
- contract_first: float32 [2, 2048, 512], P(None, ('img', 'col')), may hold values from -160 to 160
- contract_second: float32 [2, 2048, 512], P(None, ('img', 'col')), may hold values from 49.17248 to 196.68993
- small_params: float32 [2, 6144], replicated, may hold values from -1 to 1.5, as said below
- small_first: float32 [2, 6144], replicated, may hold values from -160 to 160
- small_second: float32 [2, 6144], replicated, may hold values from 30.1056 to 301.056
- bias_table: float32 [2, 169, 16], replicated, may hold values from -4 to 4
- table_first: float32 [2, 169, 16], replicated, may hold values from -160 to 160
- table_second: float32 [2, 169, 16], replicated, may hold values from 20.0704 to 200.704
Outputs:
- activations: bfloat16 [16, 112, 56, 512], P('img', 'seq', 'col')
- input_grad: float32 [16, 112, 56, 512], P('img', 'seq', 'col')
- qkv_moment: float32 [2, 512, 1536], P(None, ('img', 'col'))
- qkv_variance: float32 [2, 512, 1536], P(None, ('img', 'col'))
- qkv_updated: float32 [2, 512, 1536], P(None, ('img', 'col'))
- proj_moment: float32 [2, 512, 512], P(None, ('img', 'col'))
- proj_variance: float32 [2, 512, 512], P(None, ('img', 'col'))
- proj_updated: float32 [2, 512, 512], P(None, ('img', 'col'))
- expand_moment: float32 [2, 512, 2048], P(None, ('img', 'col'))
- expand_variance: float32 [2, 512, 2048], P(None, ('img', 'col'))
- expand_updated: float32 [2, 512, 2048], P(None, ('img', 'col'))
- contract_moment: float32 [2, 2048, 512], P(None, ('img', 'col'))
- contract_variance: float32 [2, 2048, 512], P(None, ('img', 'col'))
- contract_updated: float32 [2, 2048, 512], P(None, ('img', 'col'))
- small_moment: float32 [2, 6144], replicated
- small_variance: float32 [2, 6144], replicated
- small_updated: float32 [2, 6144], replicated
- table_moment: float32 [2, 169, 16], replicated
- table_variance: float32 [2, 169, 16], replicated
- table_updated: float32 [2, 169, 16], replicated
- bias_gradient: float32 [2, 512], replicated
The draws below stay inside these ranges and needn't reach their ends.
Inputs may be any that keep to these rules, and one draw needn't show every extreme that they name: `region_ids`: in the shifted layer a query attends only the keys of its window whose cell carries its region id. `rel_index`: row of the bias table used for query position i and key position j of every window. `small_params`: per layer the norms' gains lie near one and the biases take both signs.
All inputs are finite; a program needn't handle non-finite values.
Results may differ from the reference program's by a relative error of at most 0.035.
Values may be sent and summed in bfloat16 or wider, within the bound.
No kernel may reach another device: no remote copies, remote signals or barrier semaphores. Data moves between devices by JAX's collectives and lax.ppermute only.
A program may use at most 256 MiB of HBM per device.

```python
import math
import jax
import jax.numpy as jnp
from jax import lax

D = 512
HEADS = 16
HEAD_DIM = 32
MLP = 2048
WIN = 7
SHIFT = 3
LAYERS = 2
STEP = 10
ROWS = 112
COLS = 56
IMAGES = 16
TOKENS = 100352
REL = 169
SMALL = 6144


def draw_small_params(key, part):
    key = jax.random.fold_in(key, 11)
    position = jnp.arange(SMALL)
    is_gain = ((position < D) | (position >= 5 * D) & (position < 6 * D))[None, :]
    raw_draw = jnp.clip(jax.random.normal(key, (LAYERS, SMALL), jnp.float32), -3.0, 3.0)
    return jnp.where(is_gain, 1.0 + 0.15 * raw_draw, 0.3 * raw_draw)


def set_ends(values, own_key, least, high):
    place = [jax.random.randint(jax.random.fold_in(own_key, axis), (), 0, length) for axis, length in enumerate(values.shape)]
    widest = values.shape.index(max(values.shape))
    next_to = place[:widest] + [(place[widest] + 1) % values.shape[widest]] + place[widest + 1:]
    return values.at[tuple(place)].set(least).at[tuple(next_to)].set(high)


def block_scale(key, shape, cuts, low, high):
    level = 1.0
    for axis_at, blocks in cuts:
        heights = jax.random.uniform(jax.random.fold_in(jax.random.fold_in(key, 6), axis_at), (blocks,), jnp.float32, low / len(cuts), high / len(cuts))
        level = level * jnp.repeat(jnp.exp(heights), shape[axis_at] // blocks).reshape((-1,) + (1,) * (len(shape) - 1 - axis_at))
    return level


def gaussian(key, shape, scale, reach, shards=(), dtype=jnp.bfloat16):
    drawn = jax.random.normal(key, shape, jnp.float32) * scale
    if len(shards) > 0:
        drawn = block_scale(key, shape, shards, -0.22, 0.18) * drawn
    return jnp.clip(drawn, min=-reach, max=reach).astype(dtype)


def setup_inputs(seed: int = 0) -> dict:
    splits = jax.random.split(jax.random.key(seed), 23)
    images = gaussian(splits[0], (IMAGES, ROWS, COLS, D), 1.0, 6.0, ((0, 16), (1, 4), (2, 2)))
    out_grad = gaussian(splits[1], (IMAGES, ROWS, COLS, D), 1.0, 6.0, ((0, 16), (1, 4), (2, 2)))
    region_ids = set_ends(jax.random.randint(splits[2], (ROWS, COLS), 0, 4), jax.random.fold_in(splits[2], 1), 0, 3).astype(jnp.int32)
    rel_index = set_ends(jax.random.randint(splits[3], (WIN * WIN, WIN * WIN), 0, REL), jax.random.fold_in(splits[3], 1), 0, REL - 1).astype(jnp.int32)
    qkv_weight = gaussian(splits[4], (LAYERS, D, 3 * D), D ** -0.5, 0.25, ((1, 32),), jnp.float32)
    qkv_first = gaussian(splits[5], (LAYERS, D, 3 * D), (0.09 * TOKENS ** 0.5), 160.0, ((1, 32),), jnp.float32)
    qkv_second = jnp.clip(jnp.exp(math.log(256.90112) - 1.3862944 * jax.random.uniform(splits[6], (LAYERS, D, 3 * D), jnp.float32) ** block_scale(splits[6], (LAYERS, D, 3 * D), ((1, 32),), -0.2, 0.2)), 64.22528, 256.90112)
    proj_weight = gaussian(splits[7], (LAYERS, D, D), (D // 9) ** -0.5, 0.75, ((1, 32),), jnp.float32)
    proj_first = gaussian(splits[8], (LAYERS, D, D), (0.056 * TOKENS ** 0.5), 112.0, ((1, 32),), jnp.float32)
    proj_second = jnp.clip(jnp.exp(math.log(100.352) - 1.3862944 * jax.random.uniform(splits[9], (LAYERS, D, D), jnp.float32) ** block_scale(splits[9], (LAYERS, D, D), ((1, 32),), -0.2, 0.2)), 25.088, 100.352)
    expand_weight = gaussian(splits[10], (LAYERS, D, MLP), D ** -0.5, 0.25, ((1, 32),), jnp.float32)
    expand_first = gaussian(splits[11], (LAYERS, D, MLP), (0.044 * TOKENS ** 0.5), 80.0, ((1, 32),), jnp.float32)
    expand_second = jnp.clip(jnp.exp(math.log(64.22528) - 1.3862944 * jax.random.uniform(splits[12], (LAYERS, D, MLP), jnp.float32) ** block_scale(splits[12], (LAYERS, D, MLP), ((1, 32),), -0.2, 0.2)), 16.05632, 64.22528)
    contract_weight = gaussian(splits[13], (LAYERS, MLP, D), MLP ** -0.5, 0.125, ((1, 32),), jnp.float32)
    contract_first = gaussian(splits[14], (LAYERS, MLP, D), (0.078 * TOKENS ** 0.5), 160.0, ((1, 32),), jnp.float32)
    contract_second = jnp.clip(jnp.exp(math.log(196.68993) - 1.3862944 * jax.random.uniform(splits[15], (LAYERS, MLP, D), jnp.float32) ** block_scale(splits[15], (LAYERS, MLP, D), ((1, 32),), -0.2, 0.2)), 49.17248, 196.68993)
    small_params = draw_small_params(jax.random.fold_in(splits[22], 71), 0)
    small_first = gaussian(splits[17], (LAYERS, SMALL), (0.09 * TOKENS ** 0.5), 160.0, (), jnp.float32)
    small_second = jnp.clip(jnp.exp(jax.random.uniform(splits[18], (LAYERS, SMALL), jnp.float32, math.log(30.1056), math.log(301.056))), 30.1056, 301.056)
    bias_table = gaussian(splits[19], (LAYERS, REL, HEADS), 0.8, 4.0, (), jnp.float32)
    table_first = gaussian(splits[20], (LAYERS, REL, HEADS), (0.078 * TOKENS ** 0.5), 160.0, (), jnp.float32)
    table_second = jnp.clip(jnp.exp(jax.random.uniform(splits[21], (LAYERS, REL, HEADS), jnp.float32, math.log(20.0704), math.log(200.704))), 20.0704, 200.704)
    return {"images": images, "out_grad": out_grad, "region_ids": region_ids, "rel_index": rel_index, "qkv_weight": qkv_weight, "qkv_first": qkv_first, "qkv_second": qkv_second, "proj_weight": proj_weight, "proj_first": proj_first, "proj_second": proj_second, "expand_weight": expand_weight, "expand_first": expand_first, "expand_second": expand_second, "contract_weight": contract_weight, "contract_first": contract_first, "contract_second": contract_second, "small_params": small_params, "small_first": small_first, "small_second": small_second, "bias_table": bias_table, "table_first": table_first, "table_second": table_second}


@jax.custom_vjp
def low(v):
    return lax.optimization_barrier(v.astype(jnp.bfloat16)).astype(jnp.float32)

@jax.custom_vjp
def low_back(v):
    return v

def low_keep(v):
    return (low(v), None)

def low_pass(kept, grad):
    return (grad,)

def back_keep(v):
    return (v, None)

def back_low(kept, grad):
    return (low(grad),)
low.defvjp(low_keep, low_pass)
low_back.defvjp(back_keep, back_low)
norm_epsilon = 1e-05
masked_score = -1000000000.0
highest = lax.Precision.HIGHEST

def layer_norm(values_in, gain_row, bias_row):
    centred = values_in - lax.optimization_barrier(jnp.mean(values_in, -1, keepdims=True))
    variance = lax.optimization_barrier(jnp.mean(centred * centred, -1, keepdims=True))
    return centred * lax.rsqrt(variance + norm_epsilon) * gain_row + bias_row

def split_small(vector):
    pieces = [vector[piece_index * D:(piece_index + 1) * D] for piece_index in range(8)]
    return pieces + [vector[8 * D:]]

def image_forward(image, params, region_ids, rel_index):
    qkv_weight, proj_weight, expand_weight, contract_weight, small_params, bias_table = params
    resid = image
    for layer_index in range(LAYERS):
        shifted = layer_index % 2 == 1
        gain_one, bias_one, query_bias, value_bias, proj_bias, gain_two, bias_two, out_bias, hidden_bias = split_small(small_params[layer_index])
        normed = low(layer_norm(resid, gain_one, bias_one))
        if shifted:
            normed = jnp.roll(normed, (-SHIFT, -SHIFT), (0, 1))
        head_rows = query_bias.reshape(HEADS, HEAD_DIM)
        qkv_bias = jnp.stack([head_rows, jnp.zeros_like(head_rows), value_bias.reshape(HEADS, HEAD_DIM)], 1).reshape(3 * D)
        projected = jnp.dot(normed.reshape(-1, D), low(qkv_weight[layer_index]), precision=highest) + qkv_bias
        projected = low_back(low(projected))
        grid = projected.reshape(ROWS // WIN, WIN, COLS // WIN, WIN, HEADS, 3, HEAD_DIM)
        grid = grid.transpose(0, 2, 4, 5, 1, 3, 6).reshape(ROWS // WIN, COLS // WIN, HEADS, 3, WIN * WIN, HEAD_DIM)
        queries, key_rows, value_rows = (grid[:, :, :, 0], grid[:, :, :, 1], grid[:, :, :, 2])
        scores = jnp.einsum('abhid,abhjd->abhij', queries, key_rows, precision=highest) * HEAD_DIM ** (-0.5)
        scores = scores + jnp.transpose(bias_table[layer_index][rel_index], (2, 0, 1))
        if shifted:
            region_win = region_ids.reshape(ROWS // WIN, WIN, COLS // WIN, WIN).transpose(0, 2, 1, 3)
            region_win = region_win.reshape(ROWS // WIN, COLS // WIN, WIN * WIN)
            allowed = region_win[:, :, :, None] == region_win[:, :, None, :]
            scores = jnp.where(allowed[:, :, None], scores, masked_score)
        scores = low_back(scores)
        attn_weights = low(jax.nn.softmax(scores, -1))
        context = jnp.einsum('abhij,abhjd->abhid', attn_weights, value_rows, precision=highest)
        context = low_back(low(context))
        context = context.reshape(ROWS // WIN, COLS // WIN, HEADS, WIN, WIN, HEAD_DIM)
        context = context.transpose(0, 3, 1, 4, 2, 5).reshape(ROWS, COLS, D)
        if shifted:
            context = jnp.roll(context, (SHIFT, SHIFT), (0, 1))
        branch = jnp.dot(context.reshape(-1, D), low(proj_weight[layer_index]), precision=highest) + proj_bias
        resid = resid + low_back(branch).reshape(ROWS, COLS, D)
        normed_two = low(layer_norm(resid, gain_two, bias_two))
        hidden_pre = low_back(jnp.dot(normed_two.reshape(-1, D), low(expand_weight[layer_index]), precision=highest) + hidden_bias)
        hidden = low(jax.nn.gelu(hidden_pre, approximate=False))
        branch = jnp.dot(hidden, low(contract_weight[layer_index]), precision=highest) + out_bias
        resid = resid + low_back(branch).reshape(ROWS, COLS, D)
    return resid

def adamw(weight, first, second, grad, rate, decay):
    first = 0.9 * first + 0.1 * grad
    second = 0.999 * second + 0.001 * grad * grad
    first_hat = first / (1.0 - 0.9 ** STEP)
    second_hat = second / (1.0 - 0.999 ** STEP)
    return (first, second, weight - rate * (first_hat / (jnp.sqrt(second_hat) + 1e-08) + decay * weight))

def reference(images, out_grad, region_ids, rel_index, qkv_weight, qkv_first, qkv_second, proj_weight, proj_first, proj_second, expand_weight, expand_first, expand_second, contract_weight, contract_first, contract_second, small_params, small_first, small_second, bias_table, table_first, table_second):
    params = (qkv_weight, proj_weight, expand_weight, contract_weight, small_params, bias_table)
    zero_grads = jax.tree.map(jnp.zeros_like, params)

    def per_image(carry, pair):
        image, cotangent = pair

        def forward(image_in, params_in):
            return image_forward(image_in, params_in, region_ids, rel_index)
        output, back_fn = jax.vjp(forward, image.astype(jnp.float32), params)
        image_grad, param_grads = back_fn(cotangent.astype(jnp.float32))
        carry = jax.tree.map(jnp.add, carry, param_grads)
        return (carry, (output.astype(jnp.bfloat16), image_grad))
    grads, (activations, input_grad) = lax.scan(per_image, zero_grads, (images, out_grad))
    grad_qkv, grad_proj, grad_expand, grad_contract, grad_small, grad_table = grads
    qkv_new = adamw(qkv_weight, qkv_first, qkv_second, grad_qkv, 0.03, 0.05)
    proj_new = adamw(proj_weight, proj_first, proj_second, grad_proj, 0.1, 0.05)
    expand_new = adamw(expand_weight, expand_first, expand_second, grad_expand, 0.03, 0.05)
    contract_new = adamw(contract_weight, contract_first, contract_second, grad_contract, 0.03, 0.05)
    small_new = adamw(small_params, small_first, small_second, grad_small, 0.3, 0.0)
    table_new = adamw(bias_table, table_first, table_second, grad_table, 0.6, 0.0)
    bias_gradient = grad_small[:, 7 * D:8 * D]
    return (activations, input_grad, qkv_new[0], qkv_new[1], qkv_new[2], proj_new[0], proj_new[1], proj_new[2], expand_new[0], expand_new[1], expand_new[2], contract_new[0], contract_new[1], contract_new[2], small_new[0], small_new[1], small_new[2], table_new[0], table_new[1], table_new[2], bias_gradient)
```

```python
import functools
import math

import jax
import jax.numpy as jnp
import numpy as np
from jax import lax
from jax.experimental import pallas as pl
from jax.experimental.pallas import tpu as pltpu
from jax.sharding import PartitionSpec as P

D = 512
HEADS = 16
HEAD_DIM = 32
WIN = 7
SHIFT = 3
LAYERS = 2
STEP = 10
REL = 169
SIDE = 28
CELLS = SIDE * SIDE
AREA = WIN * WIN
SLOT = 64
PADDED = 16 * SLOT
PAIRS = 8
GROUPS = 4
SLAB = 96
CORNER = 16
HALO = 2 * SLAB + CORNER
HIDDEN = 4 * D

BF = jnp.bfloat16
F32 = jnp.float32
epsilon = 1e-05
log2e = math.log2(math.e)
masked_score = -1000000000.0 * log2e
padded_score = -1e30
highest = lax.Precision.HIGHEST
VMEM_BYTES = 58 * 2**20


def padded_row(r, c):
    return ((r // WIN) * 4 + c // WIN) * SLOT + (r % WIN) * WIN + c % WIN


def ahead_source(r, c):
    r, c = r + SHIFT, c + SHIFT
    if r < SIDE and c < SIDE:
        return r * SIDE + c
    if c < SIDE:
        return CELLS + (r - SIDE) * SIDE + c
    if r < SIDE:
        return CELLS + SLAB + r * SHIFT + c - SIDE
    return CELLS + 2 * SLAB + (r - SIDE) * SHIFT + c - SIDE


def back_source(r, c):
    if r >= SHIFT and c >= SHIFT:
        return padded_row(r - SHIFT, c - SHIFT)
    if c >= SHIFT:
        return PADDED + r * SIDE + c - SHIFT
    if r >= SHIFT:
        return PADDED + SLAB + (r - SHIFT) * SHIFT + c
    return PADDED + 2 * SLAB + r * SHIFT + c


def placements():
    plain = np.zeros((PADDED, CELLS), np.float32)
    ahead = np.zeros((PADDED, CELLS + HALO), np.float32)
    back = np.zeros((CELLS, PADDED + HALO), np.float32)
    take_first = np.zeros((HALO, CELLS), np.float32)
    take_last = np.zeros((HALO, PADDED), np.float32)
    for r in range(SIDE):
        for c in range(SIDE):
            plain[padded_row(r, c), r * SIDE + c] = 1
            ahead[padded_row(r, c), ahead_source(r, c)] = 1
            back[r * SIDE + c, back_source(r, c)] = 1
    edge = SIDE - SHIFT
    for a in range(SHIFT):
        for b in range(SIDE):
            take_first[a * SIDE + b, a * SIDE + b] = 1
            take_first[SLAB + b * SHIFT + a, b * SIDE + a] = 1
            take_last[a * SIDE + b, padded_row(edge + a, b)] = 1
            take_last[SLAB + b * SHIFT + a, padded_row(b, edge + a)] = 1
        for b in range(SHIFT):
            take_first[2 * SLAB + a * SHIFT + b, a * SIDE + b] = 1
            take_last[2 * SLAB + a * SHIFT + b, padded_row(edge + a, edge + b)] = 1
    return (plain, plain.T.copy(), ahead, back, take_first, take_last)


def column_orders():
    heads = np.zeros((384, 384), np.float32)
    units = np.zeros((512, 512), np.float32)
    for n in range(4):
        for part in range(3):
            for d in range(HEAD_DIM):
                heads[n * 96 + part * 32 + d, part * 128 + n * 32 + d] = 1
    for r in range(8):
        for b in range(4):
            for i in range(16):
                units[r * 64 + b * 16 + i, b * 128 + r * 16 + i] = 1
    return heads, units


def dot(a, b):
    return lax.dot_general(a, b, (((1,), (0,)), ((), ())), preferred_element_type=F32)


def dot_nt(a, b):
    return lax.dot_general(a, b, (((1,), (1,)), ((), ())), preferred_element_type=F32)


def dot_tn(a, b):
    return lax.dot_general(a, b, (((0,), (0,)), ((), ())), preferred_element_type=F32)


def normalized(x):
    centred = x - jnp.mean(x, -1, keepdims=True)
    inverse = lax.rsqrt(jnp.mean(centred * centred, -1, keepdims=True) + epsilon)
    return centred * inverse, inverse


def norm_back(grad, x, gain):
    hat, inverse = normalized(x)
    grad_hat = grad * gain
    grad_x = inverse * (
        grad_hat
        - jnp.mean(grad_hat, -1, keepdims=True)
        - hat * jnp.mean(grad_hat * hat, -1, keepdims=True)
    )
    return grad_x, jnp.sum(grad * hat, 0, keepdims=True), jnp.sum(grad, 0, keepdims=True)


def gelu_both(u):
    a = jnp.abs(u)
    t = 1.0 / (1.0 + (0.3275911 * 0.5**0.5) * a)
    e = jnp.exp2((-0.5 * log2e) * u * u)
    poly = t * (
        0.5 * 0.254829592
        + t * (0.5 * -0.284496736 + t * (0.5 * 1.421413741 + t * (0.5 * -1.453152027 + t * (0.5 * 1.061405429))))
    )
    tail = poly * e
    phi = jnp.where(u >= 0, 1.0 - tail, tail)
    return u * phi, phi + u * e * (1.0 / math.sqrt(2 * math.pi))


def head_rows(pair):
    lane = lax.broadcasted_iota(jnp.int32, pair.shape, 1) % 128 // HEAD_DIM
    zero = jnp.zeros_like(pair)
    return jnp.concatenate([jnp.where(lane == h, pair, zero) for h in range(4)], 0)


def head_fold(rows):
    lane = lax.broadcasted_iota(jnp.int32, (SLOT, 256), 1) % 128 // HEAD_DIM
    out = rows[:SLOT]
    for h in range(1, 4):
        out = jnp.where(lane == h, rows[h * SLOT : (h + 1) * SLOT], out)
    return out


def side_by_side(ref, start, lane):
    return jnp.concatenate(
        [ref[pl.ds(start, SLOT), lane : lane + 128], ref[pl.ds(start + SLOT, SLOT), lane : lane + 128]], 1
    )


def block_diagonal(pair):
    lane = lax.broadcasted_iota(jnp.int32, pair.shape, 1)
    zero = jnp.zeros_like(pair)
    return jnp.concatenate([jnp.where(lane < 128, pair, zero), jnp.where(lane >= 128, pair, zero)], 0)


def store_diagonal(ref, start, lane, rows):
    ref[pl.ds(start, SLOT), lane : lane + 128] = rows[:SLOT, :128].astype(ref.dtype)
    ref[pl.ds(start + SLOT, SLOT), lane : lane + 128] = rows[SLOT:, 128:].astype(ref.dtype)


def call(body, outs, args, scratch=(), pieces=(), place=None, us=1, after=(), blocks=None):
    shapes = [jax.ShapeDtypeStruct(s, d) for s, d in outs]
    lead = [] if place is None else [place]
    anywhere = pl.BlockSpec(memory_space=pl.ANY)
    specs = [anywhere] * len(after)
    specs += [pl.BlockSpec(memory_space=pltpu.SMEM)] * len(lead)
    specs += [anywhere] * len(pieces)
    for i in range(len(args)):
        if blocks and i in blocks:
            shape, index = blocks[i]
            specs.append(pl.BlockSpec(shape, lambda _, at=index: at, memory_space=pltpu.VMEM))
        else:
            specs.append(pl.BlockSpec(memory_space=pltpu.VMEM))

    def whole(*refs):
        body(*refs[len(after) :])

    return pl.pallas_call(
        whole,
        grid=(1,) if blocks else (),
        out_shape=shapes,
        in_specs=specs,
        out_specs=[pl.BlockSpec(memory_space=pltpu.VMEM)] * len(shapes),
        scratch_shapes=list(scratch),
        compiler_params=pltpu.CompilerParams(vmem_limit_bytes=VMEM_BYTES),
        cost_estimate=pl.CostEstimate(flops=us * 10**9, bytes_accessed=us * 10**6, transcendentals=0),
    )(*after, *lead, *pieces, *args)


def owner_of(z, x, core):
    return z * 8 + (x // 2) * 4 + core * 2 + x % 2


def assembly(coords_ref, sets, w_ref, sems):
    z, x, core = coords_ref[0], coords_ref[1], coords_ref[2]
    copies = []
    for pieces, heavy_z, taken, first in sets:
        for k, piece in enumerate(pieces):
            for i in range(4):
                in_z, in_x = (k % 4, i) if heavy_z else (i, k % 4)
                owner = owner_of(lax.rem(z + in_z, 4), lax.bitwise_xor(x, in_x), core if k < 4 else 1 - core)
                source = piece.at[i, pl.ds(taken[0], taken[1])]
                target = w_ref.at[pl.ds(first, taken[1]), owner]
                copies.append(pltpu.make_async_copy(source, target, sems.at[len(copies)]))
    for c in copies:
        c.start()
    return copies


def block(ref, b):
    return ref[b].reshape(D, D)


def block_lanes(ref, b, lanes):
    return ref[b, :, :, lanes].reshape(D, lanes.stop - lanes.start)


def block_rows(ref, b, half):
    return ref[b, half * 16 : half * 16 + 16].reshape(256, D)


def store_grad(place_ref, keep_ref, send_ref, b, half, rows):
    first = place_ref[2] == 0
    rows = rows.astype(BF)
    for zz in range(2):
        for x in range(4):
            base = (zz * 8 + (x // 2) * 4 + x % 2) * 16
            one, two = rows[base : base + 16], rows[base + 32 : base + 48]
            keep_ref[half * 2 + zz, x, b] = jnp.where(first, one, two)
            send_ref[half * 2 + zz, x, b] = jnp.where(first, two, one)


def pack_kernel(qkv_ref, proj_ref, expand_ref, contract_ref, heads_ref, units_ref, one_ref, two_ref):
    for layer in range(LAYERS):
        at = 6 * layer
        one_ref[at + 3] = proj_ref[layer].astype(BF)
        for b in range(4):
            two_ref[at + 2 + b] = contract_ref[layer, 16 * b : 16 * b + 16, :].astype(BF)
        for g in range(GROUPS):
            lanes = slice(128 * g, 128 * g + 128)
            part = dot(qkv_ref[layer, :, 384 * g : 384 * g + 384].astype(BF), heads_ref[...]).astype(BF)
            for s in range(3):
                one_ref[at + s, :, lanes] = part[:, 128 * s : 128 * s + 128]
            part = dot(expand_ref[layer, :, 512 * g : 512 * g + 512].astype(BF), units_ref[...]).astype(BF)
            for b in range(2):
                one_ref[at + 4 + b, :, lanes] = part[:, 128 * b : 128 * b + 128]
                two_ref[at + b, :, lanes] = part[:, 256 + 128 * b : 384 + 128 * b]


def stack_kernel(*refs):
    for k in range(4):
        refs[8][k] = refs[k][6:]
        refs[9][k] = refs[4 + k][6:]


def enter_kernel(x_ref, gain_ref, bias_ref, place_ref, hp_ref):
    hat, _ = normalized(x_ref[...].astype(F32))
    h = (hat * gain_ref[...] + bias_ref[...]).astype(BF)
    hp_ref[...] = dot(place_ref[...], h).astype(BF)


def attend_kernel(shifted, *refs):
    coords_ref, pieces, refs = refs[0], refs[1:9], refs[9:]
    if shifted:
        h_ref, rows_ref, cols_ref, corner_ref, place_ref, bias_ref, table_ref, mask_ref, take_ref = refs[:9]
        w_ref, hp_ref, qkv_ref, attn_ref, ctx_ref, rows_out, cols_out, corner_out, sems = refs[9:]
        copies = assembly(coords_ref, [(pieces, True, (0, 3), 0)], w_ref, sems)
        place = place_ref[...]
        hp = dot(place[:, :CELLS], h_ref[...])
        slabs = jnp.concatenate([rows_ref[...], cols_ref[...], corner_ref[...]], 0)
        hp_ref[...] = (hp + dot(place[:, CELLS:], slabs)).astype(BF)
    else:
        hp_ref, bias_ref, table_ref, place_ref = refs[:4]
        w_ref, qkv_ref, attn_ref, ctx_ref, ctxp_ref, sems = refs[4:]
        copies = assembly(coords_ref, [(pieces, True, (0, 3), 0)], w_ref, sems)
    for c in copies:
        c.wait()
    for s in range(3):
        for half in range(2):
            lanes = slice(half * 256, half * 256 + 256)
            wide = slice(s * D + half * 256, s * D + half * 256 + 256)
            qkv_ref[:, wide] = (dot(hp_ref[...], block_lanes(w_ref, s, lanes)) + bias_ref[:, wide]).astype(BF)
    into = ctx_ref if shifted else ctxp_ref

    def one_pair(p, carry):
        start = pl.multiple_of(p * 128, 128)
        for g in range(GROUPS):
            lane = g * 128
            keys = head_rows(side_by_side(qkv_ref, start, D + lane))
            queries = block_diagonal(side_by_side(qkv_ref, start, lane))
            scores = dot_nt(keys, queries) * (HEAD_DIM**-0.5 * log2e) + table_ref[g * 256 : (g + 1) * 256, :]
            scores = scores.reshape(4, SLOT, 128)
            if shifted:
                scores = jnp.where(mask_ref[p][None] > 0, scores, masked_score)
            scores = jnp.exp2(scores - jnp.max(scores, 1, keepdims=True))
            scores = scores * (1.0 / jnp.sum(scores, 1, keepdims=True))
            attn = scores.reshape(256, 128).astype(BF)
            attn_ref[p, g] = attn
            values = head_rows(side_by_side(qkv_ref, start, 2 * D + lane))
            store_diagonal(into, start, lane, dot_tn(attn, values))
        return carry

    lax.fori_loop(0, PAIRS, one_pair, 0)
    if shifted:
        sent = dot(take_ref[...], ctx_ref[...]).astype(BF)
        rows_out[...] = sent[:SLAB]
        cols_out[...] = sent[SLAB : 2 * SLAB]
        corner_out[...] = sent[2 * SLAB :]
    else:
        ctx_ref[...] = dot(place_ref[...], ctxp_ref[...]).astype(BF)


def forward_kernel(last, *refs):
    coords_ref, ones, twos, refs = refs[0], refs[1:9], refs[9:17], refs[17:]
    w_ref, sems = refs[11] if last else refs[10], refs[-1]
    copies = assembly(coords_ref, [(ones, True, (3, 3), 0), (twos, False, (0, 6), 3)], w_ref, sems)
    if last:
        x_ref, ctxp_ref, rows_ref, cols_ref, corner_ref, place_ref = refs[:6]
        bp_ref, g2_ref, b2_ref, bo_ref, bh_ref = refs[6:11]
        ctx_ref, mid_ref, h2_ref, hidden_ref, slope_ref, out_ref = refs[12:18]
        place = place_ref[...]
        slabs = jnp.concatenate([rows_ref[...], cols_ref[...], corner_ref[...]], 0)
        ctx_ref[...] = (dot(place[:, :PADDED], ctxp_ref[...]) + dot(place[:, PADDED:], slabs)).astype(BF)
    else:
        x_ref, ctx_ref, bp_ref, g2_ref, b2_ref, bo_ref, bh_ref = refs[:7]
        g1_ref, b1_ref, take_ref = refs[7:10]
        mid_ref, h2_ref, hidden_ref, slope_ref, out_ref, h_ref, rows_out, cols_out, corner_out = refs[11:20]
    for c in copies:
        c.wait()
    mid_ref[...] = x_ref[...].astype(F32) + dot(ctx_ref[...], block(w_ref, 0)) + bp_ref[...]
    hat, _ = normalized(mid_ref[...])
    h2_ref[...] = (hat * g2_ref[...] + b2_ref[...]).astype(BF)
    for b in range(4):
        for half in range(2):
            lanes = slice(half * 256, half * 256 + 256)
            wide = slice(b * D + half * 256, b * D + half * 256 + 256)
            pre = dot(h2_ref[...], block_lanes(w_ref, 1 + b, lanes)) + bh_ref[:, wide]
            hidden, slope = gelu_both(pre)
            hidden_ref[:, wide] = hidden.astype(BF)
            slope_ref[:, wide] = slope.astype(BF)
    out = mid_ref[...] + bo_ref[...]
    for b in range(4):
        out = out + dot(hidden_ref[:, b * D : (b + 1) * D], block(w_ref, 5 + b))
    out_ref[...] = out.astype(out_ref.dtype)
    if not last:
        hat, _ = normalized(out)
        h_ref[...] = (hat * g1_ref[...] + b1_ref[...]).astype(BF)
        sent = dot(take_ref[...], h_ref[...]).astype(BF)
        rows_out[...] = sent[:SLAB]
        cols_out[...] = sent[SLAB : 2 * SLAB]
        corner_out[...] = sent[2 * SLAB :]


def hidden_back_pass(gm_ref, slope_ref, w_ref, dpre_ref, dbh_ref):
    for b in range(4):
        for half in range(2):
            wide = slice(b * D + half * 256, b * D + half * 256 + 256)
            dpre = dot_nt(gm_ref[...], block_rows(w_ref, 5 + b, half)) * slope_ref[:, wide].astype(F32)
            dpre = dpre.astype(BF)
            dpre_ref[:, wide] = dpre
            dbh_ref[:, wide] = jnp.sum(dpre.astype(F32), 0, keepdims=True)


def middle_back_pass(dpre_ref, w_ref, mid_ref, g2_ref, dmid_ref, go_ref, small_ref):
    dh2 = dot_nt(dpre_ref[:, :D], block(w_ref, 1))
    for b in range(1, 4):
        dh2 = dh2 + dot_nt(dpre_ref[:, b * D : (b + 1) * D], block(w_ref, 1 + b))
    dx, dg2, db2 = norm_back(dh2, mid_ref[...], g2_ref[...])
    small_ref[1:2, :] = dg2
    small_ref[2:3, :] = db2
    dmid_ref[...] += dx
    go_ref[...] = dmid_ref[...].astype(BF)
    small_ref[0:1, :] = jnp.sum(go_ref[...].astype(F32), 0, keepdims=True)


def back_last_kernel(*refs):
    g_ref, slope_ref, mid_ref, w_ref, g2_ref, take_ref = refs[:6]
    dmid_ref, dpre_ref, go_ref, small_ref, dbh_ref, dctx_ref, rows_out, cols_out, corner_out = refs[6:]
    dmid_ref[...] = g_ref[...].astype(F32)
    small_ref[3:4, :] = jnp.sum(g_ref[...].astype(F32), 0, keepdims=True)
    hidden_back_pass(g_ref, slope_ref, w_ref, dpre_ref, dbh_ref)
    middle_back_pass(dpre_ref, w_ref, mid_ref, g2_ref, dmid_ref, go_ref, small_ref)
    dctx_ref[...] = dot_nt(go_ref[...], block(w_ref, 0)).astype(BF)
    sent = dot(take_ref[...], dctx_ref[...]).astype(BF)
    rows_out[...] = sent[:SLAB]
    cols_out[...] = sent[SLAB : 2 * SLAB]
    corner_out[...] = sent[2 * SLAB :]


def grads_last_kernel(coords_ref, gm_ref, hidden_ref, h2_ref, dpre_ref, ctx_ref, go_ref, keep_ref, send_ref):
    for half in range(2):
        rows = slice(half * 256, half * 256 + 256)
        store_grad(coords_ref, keep_ref, send_ref, 0, half, dot_tn(ctx_ref[:, rows], go_ref[...]))
        for b in range(4):
            wide = slice(b * D + half * 256, b * D + half * 256 + 256)
            grad_e = dot_tn(h2_ref[:, rows], dpre_ref[:, b * D : (b + 1) * D])
            store_grad(coords_ref, keep_ref, send_ref, 1 + b, half, grad_e)
            store_grad(coords_ref, keep_ref, send_ref, 5 + b, half, dot_tn(hidden_ref[:, wide], gm_ref[...]))


def back_first_kernel(*refs):
    coords_ref, dmid1_ref, dhp_ref, rows_ref, cols_ref, corner_ref, back_ref, x1_ref, g1_ref = refs[:9]
    hidden_ref, slope_ref, h2_ref, w_ref = refs[9:13]
    grad_ref, dpre_ref, keep_ref, send_ref, dbo_ref, dbh_ref, above_ref, gm_ref = refs[13:]
    back = back_ref[...]
    slabs = jnp.concatenate([rows_ref[...], cols_ref[...], corner_ref[...]], 0)
    dh = dot(back[:, :PADDED], dhp_ref[...]) + dot(back[:, PADDED:], slabs)
    dx, dg1, db1 = norm_back(dh, x1_ref[...], g1_ref[...])
    above_ref[0:1, :] = dg1
    above_ref[1:2, :] = db1
    grad = dmid1_ref[...] + dx
    grad_ref[...] = grad
    gm_ref[...] = grad.astype(BF)
    dbo_ref[...] = jnp.sum(gm_ref[...].astype(F32), 0, keepdims=True)
    hidden_back_pass(gm_ref, slope_ref, w_ref, dpre_ref, dbh_ref)
    for half in range(2):
        rows = slice(half * 256, half * 256 + 256)
        for b in range(4):
            wide = slice(b * D + half * 256, b * D + half * 256 + 256)
            grad_e = dot_tn(h2_ref[:, rows], dpre_ref[:, b * D : (b + 1) * D])
            store_grad(coords_ref, keep_ref, send_ref, b, half, grad_e)
            store_grad(coords_ref, keep_ref, send_ref, 4 + b, half, dot_tn(hidden_ref[:, wide], gm_ref[...]))


def middle_first_kernel(grad_ref, dpre_ref, mid_ref, ctx_ref, w_ref, g2_ref, place_ref, *outs):
    dmid_ref, dwp_ref, small_ref, dctxp_ref, go_ref = outs
    dmid_ref[...] = grad_ref[...]
    middle_back_pass(dpre_ref, w_ref, mid_ref, g2_ref, dmid_ref, go_ref, small_ref)
    dctx = dot_nt(go_ref[...], block(w_ref, 0)).astype(BF)
    dctxp_ref[...] = dot(place_ref[...], dctx).astype(BF)
    for half in range(2):
        rows = slice(half * 256, half * 256 + 256)
        dwp_ref[rows, :] = dot_tn(ctx_ref[:, rows], go_ref[...]).astype(BF)


def attend_back_pairs(pairs, qkv_ref, attn_ref, dctxp_ref, dqkv_ref, dtable_ref):
    dtable_ref[...] = jnp.zeros_like(dtable_ref)
    scale = HEAD_DIM**-0.5

    def one_pair(p, carry):
        start = pl.multiple_of(p * 128, 128)
        for g in range(GROUPS):
            lane = g * 128
            attn = attn_ref[p, g]
            keys = head_rows(side_by_side(qkv_ref, start, D + lane))
            values = head_rows(side_by_side(qkv_ref, start, 2 * D + lane))
            queries = block_diagonal(side_by_side(qkv_ref, start, lane))
            grads = block_diagonal(side_by_side(dctxp_ref, start, lane))
            probs = attn.astype(F32).reshape(4, SLOT, 128)
            dprobs = dot_nt(values, grads).reshape(4, SLOT, 128)
            dscores = probs * (dprobs - jnp.sum(probs * dprobs, 1, keepdims=True))
            dscores = dscores.reshape(256, 128).astype(BF)
            dtable_ref[g * 256 : (g + 1) * 256, :] += dscores.astype(F32)
            store_diagonal(dqkv_ref, start, lane, dot_tn(dscores, keys) * scale)
            dkeys = (head_fold(dot(dscores, queries)) * scale).astype(BF)
            dqkv_ref[pl.ds(start, SLOT), D + lane : D + lane + 128] = dkeys[:, :128]
            dqkv_ref[pl.ds(start + SLOT, SLOT), D + lane : D + lane + 128] = dkeys[:, 128:]
            dvalues = head_fold(dot(attn, grads)).astype(BF)
            dqkv_ref[pl.ds(start, SLOT), 2 * D + lane : 2 * D + lane + 128] = dvalues[:, :128]
            dqkv_ref[pl.ds(start + SLOT, SLOT), 2 * D + lane : 2 * D + lane + 128] = dvalues[:, 128:]
        return carry

    lax.fori_loop(0, pairs, one_pair, 0)


def table_sum(dtable_ref, hot_ref, out_ref):
    total = jnp.zeros((2 * HEADS, 256), F32)
    for c in range(25):
        keys = [dtable_ref[pl.ds(2 * c + k, HEADS, stride=SLOT), :] for k in range(2)]
        rows = jnp.concatenate(keys, 1)
        high = rows.astype(BF)
        low = (rows - high.astype(F32)).astype(BF)
        total = total + dot(jnp.concatenate([high, low], 0), hot_ref[256 * c : 256 * c + 256, :])
    out_ref[...] = total[:HEADS] + total[HEADS:]


def attend_back_kernel(*refs):
    dctx_ref, rows_ref, cols_ref, corner_ref, place_ref, qkv_ref, attn_ref, w_ref, take_ref, hot_ref = refs[:10]
    dqkv_ref, dbias_ref, table_ref, dhp_ref, rows_out, cols_out, corner_out, dctxp_ref, dtable_ref = refs[10:]
    place = place_ref[...]
    slabs = jnp.concatenate([rows_ref[...], cols_ref[...], corner_ref[...]], 0)
    dctxp_ref[...] = (dot(place[:, :CELLS], dctx_ref[...]) + dot(place[:, CELLS:], slabs)).astype(BF)
    attend_back_pairs(PAIRS, qkv_ref, attn_ref, dctxp_ref, dqkv_ref, dtable_ref)
    table_sum(dtable_ref, hot_ref, table_ref)
    for s in range(3):
        dbias_ref[s : s + 1, :] = jnp.sum(dqkv_ref[:, s * D : (s + 1) * D].astype(F32), 0, keepdims=True)
    dhp = dot_nt(dqkv_ref[:, :D], block(w_ref, 0))
    for s in range(1, 3):
        dhp = dhp + dot_nt(dqkv_ref[:, s * D : (s + 1) * D], block(w_ref, s))
    dhp_ref[...] = dhp.astype(BF)
    sent = dot(take_ref[...], dhp_ref[...]).astype(BF)
    rows_out[...] = sent[:SLAB]
    cols_out[...] = sent[SLAB : 2 * SLAB]
    corner_out[...] = sent[2 * SLAB :]


def grads_heads_kernel(coords_ref, hp_ref, dqkv_ref, keep_ref, send_ref):
    for s in range(3):
        for half in range(2):
            rows = slice(half * 256, half * 256 + 256)
            grad_w = dot_tn(hp_ref[:, rows], dqkv_ref[:, s * D : (s + 1) * D])
            store_grad(coords_ref, keep_ref, send_ref, s, half, grad_w)


def attend_back_half_kernel(dctxp_ref, qkv_ref, attn_ref, dqkv_ref, dtable_ref):
    attend_back_pairs(PAIRS // 2, qkv_ref, attn_ref, dctxp_ref, dqkv_ref, dtable_ref)


def attend_back_end_kernel(*refs):
    coords_ref, dctxp_ref, qkv_ref, attn_ref, one_ref, first_ref, hp_ref, dwp_ref, hot_ref, w_ref, place_ref = refs[:11]
    x_ref, dmid_ref, g1_ref, norm1, dqb1, sums1, dbh1, table1, sums0, dbo0, dbh0 = refs[11:22]
    keep_ref, send_ref, out_ref, sums_ref, two_ref, dtable_ref, dhp_ref = refs[22:]
    attend_back_pairs(PAIRS // 2, qkv_ref, attn_ref, dctxp_ref, two_ref, dtable_ref)
    upper = PADDED // 2
    dqb = []
    for s in range(3):
        wide = slice(s * D, (s + 1) * D)
        dqb.append(
            jnp.sum(one_ref[:, wide].astype(F32), 0, keepdims=True)
            + jnp.sum(two_ref[:, wide].astype(F32), 0, keepdims=True)
        )
        for half in range(2):
            rows = slice(half * 256, half * 256 + 256)
            grad_w = dot_tn(hp_ref[:upper, rows], one_ref[:, wide]) + dot_tn(hp_ref[upper:, rows], two_ref[:, wide])
            store_grad(coords_ref, keep_ref, send_ref, s, half, grad_w)
    for half in range(2):
        store_grad(coords_ref, keep_ref, send_ref, 3, half, dwp_ref[half * 256 : half * 256 + 256, :])
    for half, half_ref in enumerate((one_ref, two_ref)):
        part = dot_nt(half_ref[:, :D], block(w_ref, 0))
        for s in range(1, 3):
            part = part + dot_nt(half_ref[:, s * D : (s + 1) * D], block(w_ref, s))
        dhp_ref[half * upper : half * upper + upper, :] = part.astype(BF)
    dh = dot(place_ref[...], dhp_ref[...])
    dx, dg1, db1 = norm_back(dh, x_ref[...].astype(F32), g1_ref[...])
    out_ref[...] = dmid_ref[...] + dx
    for at, norm, query, value, sums, dbo, dbh in (
        (0, (dg1, db1), dqb[0], dqb[2], sums0, dbo0[...], dbh0),
        (12, (norm1[0:1, :], norm1[1:2, :]), dqb1[0:1, :], dqb1[2:3, :], sums1, sums1[3:4, :], dbh1),
    ):
        rows = [*norm, query, value, sums[0:1, :], sums[1:2, :], sums[2:3, :], dbo]
        rows += [dbh[:, D * b : D * b + D] for b in range(4)]
        for i, row in enumerate(rows):
            sums_ref[at + i : at + i + 1, :] = row
    dtable_ref[...] += first_ref[...]
    table_sum(dtable_ref, hot_ref, sums_ref.at[24:40, 0:256])
    sums_ref[24:40, 256:512] = table1[...]


def add_kernel(*refs):
    out_ref, at = refs[-1], 0
    for i in range(0, len(refs) - 1, 2):
        n = refs[i].shape[2]
        total = refs[i][...].astype(F32) + refs[i + 1][...].astype(F32)
        out_ref[:, :, at : at + n] = total.astype(BF)
        at += n


def sum_split_kernel(coords_ref, parts_ref, *outs):
    for d, out in enumerate(outs):
        target = lax.bitwise_xor(coords_ref[1], d)
        total = parts_ref[0, target].astype(F32)
        for k in range(1, 4):
            total = total + parts_ref[k, target].astype(F32)
        out[...] = total.astype(BF)


def four(refs, b):
    return (refs[0][b].astype(F32) + refs[1][b].astype(F32)) + (refs[2][b].astype(F32) + refs[3][b].astype(F32))


def reorder(values, order):
    high = values.astype(BF)
    rest = values - high.astype(F32)
    low = rest.astype(BF)
    last = (rest - low.astype(F32)).astype(BF)
    return dot_nt(high, order) + dot_nt(low, order) + dot_nt(last, order)


def step_into(at, grad, old, new, rate, decay):
    weight, first, second = (ref[at] for ref in old)
    for ref, value in zip(new, adamw(weight, first, second, grad, rate, decay)):
        ref[at] = value


def update_small_kernel(sums_ref, units_ref, *refs):
    small, table, new_small, new_table, bias_ref = refs[:3], refs[3:6], refs[6:9], refs[9:12], refs[12]
    for layer in range(LAYERS):
        rows = [sums_ref[12 * layer + i : 12 * layer + i + 1, :] for i in range(12)]
        bias_ref[layer : layer + 1, :] = rows[7]
        for g in range(GROUPS):
            part = jnp.concatenate([rows[8 + b][:, 128 * g : 128 * g + 128] for b in range(4)], 1)
            rows.append(reorder(jnp.broadcast_to(part, (8, D)), units_ref[...])[:1])
        for i, grad in enumerate(rows[:8] + rows[12:]):
            at = (slice(layer, layer + 1), slice(D * i, D * i + D))
            step_into(at, grad, small, new_small, 0.3, 0.0)
        grad = sums_ref[24:40, 256 * layer : 256 * layer + 256].T[:REL]
        step_into((layer,), grad, table, new_table, 0.6, 0.0)


def update_kernel(*refs):
    early, late, heads_ref, units_ref, refs = refs[:4], refs[4:8], refs[8], refs[9], refs[10:]
    old = [refs[3 * i : 3 * i + 3] for i in range(4)]
    new = [refs[12 + 3 * i : 15 + 3 * i] for i in range(4)]

    def layer_step(heads, head_at, rest, rest_at):
        step_into((0,), four(rest, rest_at), old[1], new[1], 0.1, 0.05)
        for b in range(4):
            step_into((0, slice(16 * b, 16 * b + 16)), four(rest, rest_at + 5 + b), old[3], new[3], 0.03, 0.05)
        for n, wide, order_ref, i, pieces, at in (
            (3, 384, heads_ref, 0, heads, head_at),
            (4, 512, units_ref, 2, rest, rest_at + 1),
        ):
            grads = [four(pieces, at + b) for b in range(n)]
            for g in range(GROUPS):
                part = jnp.concatenate([v[:, 128 * g : 128 * g + 128] for v in grads], 1)
                lanes = (0, slice(None), slice(wide * g, wide * g + wide))
                step_into(lanes, reorder(part, order_ref[...]), old[i], new[i], 0.03, 0.05)

    @pl.when(pl.program_id(0) == 0)
    def _():
        layer_step(late, 0, late, 3)

    @pl.when(pl.program_id(0) == 1)
    def _():
        layer_step(late, 12, early, 0)


def to_neighbours(slabs, ahead):
    step = -1 if ahead else 1
    along = [(i, (i + step) % 4) for i in range(4)]
    over = [(0, 1), (1, 0)]
    both = [(i * 2 + c, ((i + step) % 4) * 2 + 1 - c) for i in range(4) for c in range(2)]
    rows, cols, corner = slabs
    return (
        lax.ppermute(rows, "seq", along),
        lax.ppermute(cols, "col", over),
        lax.ppermute(corner, ("seq", "col"), both),
    )


def flat(z, x, core):
    return (z * 4 + (x // 2) * 2 + core) * 2 + x % 2


ALONG_X = [[flat(z, x, core) for x in range(4)] for z in range(4) for core in range(2)]
OVER_XZ = [[flat(z, x, core) for z in range(4) for x in range(4)] for core in range(2)]
OTHER_CORE = [(i, i ^ 1) for i in range(16)]


def from_z(distance):
    return [(((z + distance) % 4) * 4 + k, z * 4 + k) for z in range(4) for k in range(4)]


ALONG_Z = [[z * 4 + k for z in range(4)] for k in range(4)]


def along_x(value):
    return lax.all_to_all(value, ("img", "col"), 0, 0, tiled=True, axis_index_groups=ALONG_X)


def along_z(value):
    return lax.all_to_all(value, "img", 0, 0, tiled=True, axis_index_groups=ALONG_Z)


def from_core(value):
    return lax.ppermute(value, "img", OTHER_CORE)


def four_sum(value, axis, pairs):
    one, two, three = (lax.ppermute(value, axis, p) for p in pairs)
    return (value.astype(F32) + one.astype(F32)) + (two.astype(F32) + three.astype(F32))


BY_SEQ = [[(i, i ^ d) for i in range(4)] for d in (1, 2, 3)]
BY_Z = [[(z * 4 + k, (z ^ d) * 4 + k) for z in range(4) for k in range(4)] for d in (1, 2, 3)]
BY_X = [
    [(flat(z, x, c), flat(z, x ^ d, c)) for z in range(4) for x in range(4) for c in range(2)] for d in (1, 2, 3)
]


def both_cores(*pairs):
    arrays = [a for pair in pairs for a in pair]
    specs = [pl.BlockSpec((1, *a.shape[1:]), lambda i: (i, 0, 0, 0, 0)) for a in arrays]
    shape = (4, 4, sum(keep.shape[2] for keep, _ in pairs), 16, D)
    size = math.prod(shape) * 2
    return pl.pallas_call(
        add_kernel,
        grid=(4,),
        out_shape=jax.ShapeDtypeStruct(shape, BF),
        in_specs=specs,
        out_specs=pl.BlockSpec((1, *shape[1:]), lambda i: (i, 0, 0, 0, 0)),
        compiler_params=pltpu.CompilerParams(vmem_limit_bytes=VMEM_BYTES),
        cost_estimate=pl.CostEstimate(flops=size, bytes_accessed=3 * size, transcendentals=0),
    )(*arrays)


def summed(parts):
    return parts.astype(F32).sum(0).astype(BF)


def by_seq(value):
    return [value] + [lax.ppermute(value, "seq", p) for p in BY_SEQ]


def all_sum(value):
    value = value + lax.ppermute(value, "img", OTHER_CORE)
    value = four_sum(value, ("img", "col"), BY_X)
    value = four_sum(value, "img", BY_Z)
    return four_sum(value, "seq", BY_SEQ)


def update(early, late, heads, units, state):
    whole = [pl.BlockSpec(memory_space=pltpu.VMEM)] * 10
    parts = [pl.BlockSpec((1, *a.shape[1:]), lambda layer: (layer, 0, 0)) for a in state]
    return pl.pallas_call(
        update_kernel,
        grid=(LAYERS,),
        out_shape=[jax.ShapeDtypeStruct(a.shape, F32) for a in state],
        in_specs=whole + parts,
        out_specs=parts,
        compiler_params=pltpu.CompilerParams(vmem_limit_bytes=VMEM_BYTES),
        cost_estimate=pl.CostEstimate(flops=20 * 10**9, bytes_accessed=2 * 10**7, transcendentals=0),
    )(*early, *late, heads, units, *state)


def adamw(weight, first, second, grad, rate, decay):
    first = 0.9 * first + 0.1 * grad
    second = 0.999 * second + 0.001 * grad * grad
    first_hat = first / (1.0 - 0.9**STEP)
    second_hat = second / (1.0 - 0.999**STEP)
    return (first, second, weight - rate * (first_hat / (jnp.sqrt(second_hat) + 1e-08) + decay * weight))


def hidden_order(vector):
    return vector.reshape(32, 4, 16).transpose(1, 0, 2).reshape(HIDDEN)


def split_small(vector):
    pieces = [vector[i * D : (i + 1) * D][None] for i in range(8)]
    return pieces + [hidden_order(vector[8 * D :])[None]]


def score_table(table, hot):
    rows = lax.dot_general(table, hot, (((0,), (0,)), ((), ())), precision=highest, preferred_element_type=F32)
    rows = rows.reshape(HEADS, AREA, AREA) * log2e
    rows = jnp.pad(rows, ((0, 0), (0, 0), (0, SLOT - AREA)))
    rows = jnp.pad(rows, ((0, 0), (0, SLOT - AREA), (0, 0)), constant_values=padded_score)
    return jnp.concatenate([rows, rows], 2).reshape(HEADS * SLOT, 128)


def allowed_pairs(region):
    win = region.reshape(4, WIN, 4, WIN).transpose(0, 2, 1, 3).reshape(16, AREA)
    win = jnp.pad(win, ((0, 0), (0, SLOT - AREA)))
    same = win[:, :, None] == win[:, None, :]
    same = same | (jnp.arange(SLOT) >= AREA)[None, :, None]
    same = same.reshape(PAIRS, 2, SLOT, SLOT).transpose(0, 2, 1, 3).reshape(PAIRS, SLOT, 128)
    return same.astype(F32)


def half_blocks(half):
    return {
        0: ((PADDED // 2, D), (half, 0)),
        1: ((PADDED // 2, 3 * D), (half, 0)),
        2: ((PAIRS // 2, GROUPS, 256, 128), (half, 0, 0, 0)),
    }


def local(
    images,
    out_grad,
    region_ids,
    rel_index,
    qkv_weight,
    qkv_first,
    qkv_second,
    proj_weight,
    proj_first,
    proj_second,
    expand_weight,
    expand_first,
    expand_second,
    contract_weight,
    contract_first,
    contract_second,
    small_params,
    small_first,
    small_second,
    bias_table,
    table_first,
    table_second,
):
    plain, plain_back, ahead, back, take_first, take_last = (jnp.asarray(a, BF) for a in placements())
    heads, units = (jnp.asarray(a, BF) for a in column_orders())
    img = lax.axis_index("img")
    x = (img // 2 % 2) * 2 + lax.axis_index("col")
    coords = jnp.stack([img // 4, x, img % 2]).astype(jnp.int32)
    packed = call(
        pack_kernel,
        [((12, 16, D), BF)] * 2,
        (qkv_weight, proj_weight, expand_weight, contract_weight, heads, units),
        us=3,
    )
    by_x = [packed[0]] + [lax.ppermute(packed[0], ("img", "col"), p) for p in BY_X]
    by_z = [packed[1]] + [lax.ppermute(packed[1], "img", from_z(d)) for d in (1, 2, 3)]

    def gathered(by_x, by_z):
        one = [by_x] + [lax.ppermute(by_x, "img", from_z(d)) for d in (1, 2, 3)]
        two = [by_z] + [lax.ppermute(by_z, ("img", "col"), p) for p in BY_X]
        return one + [from_core(v) for v in one], two + [from_core(v) for v in two]

    one0, two0 = gathered(jnp.stack([v[:6] for v in by_x]), jnp.stack([v[:6] for v in by_z]))
    x0 = images.reshape(CELLS, D)
    g_out = out_grad.reshape(CELLS, D)
    by_key = jnp.pad(rel_index.T, ((0, 1), (0, SLOT - AREA)), constant_values=-1)
    by_key = jnp.concatenate([by_key, by_key], 1)
    hot = (by_key.reshape(-1, 1) == jnp.arange(256, dtype=jnp.int32)).astype(BF)
    keys_hot = (jnp.arange(REL, dtype=jnp.int32)[:, None] == rel_index.T.reshape(1, AREA * AREA)).astype(F32)
    tables = [score_table(bias_table[layer], keys_hot) for layer in range(LAYERS)]
    region = lax.dynamic_slice_in_dim(region_ids, lax.axis_index("seq") * SIDE, SIDE, 0)
    mask = allowed_pairs(region)
    small = [split_small(small_params[layer]) for layer in range(LAYERS)]
    zero = jnp.zeros((1, D), F32)
    qkv_bias = [jnp.concatenate([s[2], zero, s[3]], 1) for s in small]

    qkv_shape = ((PADDED, 3 * D), BF)
    attn_shape = ((PAIRS, GROUPS, 256, 128), BF)
    slab_shapes = [((SLAB, D), BF), ((SLAB, D), BF), ((CORNER, D), BF)]
    cells16, cells32 = ((CELLS, D), BF), ((CELLS, D), F32)
    padded16 = ((PADDED, D), BF)
    wide16 = ((CELLS, HIDDEN), BF)

    copies, more_copies = pltpu.SemaphoreType.DMA((32,)), pltpu.SemaphoreType.DMA((64,))
    w_shapes = [((3, 32, 16, D), BF), ((9, 32, 16, D), BF)]
    g1, b1, _, _, bp, g2, b2, bo, bh = small[0]
    (hp0,) = call(enter_kernel, [padded16], (x0, g1, b1, plain), us=4)
    wq0, qkv0, attn0, ctx0 = call(
        functools.partial(attend_kernel, False),
        [w_shapes[0], qkv_shape, attn_shape, cells16],
        (hp0, qkv_bias[0], tables[0], plain_back),
        [pltpu.VMEM((PADDED, D), BF), copies],
        one0,
        coords,
        us=17,
    )
    one1, two1 = gathered(*call(stack_kernel, [((4, 6, 16, D), BF)] * 2, (*by_x, *by_z), after=(ctx0,)))
    wm0, mid0, h20, hidden0, slope0, x1, h1, *slabs = call(
        functools.partial(forward_kernel, False),
        [w_shapes[1], cells32, cells16, wide16, wide16, cells32, cells16, *slab_shapes],
        (x0, ctx0, bp, g2, b2, bo, bh, small[1][0], small[1][1], take_first),
        [more_copies],
        one0 + two0,
        coords,
        us=15,
    )
    g1, b1, _, _, bp, g2, b2, bo, bh = small[1]
    slabs = to_neighbours(slabs, True)
    wq1, hp1, qkv1, attn1, ctxp1, *slabs = call(
        functools.partial(attend_kernel, True),
        [w_shapes[0], padded16, qkv_shape, attn_shape, padded16, *slab_shapes],
        (h1, *slabs, ahead, qkv_bias[1], tables[1], mask, take_last),
        [copies],
        one1,
        coords,
        us=18,
    )
    slabs = to_neighbours(slabs, False)
    wm1, ctx1, mid1, h21, hidden1, slope1, out = call(
        functools.partial(forward_kernel, True),
        [w_shapes[1], cells16, cells32, cells16, wide16, wide16, cells16],
        (x1, ctxp1, *slabs, back, bp, g2, b2, bo, bh),
        [more_copies],
        one1 + two1,
        coords,
        us=15,
    )
    dmid1, dpre1, go1, sums1, dbh1, dctx1, *slabs = call(
        back_last_kernel,
        [cells32, wide16, cells16, ((4, D), F32), ((1, HIDDEN), F32), cells16, *slab_shapes],
        (g_out, slope1, mid1, wm1, g2, take_first),
        us=11,
    )
    slabs = to_neighbours(slabs, True)
    keep, send = call(
        grads_last_kernel,
        [((4, 4, 9, 16, D), BF)] * 2,
        (g_out, hidden1, h21, dpre1, ctx1, go1),
        place=coords,
        us=8,
    )
    part_m1 = both_cores((keep, from_core(send)))
    dqkv1, dqb1, table1, dhp1, *slabs = call(
        attend_back_kernel,
        [qkv_shape, ((3, D), F32), ((HEADS, 256), F32), padded16, *slab_shapes],
        (dctx1, *slabs, ahead, qkv1, attn1, wq1, take_last, hot),
        [pltpu.VMEM((PADDED, D), BF), pltpu.VMEM((HEADS * SLOT, 128), F32)],
        us=20,
        after=(part_m1,),
    )
    slabs = to_neighbours(slabs, False)
    keep, send = call(grads_heads_kernel, [((4, 4, 3, 16, D), BF)] * 2, (hp1, dqkv1), place=coords, us=4)
    pair_q1 = (keep, from_core(send))
    half_m1 = summed(along_z(part_m1))
    grad1, dpre0, keep, send, dbo0, dbh0, norm1 = call(
        back_first_kernel,
        [cells32, wide16, *[((4, 4, 8, 16, D), BF)] * 2, ((1, D), F32), ((1, HIDDEN), F32), ((2, D), F32)],
        (dmid1, dhp1, *slabs, back, x1, small[1][0], hidden0, slope0, h20, wm0),
        [pltpu.VMEM((CELLS, D), BF)],
        place=coords,
        us=16,
        after=(half_m1,),
    )
    grad_m1 = summed(along_x(half_m1))
    dmid0, dwp0, sums0, dctxp0 = call(
        middle_first_kernel,
        [cells32, ((D, D), BF), ((3, D), F32), padded16],
        (grad1, dpre0, mid0, ctx0, wm0, small[0][5], plain),
        [pltpu.VMEM((CELLS, D), BF)],
        us=8,
        after=(grad_m1,),
    )
    part_0 = both_cores((keep, from_core(send)), pair_q1)
    grads_m1 = by_seq(grad_m1)
    half_qkv, table_shape = ((PADDED // 2, 3 * D), BF), ((HEADS * SLOT, 128), F32)
    one, dtable0 = call(
        attend_back_half_kernel,
        [half_qkv, table_shape],
        (dctxp0, qkv0, attn0),
        us=9,
        after=(part_0,),
        blocks=half_blocks(0),
    )
    half_0 = along_z(part_0)
    keep, send, input_grad, sums = call(
        attend_back_end_kernel,
        [*[((4, 4, 4, 16, D), BF)] * 2, cells32, ((40, D), F32)],
        (dctxp0, qkv0, attn0, one, dtable0, hp0, dwp0, hot, wq0, plain_back, x0, dmid0, small[0][0])
        + (norm1, dqb1, sums1, dbh1, table1, sums0, dbo0, dbh0),
        [pltpu.VMEM(*half_qkv), pltpu.VMEM(*table_shape), pltpu.VMEM(*padded16)],
        place=coords,
        us=22,
        blocks=half_blocks(1),
        after=grads_m1,
    )
    part_q0 = both_cores((keep, from_core(send))).reshape(16, 4, 16, D)
    part_q0 = lax.all_to_all(part_q0, ("img", "col"), 0, 0, tiled=True, axis_index_groups=OVER_XZ)
    half_0, *others = call(sum_split_kernel, [((11, 16, D), BF)] * 4, (half_0,), place=coords)
    others = [lax.ppermute(v, ("img", "col"), p) for v, p in zip(others, BY_X)]
    grad_0 = sum((v.astype(F32) for v in others), half_0.astype(F32)).astype(BF)
    late = by_seq(jnp.concatenate([summed(part_q0), grad_0], 0))

    state = (
        (qkv_weight, qkv_first, qkv_second),
        (proj_weight, proj_first, proj_second),
        (expand_weight, expand_first, expand_second),
        (contract_weight, contract_first, contract_second),
    )
    flat_state = [a for three in state for a in three]
    done = update(grads_m1, late, heads, units, flat_state)
    qkv_new, proj_new, expand_new, contract_new = done[:3], done[3:6], done[6:9], done[9:]
    last = call(
        update_small_kernel,
        [((LAYERS, 12 * D), F32)] * 3 + [((LAYERS, REL, HEADS), F32)] * 3 + [((LAYERS, D), F32)],
        (all_sum(sums), units, small_params, small_first, small_second, bias_table, table_first, table_second),
        us=2,
    )
    return (
        out.reshape(images.shape),
        input_grad.reshape(images.shape),
        *qkv_new,
        *proj_new,
        *expand_new,
        *contract_new,
        *last,
    )


def solution(mesh):
    cells = P("img", "seq", "col", None)
    matrix = P(None, ("img", "col"), None)
    in_specs = (cells, cells, P(None, "col"), P(), *([matrix] * 12), *([P()] * 6))
    out_specs = (cells, cells, *([matrix] * 12), *([P()] * 7))
    return jax.shard_map(local, mesh=mesh, in_specs=in_specs, out_specs=out_specs, check_vma=False)
```

```python
import functools
import math

import jax
import jax.numpy as jnp
import numpy as np
from jax import lax
from jax.experimental import pallas as pl
from jax.experimental.pallas import tpu as pltpu
from jax.sharding import PartitionSpec as P

D = 512
HEADS = 16
HEAD_DIM = 32
WIN = 7
SHIFT = 3
LAYERS = 2
STEP = 10
REL = 169
SIDE = 28
CELLS = SIDE * SIDE
AREA = WIN * WIN
SLOT = 64
PADDED = 16 * SLOT
PAIRS = 8
GROUPS = 4
SLAB = 96
CORNER = 16
HALO = 2 * SLAB + CORNER
HIDDEN = 4 * D

BF = jnp.bfloat16
F32 = jnp.float32
epsilon = 1e-05
log2e = math.log2(math.e)
masked_score = -1000000000.0 * log2e
padded_score = -1e30
highest = lax.Precision.HIGHEST
VMEM_BYTES = 58 * 2**20


def padded_row(r, c):
    return ((r // WIN) * 4 + c // WIN) * SLOT + (r % WIN) * WIN + c % WIN


def ahead_source(r, c):
    r, c = r + SHIFT, c + SHIFT
    if r < SIDE and c < SIDE:
        return r * SIDE + c
    if c < SIDE:
        return CELLS + (r - SIDE) * SIDE + c
    if r < SIDE:
        return CELLS + SLAB + r * SHIFT + c - SIDE
    return CELLS + 2 * SLAB + (r - SIDE) * SHIFT + c - SIDE


def back_source(r, c):
    if r >= SHIFT and c >= SHIFT:
        return padded_row(r - SHIFT, c - SHIFT)
    if c >= SHIFT:
        return PADDED + r * SIDE + c - SHIFT
    if r >= SHIFT:
        return PADDED + SLAB + (r - SHIFT) * SHIFT + c
    return PADDED + 2 * SLAB + r * SHIFT + c


def placements():
    plain = np.zeros((PADDED, CELLS), np.float32)
    ahead = np.zeros((PADDED, CELLS + HALO), np.float32)
    back = np.zeros((CELLS, PADDED + HALO), np.float32)
    take_first = np.zeros((HALO, CELLS), np.float32)
    take_last = np.zeros((HALO, PADDED), np.float32)
    for r in range(SIDE):
        for c in range(SIDE):
            plain[padded_row(r, c), r * SIDE + c] = 1
            ahead[padded_row(r, c), ahead_source(r, c)] = 1
            back[r * SIDE + c, back_source(r, c)] = 1
    edge = SIDE - SHIFT
    for a in range(SHIFT):
        for b in range(SIDE):
            take_first[a * SIDE + b, a * SIDE + b] = 1
            take_first[SLAB + b * SHIFT + a, b * SIDE + a] = 1
            take_last[a * SIDE + b, padded_row(edge + a, b)] = 1
            take_last[SLAB + b * SHIFT + a, padded_row(b, edge + a)] = 1
        for b in range(SHIFT):
            take_first[2 * SLAB + a * SHIFT + b, a * SIDE + b] = 1
            take_last[2 * SLAB + a * SHIFT + b, padded_row(edge + a, edge + b)] = 1
    return (plain, plain.T.copy(), ahead, back, take_first, take_last)


def column_orders():
    heads = np.zeros((384, 384), np.float32)
    units = np.zeros((512, 512), np.float32)
    for n in range(4):
        for part in range(3):
            for d in range(HEAD_DIM):
                heads[n * 96 + part * 32 + d, part * 128 + n * 32 + d] = 1
    for r in range(8):
        for b in range(4):
            for i in range(16):
                units[r * 64 + b * 16 + i, b * 128 + r * 16 + i] = 1
    return heads, units


def dot(a, b):
    return lax.dot_general(a, b, (((1,), (0,)), ((), ())), preferred_element_type=F32)


def dot_nt(a, b):
    return lax.dot_general(a, b, (((1,), (1,)), ((), ())), preferred_element_type=F32)


def dot_tn(a, b):
    return lax.dot_general(a, b, (((0,), (0,)), ((), ())), preferred_element_type=F32)


def normalized(x):
    centred = x - jnp.mean(x, -1, keepdims=True)
    inverse = lax.rsqrt(jnp.mean(centred * centred, -1, keepdims=True) + epsilon)
    return centred * inverse, inverse


def norm_back(grad, x, gain):
    hat, inverse = normalized(x)
    grad_hat = grad * gain
    grad_x = inverse * (
        grad_hat
        - jnp.mean(grad_hat, -1, keepdims=True)
        - hat * jnp.mean(grad_hat * hat, -1, keepdims=True)
    )
    return grad_x, jnp.sum(grad * hat, 0, keepdims=True), jnp.sum(grad, 0, keepdims=True)


def gelu_both(u):
    a = jnp.abs(u)
    t = 1.0 / (1.0 + (0.3275911 * 0.5**0.5) * a)
    e = jnp.exp2((-0.5 * log2e) * u * u)
    poly = t * (
        0.5 * 0.254829592
        + t * (0.5 * -0.284496736 + t * (0.5 * 1.421413741 + t * (0.5 * -1.453152027 + t * (0.5 * 1.061405429))))
    )
    tail = poly * e
    phi = jnp.where(u >= 0, 1.0 - tail, tail)
    return u * phi, phi + u * e * (1.0 / math.sqrt(2 * math.pi))


def head_rows(pair):
    lane = lax.broadcasted_iota(jnp.int32, pair.shape, 1) % 128 // HEAD_DIM
    zero = jnp.zeros_like(pair)
    return jnp.concatenate([jnp.where(lane == h, pair, zero) for h in range(4)], 0)


def head_fold(rows):
    lane = lax.broadcasted_iota(jnp.int32, (SLOT, 256), 1) % 128 // HEAD_DIM
    out = rows[:SLOT]
    for h in range(1, 4):
        out = jnp.where(lane == h, rows[h * SLOT : (h + 1) * SLOT], out)
    return out


def side_by_side(ref, start, lane):
    return jnp.concatenate(
        [ref[pl.ds(start, SLOT), lane : lane + 128], ref[pl.ds(start + SLOT, SLOT), lane : lane + 128]], 1
    )


def block_diagonal(pair):
    lane = lax.broadcasted_iota(jnp.int32, pair.shape, 1)
    zero = jnp.zeros_like(pair)
    return jnp.concatenate([jnp.where(lane < 128, pair, zero), jnp.where(lane >= 128, pair, zero)], 0)


def store_diagonal(ref, start, lane, rows):
    ref[pl.ds(start, SLOT), lane : lane + 128] = rows[:SLOT, :128].astype(ref.dtype)
    ref[pl.ds(start + SLOT, SLOT), lane : lane + 128] = rows[SLOT:, 128:].astype(ref.dtype)


class Moves:
    def __init__(self, sems):
        self.loads, self.stores, self.started, self.sems = {}, {}, [], sems

    def load(self, pairs, buffer):
        at = len(self.started)
        for source, target in pairs:
            copy = pltpu.make_async_copy(source, target, self.sems.at[len(self.started)])
            copy.start()
            self.started.append(copy)
        self.loads[id(buffer)] = range(at, len(self.started))

    def need(self, *refs, part=None):
        for ref in refs:
            places = self.loads.get(id(ref), ())
            for at in places if part is None else places[part : part + 1]:
                if self.started[at] is not None:
                    self.started[at].wait()
                    self.started[at] = None

    def ship(self, ref, at=()):
        if id(ref) in self.stores:
            copy = pltpu.make_async_copy(
                ref.at[at] if at else ref,
                self.stores[id(ref)].at[at] if at else self.stores[id(ref)],
                self.sems.at[len(self.started)],
            )
            copy.start()
            self.started.append(copy)

    def finish(self):
        for copy in self.started:
            if copy is not None:
                copy.wait()


def columns(b):
    return (slice(None), slice(b * D, (b + 1) * D))


def of_blocks(b):
    return (slice(None), slice(None), b)


def call(body, outs, args, scratch=(), pieces=(), place=None, us=1, after=(), late=None, early=()):
    shapes = [jax.ShapeDtypeStruct(s, d) for s, d in outs]
    late = late or {}
    lead = [] if place is None else [place]
    anywhere, inside = pl.BlockSpec(memory_space=pl.ANY), pl.BlockSpec(memory_space=pltpu.VMEM)
    specs = [anywhere] * len(after) + [pl.BlockSpec(memory_space=pltpu.SMEM)] * len(lead) + [anywhere] * len(pieces)
    specs += [anywhere if i in late else inside for i in range(len(args))]
    buffers = []
    for i, parts in late.items():
        rows = parts[1:] if isinstance(parts, tuple) else args[i].shape[:1]
        buffers.append(pltpu.VMEM((*rows, *args[i].shape[1:]), args[i].dtype))
    buffers += [pltpu.VMEM(*outs[i]) for i in early]
    moving = bool(buffers)
    if moving:
        buffers.append(pltpu.SemaphoreType.DMA((96,)))

    def whole(*refs):
        refs = refs[len(after) :]
        first, n_in = len(lead) + len(pieces), len(lead) + len(pieces) + len(args)
        ins, results = list(refs[:n_in]), list(refs[n_in : n_in + len(outs)])
        rest = refs[n_in + len(outs) :]
        if not moving:
            body(*refs)
            return
        own, buffer = rest[: len(scratch)], rest[len(scratch) :]
        moves = Moves(buffer[-1])
        for (i, parts), target in zip(late.items(), buffer):
            source = ins[first + i]
            if parts is None:
                pairs = [(source, target)]
            elif isinstance(parts, tuple):
                pairs = [(source.at[pl.ds(*parts)], target)]
            else:
                pairs = [(source.at[part], target.at[part]) for part in parts]
            moves.load(pairs, target)
            ins[first + i] = target
        for i, source in zip(early, buffer[len(late) :]):
            moves.stores[id(source)] = results[i]
            results[i] = source
        body(moves, *ins, *results, *own)
        moves.finish()

    return pl.pallas_call(
        whole,
        out_shape=shapes,
        in_specs=specs,
        out_specs=[anywhere if i in early else inside for i in range(len(outs))],
        scratch_shapes=list(scratch) + buffers,
        compiler_params=pltpu.CompilerParams(vmem_limit_bytes=VMEM_BYTES),
        cost_estimate=pl.CostEstimate(flops=us * 3 * 10**9, bytes_accessed=us * 10**6, transcendentals=0),
    )(*after, *lead, *pieces, *args)


def held(arrays, after):
    anywhere = pl.BlockSpec(memory_space=pl.ANY)
    return pl.pallas_call(
        lambda *refs: None,
        out_shape=[jax.ShapeDtypeStruct(a.shape, a.dtype) for a in arrays],
        in_specs=[anywhere] * (len(arrays) + len(after)),
        out_specs=[anywhere] * len(arrays),
        input_output_aliases={i: i for i in range(len(arrays))},
    )(*arrays, *after)


def owner_of(z, x, core):
    return z * 8 + (x % 2) * 4 + core * 2 + x // 2


def assembly(coords_ref, sets, w_ref, sems):
    z, x, core = coords_ref[0], coords_ref[1], coords_ref[2]
    copies = []
    for pieces, far, (low, count), first in sets:
        for k, piece in enumerate(pieces):
            from_core = core if k < len(pieces) // 2 else 1 - core
            for i in range(piece.shape[0]):
                if far == "zx":
                    owner = owner_of(i // 4, i % 4, from_core)
                elif far == "z":
                    owner = owner_of(i // 4, lax.rem(x + i % 4, 4), from_core)
                elif far == "by z":
                    owner = owner_of(lax.rem(z + k % 4, 4), i, from_core)
                else:
                    owner = owner_of(lax.rem(z + i, 4), lax.rem(x + k % 4, 4), from_core)
                source, target = piece.at[i, pl.ds(low, count)], w_ref.at[pl.ds(first, count), owner]
                copies.append(pltpu.make_async_copy(source, target, sems.at[len(copies)]))
    for c in copies:
        c.start()
    return copies


def block(ref, b):
    return ref[b].reshape(D, D)


def block_lanes(ref, b, lanes):
    return ref[b, :, :, lanes].reshape(D, lanes.stop - lanes.start)


def block_rows(ref, b, half):
    return ref[b, half * 16 : half * 16 + 16].reshape(256, D)


def store_grad(place_ref, keep_ref, send_ref, b, half, rows):
    first = place_ref[2] == 0
    rows = rows.astype(BF)
    for zz in range(2):
        for x in range(4):
            base = (zz * 8 + (x % 2) * 4 + x // 2) * 16
            one, two = rows[base : base + 16], rows[base + 32 : base + 48]
            keep_ref[half * 2 + zz, x, b] = jnp.where(first, one, two)
            send_ref[half * 2 + zz, x, b] = jnp.where(first, two, one)


def pack_blocks(layer, qkv_ref, proj_ref, expand_ref, contract_ref, heads_ref, units_ref, store):
    every = slice(None)
    store(3, every, proj_ref[layer].astype(BF))
    for b in range(4):
        store(8 + b, every, contract_ref[layer, 16 * b : 16 * b + 16, :].astype(BF))
    for g in range(GROUPS):
        lanes = slice(128 * g, 128 * g + 128)
        part = dot(qkv_ref[layer, :, 384 * g : 384 * g + 384].astype(BF), heads_ref[...]).astype(BF)
        for s in range(3):
            store(s, lanes, part[:, 128 * s : 128 * s + 128])
        part = dot(expand_ref[layer, :, 512 * g : 512 * g + 512].astype(BF), units_ref[...]).astype(BF)
        for b in range(4):
            store(4 + b, lanes, part[:, 128 * b : 128 * b + 128])


def pack_kernel(*refs):
    one_ref, two_ref = refs[6:]

    def store(b, lanes, value):
        if b < 6:
            for i in range(4):
                one_ref[i, b, :, lanes] = value
        else:
            two_ref[b - 6, :, lanes] = value

    pack_blocks(0, *refs[:6], store)


def pack_next_kernel(*refs):
    spread_ref, rest_ref = refs[6:]

    def store(b, lanes, value):
        if b < 3:
            for i in range(16):
                spread_ref[i, b, :, lanes] = value
        else:
            rest_ref[b - 3, :, lanes] = value

    pack_blocks(1, *refs[:6], store)


def stack_kernel(*refs):
    for k in range(4):
        refs[4][k] = refs[k][...]


def stack_spread_kernel(*refs):
    for k in range(4):
        for x in range(4):
            refs[4][x, k] = refs[k][...]


def enter_kernel(x_ref, gain_ref, bias_ref, place_ref, hp_ref):
    hat, _ = normalized(x_ref[...].astype(F32))
    h = (hat * gain_ref[...] + bias_ref[...]).astype(BF)
    hp_ref[...] = dot(place_ref[...], h).astype(BF)


def attend_pairs(qkv_ref, first, table_ref, mask_ref, attn_ref, into_ref):
    def one_pair(p, carry):
        start = pl.multiple_of(first + p * 128, 128)
        for g in range(GROUPS):
            lane = g * 128
            keys = head_rows(side_by_side(qkv_ref, start, D + lane))
            queries = block_diagonal(side_by_side(qkv_ref, start, lane))
            scores = dot_nt(keys, queries) * (HEAD_DIM**-0.5 * log2e) + table_ref[g * 256 : (g + 1) * 256, :]
            scores = scores.reshape(4, SLOT, 128)
            if mask_ref is not None:
                scores = jnp.where(mask_ref[p][None] > 0, scores, masked_score)
            scores = jnp.exp2(scores - jnp.max(scores, 1, keepdims=True))
            scores = scores * (1.0 / jnp.sum(scores, 1, keepdims=True))
            attn = scores.reshape(256, 128).astype(BF)
            attn_ref[p, g] = attn
            values = head_rows(side_by_side(qkv_ref, start, 2 * D + lane))
            store_diagonal(into_ref, pl.multiple_of(p * 128, 128), lane, dot_tn(attn, values))
        return carry

    lax.fori_loop(0, PAIRS // 2, one_pair, 0)


def attend_kernel(shifted, moves, *refs):
    count = 2 if shifted else 8
    coords_ref, pieces, refs = refs[0], refs[1 : count + 1], refs[count + 1 :]
    if shifted:
        h_ref, rows_ref, cols_ref, corner_ref, place_ref, bias_ref, table_ref, mask_ref, take_ref = refs[:9]
        w_ref, hp_ref, qkv_ref, one_ref, two_ref, ctxp_ref, rows_out, cols_out, corner_out, sems = refs[9:]
        copies = assembly(coords_ref, [(pieces, "zx", (0, 3), 0)], w_ref, sems)
        moves.need(place_ref, h_ref)
        place = place_ref[...]
        hp = dot(place[:, :CELLS], h_ref[...])
        slabs = jnp.concatenate([rows_ref[...], cols_ref[...], corner_ref[...]], 0)
        hp_ref[...] = (hp + dot(place[:, CELLS:], slabs)).astype(BF)
        moves.ship(hp_ref)
    else:
        hp_ref, bias_ref, table_ref, place_ref = refs[:4]
        w_ref, qkv_ref, one_ref, two_ref, ctx_ref, ctxp_ref, sems = refs[4:]
        mask_ref = None
        copies = assembly(coords_ref, [(pieces, "by z", (0, 3), 0)], w_ref, sems)
        moves.need(hp_ref)
    for c in copies:
        c.wait()
    moves.ship(w_ref)
    for s in range(3):
        for half in range(2):
            lanes = slice(half * 256, half * 256 + 256)
            wide = slice(s * D + half * 256, s * D + half * 256 + 256)
            qkv_ref[:, wide] = (dot(hp_ref[...], block_lanes(w_ref, s, lanes)) + bias_ref[:, wide]).astype(BF)
        moves.ship(qkv_ref, columns(s))
    upper = PADDED // 2
    masks = (None, None) if mask_ref is None else (mask_ref.at[:4], mask_ref.at[4:])
    moves.need(table_ref)
    if shifted:
        moves.need(mask_ref)
    attend_pairs(qkv_ref, 0, table_ref, masks[0], one_ref, ctxp_ref.at[:upper])
    moves.ship(one_ref)
    attend_pairs(qkv_ref, upper, table_ref, masks[1], two_ref, ctxp_ref.at[upper:])
    moves.ship(two_ref)
    if shifted:
        moves.ship(ctxp_ref)
        moves.need(take_ref)
        sent = dot(take_ref[...], ctxp_ref[...]).astype(BF)
        rows_out[...] = sent[:SLAB]
        cols_out[...] = sent[SLAB : 2 * SLAB]
        corner_out[...] = sent[2 * SLAB :]
    else:
        moves.need(place_ref)
        ctx_ref[...] = dot(place_ref[...], ctxp_ref[...]).astype(BF)


def feed_forward(moves, x_ref, ctx_ref, w_ref, vectors, mid_ref, h2_ref, hidden_ref, slope_ref):
    bp_ref, g2_ref, b2_ref, bo_ref, bh_ref = vectors
    mid_ref[...] = x_ref[...].astype(F32) + dot(ctx_ref[...], block(w_ref, 0)) + bp_ref[...]
    moves.ship(mid_ref)
    hat, _ = normalized(mid_ref[...])
    h2_ref[...] = (hat * g2_ref[...] + b2_ref[...]).astype(BF)
    moves.ship(h2_ref)
    for b in range(4):
        for half in range(2):
            lanes = slice(half * 256, half * 256 + 256)
            wide = slice(b * D + half * 256, b * D + half * 256 + 256)
            pre = dot(h2_ref[...], block_lanes(w_ref, 1 + b, lanes)) + bh_ref[:, wide]
            hidden, slope = gelu_both(pre)
            hidden_ref[:, wide] = hidden.astype(BF)
            slope_ref[:, wide] = slope.astype(BF)
        moves.ship(hidden_ref, columns(b))
        moves.ship(slope_ref, columns(b))
    out = mid_ref[...] + bo_ref[...]
    for b in range(4):
        out = out + dot(hidden_ref[:, b * D : (b + 1) * D], block(w_ref, 5 + b))
    return out


def forward_kernel(moves, *refs):
    coords_ref, ones, twos, refs = refs[0], refs[1:9], refs[9:17], refs[17:]
    x_ref, ctx_ref, *vectors = refs[:7]
    g1_ref, b1_ref, take_ref, w_ref, *kept = refs[7:15]
    out_ref, h_ref, rows_out, cols_out, corner_out, sems = refs[15:]
    copies = assembly(coords_ref, [(ones, "by z", (3, 3), 0), (twos, "by x", (0, 6), 3)], w_ref, sems)
    moves.need(ctx_ref)
    for c in copies:
        c.wait()
    moves.ship(w_ref)
    moves.need(x_ref)
    out = feed_forward(moves, x_ref, ctx_ref, w_ref, vectors, *kept)
    out_ref[...] = out
    moves.ship(out_ref)
    hat, _ = normalized(out)
    h_ref[...] = (hat * g1_ref[...] + b1_ref[...]).astype(BF)
    moves.ship(h_ref)
    moves.need(take_ref)
    sent = dot(take_ref[...], h_ref[...]).astype(BF)
    rows_out[...] = sent[:SLAB]
    cols_out[...] = sent[SLAB : 2 * SLAB]
    corner_out[...] = sent[2 * SLAB :]


def hidden_back_pass(moves, gm_ref, slope_ref, w_ref, dpre_ref, dbh_ref):
    moves.need(w_ref, part=0)
    for b in range(4):
        moves.need(slope_ref, part=b)
        for half in range(2):
            wide = slice(b * D + half * 256, b * D + half * 256 + 256)
            dpre = dot_nt(gm_ref[...], block_rows(w_ref, 5 + b, half)) * slope_ref[:, wide].astype(F32)
            dpre = dpre.astype(BF)
            dpre_ref[:, wide] = dpre
            dbh_ref[:, wide] = jnp.sum(dpre.astype(F32), 0, keepdims=True)
        moves.ship(dpre_ref, columns(b))


def middle_back_pass(moves, grad_ref, dpre_ref, w_ref, mid_ref, g2_ref, dmid_ref, go_ref, small_ref):
    moves.need(w_ref)
    moves.need(dpre_ref, part=0)
    dh2 = dot_nt(dpre_ref[:, :D], block(w_ref, 1))
    for b in range(1, 4):
        moves.need(dpre_ref, part=b)
        dh2 = dh2 + dot_nt(dpre_ref[:, b * D : (b + 1) * D], block(w_ref, 1 + b))
    moves.need(mid_ref, grad_ref)
    dx, dg2, db2 = norm_back(dh2, mid_ref[...], g2_ref[...])
    small_ref[1:2, :] = dg2
    small_ref[2:3, :] = db2
    dmid_ref[...] = grad_ref[...].astype(F32) + dx
    moves.ship(dmid_ref)
    go_ref[...] = dmid_ref[...].astype(BF)
    moves.ship(go_ref)
    small_ref[0:1, :] = jnp.sum(go_ref[...].astype(F32), 0, keepdims=True)


def turn_kernel(moves, *refs):
    coords_ref, pieces, refs = refs[0], refs[1:3], refs[3:]
    x_ref, ctxp_ref, rows_ref, cols_ref, corner_ref, place_ref, *vectors = refs[:11]
    g_ref, take_ref, out_ref, dmid_ref, small_ref, dbh_ref, dctx_ref, rows_out, cols_out, corner_out = refs[11:21]
    keep_ref, send_ref, w_ref, ctx_ref, mid_ref, h2_ref, hidden_ref, slope_ref, dpre_ref, go_ref, sems = refs[21:]
    copies = assembly(coords_ref, [(pieces, "z", (0, 9), 0)], w_ref, sems)
    moves.need(place_ref, ctxp_ref)
    place = place_ref[...]
    slabs = jnp.concatenate([rows_ref[...], cols_ref[...], corner_ref[...]], 0)
    ctx_ref[...] = (dot(place[:, :PADDED], ctxp_ref[...]) + dot(place[:, PADDED:], slabs)).astype(BF)
    for c in copies:
        c.wait()
    moves.need(x_ref)
    out = feed_forward(moves, x_ref, ctx_ref, w_ref, vectors, mid_ref, h2_ref, hidden_ref, slope_ref)
    out_ref[...] = out.astype(BF)
    moves.ship(out_ref)
    moves.need(g_ref)
    small_ref[3:4, :] = jnp.sum(g_ref[...].astype(F32), 0, keepdims=True)
    hidden_back_pass(moves, g_ref, slope_ref, w_ref, dpre_ref, dbh_ref)
    middle_back_pass(moves, g_ref, dpre_ref, w_ref, mid_ref, vectors[1], dmid_ref, go_ref, small_ref)
    dctx_ref[...] = dot_nt(go_ref[...], block(w_ref, 0)).astype(BF)
    moves.ship(dctx_ref)
    moves.need(take_ref)
    sent = dot(take_ref[...], dctx_ref[...]).astype(BF)
    rows_out[...] = sent[:SLAB]
    cols_out[...] = sent[SLAB : 2 * SLAB]
    corner_out[...] = sent[2 * SLAB :]
    hidden_grads(moves, coords_ref, 1, g_ref, hidden_ref, h2_ref, dpre_ref, keep_ref, send_ref)
    for half in range(2):
        rows = slice(half * 256, half * 256 + 256)
        store_grad(coords_ref, keep_ref, send_ref, 0, half, dot_tn(ctx_ref[:, rows], go_ref[...]))
    moves.ship(keep_ref, of_blocks(0))
    moves.ship(send_ref, of_blocks(0))


def hidden_grads(moves, coords_ref, first, gm_ref, hidden_ref, h2_ref, dpre_ref, keep_ref, send_ref):
    for b in range(4):
        moves.need(hidden_ref, part=b)
        for half in range(2):
            wide = slice(b * D + half * 256, b * D + half * 256 + 256)
            grad_c = dot_tn(hidden_ref[:, wide], gm_ref[...])
            store_grad(coords_ref, keep_ref, send_ref, first + 4 + b, half, grad_c)
        moves.ship(keep_ref, of_blocks(first + 4 + b))
        moves.ship(send_ref, of_blocks(first + 4 + b))
    moves.need(h2_ref, dpre_ref)
    for b in range(4):
        for half in range(2):
            rows = slice(half * 256, half * 256 + 256)
            grad_e = dot_tn(h2_ref[:, rows], dpre_ref[:, b * D : (b + 1) * D])
            store_grad(coords_ref, keep_ref, send_ref, first + b, half, grad_e)
        moves.ship(keep_ref, of_blocks(first + b))
        moves.ship(send_ref, of_blocks(first + b))


def back_first_kernel(moves, *refs):
    coords_ref, dmid1_ref, dhp_ref, rows_ref, cols_ref, corner_ref, back_ref, x1_ref, g1_ref = refs[:9]
    hidden_ref, slope_ref, h2_ref, w_ref = refs[9:13]
    grad_ref, dpre_ref, keep_ref, send_ref, dbo_ref, dbh_ref, above_ref, gm_ref = refs[13:]
    moves.need(back_ref, dhp_ref)
    back = back_ref[...]
    slabs = jnp.concatenate([rows_ref[...], cols_ref[...], corner_ref[...]], 0)
    dh = dot(back[:, :PADDED], dhp_ref[...]) + dot(back[:, PADDED:], slabs)
    moves.need(x1_ref)
    dx, dg1, db1 = norm_back(dh, x1_ref[...], g1_ref[...])
    above_ref[0:1, :] = dg1
    above_ref[1:2, :] = db1
    moves.need(dmid1_ref)
    grad = dmid1_ref[...] + dx
    grad_ref[...] = grad
    moves.ship(grad_ref)
    gm_ref[...] = grad.astype(BF)
    dbo_ref[...] = jnp.sum(gm_ref[...].astype(F32), 0, keepdims=True)
    hidden_back_pass(moves, gm_ref, slope_ref, w_ref, dpre_ref, dbh_ref)
    hidden_grads(moves, coords_ref, 0, gm_ref, hidden_ref, h2_ref, dpre_ref, keep_ref, send_ref)


def middle_first_kernel(moves, grad_ref, dpre_ref, mid_ref, ctx_ref, w_ref, g2_ref, place_ref, *outs):
    dmid_ref, dwp_ref, small_ref, dctxp_ref, go_ref = outs
    middle_back_pass(moves, grad_ref, dpre_ref, w_ref, mid_ref, g2_ref, dmid_ref, go_ref, small_ref)
    moves.need(ctx_ref)
    for half in range(2):
        rows = slice(half * 256, half * 256 + 256)
        dwp_ref[rows, :] = dot_tn(ctx_ref[:, rows], go_ref[...]).astype(BF)
    moves.ship(dwp_ref)
    dctx = dot_nt(go_ref[...], block(w_ref, 0)).astype(BF)
    moves.need(place_ref)
    dctxp_ref[...] = dot(place_ref[...], dctx).astype(BF)


def attend_back_pairs(first, qkv_ref, attn_ref, dctxp_ref, dqkv_ref, dtable_ref):
    if first == 0:
        dtable_ref[...] = jnp.zeros_like(dtable_ref)
    scale = HEAD_DIM**-0.5

    def one_pair(p, carry):
        start = pl.multiple_of(first + p * 128, 128)
        for g in range(GROUPS):
            lane = g * 128
            attn = attn_ref[p, g]
            keys = head_rows(side_by_side(qkv_ref, start, D + lane))
            values = head_rows(side_by_side(qkv_ref, start, 2 * D + lane))
            queries = block_diagonal(side_by_side(qkv_ref, start, lane))
            grads = block_diagonal(side_by_side(dctxp_ref, start, lane))
            probs = attn.astype(F32).reshape(4, SLOT, 128)
            dprobs = dot_nt(values, grads).reshape(4, SLOT, 128)
            dscores = probs * (dprobs - jnp.sum(probs * dprobs, 1, keepdims=True))
            dscores = dscores.reshape(256, 128).astype(BF)
            dtable_ref[g * 256 : (g + 1) * 256, :] += dscores.astype(F32)
            store_diagonal(dqkv_ref, start, lane, dot_tn(dscores, keys) * scale)
            dkeys = (head_fold(dot(dscores, queries)) * scale).astype(BF)
            dqkv_ref[pl.ds(start, SLOT), D + lane : D + lane + 128] = dkeys[:, :128]
            dqkv_ref[pl.ds(start + SLOT, SLOT), D + lane : D + lane + 128] = dkeys[:, 128:]
            dvalues = head_fold(dot(attn, grads)).astype(BF)
            dqkv_ref[pl.ds(start, SLOT), 2 * D + lane : 2 * D + lane + 128] = dvalues[:, :128]
            dqkv_ref[pl.ds(start + SLOT, SLOT), 2 * D + lane : 2 * D + lane + 128] = dvalues[:, 128:]
        return carry

    lax.fori_loop(0, PAIRS // 2, one_pair, 0)


def table_sum(dtable_ref, by_key_ref, out_ref):
    total = jnp.zeros((2 * HEADS, 256), F32)
    row = lax.broadcasted_iota(jnp.int32, (256, 256), 0)
    for c in range(25):
        hot = jnp.where(row == by_key_ref[c : c + 1, :], 1.0, 0.0).astype(BF)
        keys = [dtable_ref[pl.ds(2 * c + k, HEADS, stride=SLOT), :] for k in range(2)]
        rows = jnp.concatenate(keys, 1)
        high = rows.astype(BF)
        low = (rows - high.astype(F32)).astype(BF)
        total = total + dot_nt(jnp.concatenate([high, low], 0), hot)
    out_ref[...] = total[:HEADS] + total[HEADS:]


def attend_back_kernel(moves, *refs):
    dctx_ref, rows_ref, cols_ref, corner_ref, place_ref, qkv_ref, one_ref, two_ref, w_ref, take_ref, key_ref = refs[:11]
    dqkv_ref, dbias_ref, table_ref, dhp_ref, rows_out, cols_out, corner_out, dctxp_ref, dtable_ref = refs[11:]
    moves.need(place_ref, dctx_ref)
    place = place_ref[...]
    slabs = jnp.concatenate([rows_ref[...], cols_ref[...], corner_ref[...]], 0)
    dctxp_ref[...] = (dot(place[:, :CELLS], dctx_ref[...]) + dot(place[:, CELLS:], slabs)).astype(BF)
    moves.need(qkv_ref, one_ref)
    attend_back_pairs(0, qkv_ref, one_ref, dctxp_ref, dqkv_ref, dtable_ref)
    moves.need(two_ref)
    attend_back_pairs(PADDED // 2, qkv_ref, two_ref, dctxp_ref, dqkv_ref, dtable_ref)
    moves.ship(dqkv_ref)
    moves.need(w_ref)
    table_sum(dtable_ref, key_ref, table_ref)
    for s in range(3):
        dbias_ref[s : s + 1, :] = jnp.sum(dqkv_ref[:, s * D : (s + 1) * D].astype(F32), 0, keepdims=True)
    dhp = dot_nt(dqkv_ref[:, :D], block(w_ref, 0))
    for s in range(1, 3):
        dhp = dhp + dot_nt(dqkv_ref[:, s * D : (s + 1) * D], block(w_ref, s))
    dhp_ref[...] = dhp.astype(BF)
    moves.ship(dhp_ref)
    moves.need(take_ref)
    sent = dot(take_ref[...], dhp_ref[...]).astype(BF)
    rows_out[...] = sent[:SLAB]
    cols_out[...] = sent[SLAB : 2 * SLAB]
    corner_out[...] = sent[2 * SLAB :]


def grads_heads_kernel(moves, coords_ref, hp_ref, dqkv_ref, keep_ref, send_ref):
    moves.need(hp_ref)
    for s in range(3):
        moves.need(dqkv_ref, part=s)
        for half in range(2):
            rows = slice(half * 256, half * 256 + 256)
            grad_w = dot_tn(hp_ref[:, rows], dqkv_ref[:, s * D : (s + 1) * D])
            store_grad(coords_ref, keep_ref, send_ref, s, half, grad_w)
        moves.ship(keep_ref, of_blocks(s))
        moves.ship(send_ref, of_blocks(s))


def attend_back_end_kernel(moves, *refs):
    coords_ref, dctxp_ref, qkv_ref, one_ref, two_ref, hp_ref, dwp_ref, key_ref, w_ref, place_ref = refs[:10]
    x_ref, dmid_ref, g1_ref, norm1, dqb1, sums1, dbh1, table1, sums0, dbo0, dbh0 = refs[10:21]
    keep_ref, send_ref, out_ref, sums_ref, dqkv_ref, dtable_ref, dhp_ref = refs[21:]
    moves.need(dctxp_ref, qkv_ref, one_ref)
    attend_back_pairs(0, qkv_ref, one_ref, dctxp_ref, dqkv_ref, dtable_ref)
    moves.need(two_ref)
    attend_back_pairs(PADDED // 2, qkv_ref, two_ref, dctxp_ref, dqkv_ref, dtable_ref)
    moves.need(hp_ref)
    dqb = []
    for s in range(3):
        wide = slice(s * D, (s + 1) * D)
        dqb.append(jnp.sum(dqkv_ref[:, wide].astype(F32), 0, keepdims=True))
        for half in range(2):
            rows = slice(half * 256, half * 256 + 256)
            grad_w = dot_tn(hp_ref[:, rows], dqkv_ref[:, wide])
            store_grad(coords_ref, keep_ref, send_ref, s, half, grad_w)
    moves.need(dwp_ref)
    for half in range(2):
        store_grad(coords_ref, keep_ref, send_ref, 3, half, dwp_ref[half * 256 : half * 256 + 256, :])
    moves.ship(keep_ref)
    moves.ship(send_ref)
    moves.need(w_ref)
    dhp = dot_nt(dqkv_ref[:, :D], block(w_ref, 0))
    for s in range(1, 3):
        dhp = dhp + dot_nt(dqkv_ref[:, s * D : (s + 1) * D], block(w_ref, s))
    dhp_ref[...] = dhp.astype(BF)
    moves.need(place_ref, x_ref, dmid_ref)
    dh = dot(place_ref[...], dhp_ref[...])
    dx, dg1, db1 = norm_back(dh, x_ref[...].astype(F32), g1_ref[...])
    out_ref[...] = dmid_ref[...] + dx
    moves.ship(out_ref)
    for at, norm, query, value, sums, dbo, dbh in (
        (0, (dg1, db1), dqb[0], dqb[2], sums0, dbo0[...], dbh0),
        (12, (norm1[0:1, :], norm1[1:2, :]), dqb1[0:1, :], dqb1[2:3, :], sums1, sums1[3:4, :], dbh1),
    ):
        rows = [*norm, query, value, sums[0:1, :], sums[1:2, :], sums[2:3, :], dbo]
        rows += [dbh[:, D * b : D * b + D] for b in range(4)]
        for i, row in enumerate(rows):
            sums_ref[at + i : at + i + 1, :] = row
    table_sum(dtable_ref, key_ref, sums_ref.at[24:40, 0:256])
    sums_ref[24:40, 256:512] = table1[...]


def add_kernel(*refs):
    out_ref, at = refs[-1], 0
    for i in range(0, len(refs) - 1, 2):
        n = refs[i].shape[2]
        total = refs[i][...].astype(F32) + refs[i + 1][...].astype(F32)
        out_ref[:, :, at : at + n] = total.astype(BF)
        at += n


def sum_split_kernel(coords_ref, parts_ref, *outs):
    for d, out in enumerate(outs):
        target = lax.rem(coords_ref[1] + d, 4)
        total = parts_ref[0, target].astype(F32)
        for k in range(1, 4):
            total = total + parts_ref[k, target].astype(F32)
        out[...] = total.astype(BF)


def to_xz_kernel(coords_ref, keep_ref, other_ref, parts_ref, sums_ref, more_ref, near_ref, *outs):
    smalls = jnp.concatenate([sums_ref[...] + more_ref[...], jnp.zeros((8, D), F32)], 0)
    high = smalls.astype(BF).astype(F32)
    low = smalls - high
    for z in range(4):
        for x in range(4):
            total = keep_ref[z, x].astype(F32) + other_ref[z, x].astype(F32)
            near_ref[4 * z + x, 0:4] = total.astype(BF)
            at = 3 * (4 * z + x)
            rows = [high[at : at + 3], low[at : at + 3], jnp.zeros((10, D), F32)]
            near_ref[4 * z + x, 4] = jnp.concatenate(rows, 0).astype(BF)
    for d, out in enumerate(outs):
        target = lax.rem(coords_ref[1] + d, 4)
        total = parts_ref[0, target].astype(F32)
        for k in range(1, 4):
            total = total + parts_ref[k, target].astype(F32)
        out[...] = total.astype(BF)


def to_seq_kernel(near_ref, *refs):
    pieces, late_ref, small_ref = refs[:4], refs[4], refs[5]
    total = near_ref[0].astype(F32)
    for i in range(1, 16):
        total = total + near_ref[i].astype(F32)
    late_ref[0:4] = total[0:4].astype(BF)
    rows = total[4, 0:3] + total[4, 3:6]
    rows = [rows[r : r + 1, 128 * q : 128 * q + 128] for r in range(3) for q in range(4)]
    rows = jnp.concatenate(rows + [jnp.zeros((4, 128), F32)], 0)
    for i in range(64):
        small_ref[i] = rows
    total = pieces[0][...].astype(F32)
    for piece in pieces[1:]:
        total = total + piece[...].astype(F32)
    late_ref[4:15] = total.astype(BF)


def four(refs, b):
    return (refs[0][b].astype(F32) + refs[1][b].astype(F32)) + (refs[2][b].astype(F32) + refs[3][b].astype(F32))


def reorder(values, order):
    n = values.shape[0]
    high = values.astype(BF)
    rest = values - high.astype(F32)
    low = rest.astype(BF)
    last = (rest - low.astype(F32)).astype(BF)
    rows = dot_nt(jnp.concatenate([high, low, last], 0), order)
    return rows[:n] + rows[n : 2 * n] + rows[2 * n :]


def step_into(at, grad, old, new, rate, decay):
    weight, first, second = (ref[at] for ref in old)
    for ref, value in zip(new, adamw(weight, first, second, grad, rate, decay)):
        ref[at] = value


def update_small_kernel(*refs):
    smalls_ref, units_ref, small, table = refs[0], refs[1], refs[2:5], refs[5:8]
    new_small, new_table, bias_ref, sums_ref = refs[8:11], refs[11:14], refs[14], refs[15]
    for i in range(16):
        part = (smalls_ref[4 * i] + smalls_ref[4 * i + 1]) + (smalls_ref[4 * i + 2] + smalls_ref[4 * i + 3])
        for k in range(12):
            sums_ref[3 * i + k // 4 : 3 * i + k // 4 + 1, k % 4 * 128 : k % 4 * 128 + 128] = part[k : k + 1]
    for layer in range(LAYERS):
        rows = [sums_ref[12 * layer + i : 12 * layer + i + 1, :] for i in range(12)]
        bias_ref[layer : layer + 1, :] = rows[7]
        parts = [
            jnp.concatenate([rows[8 + b][:, 128 * g : 128 * g + 128] for b in range(4)], 1) for g in range(GROUPS)
        ]
        units = reorder(jnp.concatenate(parts + [jnp.zeros((12, D), F32)], 0), units_ref[...])
        for i, grad in enumerate(rows[:8] + [units[g : g + 1] for g in range(GROUPS)]):
            at = (slice(layer, layer + 1), slice(D * i, D * i + D))
            step_into(at, grad, small, new_small, 0.3, 0.0)
        step_into((layer,), sums_ref[24:40, 256 * layer : 256 * layer + REL], table, new_table, 0.6, 0.0)


def update_kernel(*refs):
    early, late, heads_ref, units_ref, refs = refs[:4], refs[4:8], refs[8], refs[9], refs[10:]
    old = [refs[3 * i : 3 * i + 3] for i in range(4)]
    new = [refs[12 + 3 * i : 15 + 3 * i] for i in range(4)]

    def layer_step(heads, head_at, rest, rest_at):
        step_into((0,), four(rest, rest_at), old[1], new[1], 0.1, 0.05)
        for b in range(4):
            step_into((0, slice(16 * b, 16 * b + 16)), four(rest, rest_at + 5 + b), old[3], new[3], 0.03, 0.05)
        for n, wide, order_ref, i, pieces, at in (
            (3, 384, heads_ref, 0, heads, head_at),
            (4, 512, units_ref, 2, rest, rest_at + 1),
        ):
            grads = [four(pieces, at + b) for b in range(n)]
            for g in range(GROUPS):
                part = jnp.concatenate([v[:, 128 * g : 128 * g + 128] for v in grads], 1)
                lanes = (0, slice(None), slice(wide * g, wide * g + wide))
                step_into(lanes, reorder(part, order_ref[...]), old[i], new[i], 0.03, 0.05)

    @pl.when(pl.program_id(0) == 0)
    def _():
        layer_step(late, 0, late, 3)

    @pl.when(pl.program_id(0) == 1)
    def _():
        layer_step(late, 12, early, 0)


def to_neighbours(slabs, ahead):
    step = -1 if ahead else 1
    along = [(i, (i + step) % 4) for i in range(4)]
    over = [(0, 1), (1, 0)]
    both = [(i * 2 + c, ((i + step) % 4) * 2 + 1 - c) for i in range(4) for c in range(2)]
    rows, cols, corner = slabs
    return (
        lax.ppermute(rows, "seq", along),
        lax.ppermute(cols, "col", over),
        lax.ppermute(corner, ("seq", "col"), both),
    )


def flat(z, x, core):
    return (z * 4 + (x % 2) * 2 + core) * 2 + x // 2


ALONG_X = [[flat(z, x, core) for x in range(4)] for z in range(4) for core in range(2)]
OVER_XZ = [[flat(z, x, core) for z in range(4) for x in range(4)] for core in range(2)]
OVER_CHIPS = [[i * 4 + y for i in group for y in range(4)] for group in OVER_XZ]
OTHER_CORE = [(i, i ^ 1) for i in range(16)]


def from_z(distance):
    return [(((z + distance) % 4) * 4 + k, z * 4 + k) for z in range(4) for k in range(4)]


def from_x(distance):
    return [(flat(z, (x + distance) % 4, c), flat(z, x, c)) for z in range(4) for x in range(4) for c in range(2)]


ALONG_Z = [[z * 4 + k for z in range(4)] for k in range(4)]


def scattered_z(value):
    return lax.all_to_all(value, "img", 0, 0, tiled=True, axis_index_groups=ALONG_Z)


def from_core(value):
    return lax.ppermute(value, "img", OTHER_CORE)


BY_SEQ = [[(i, i ^ d) for i in range(4)] for d in (1, 2, 3)]
BY_Z = [[(z * 4 + k, (z ^ d) * 4 + k) for z in range(4) for k in range(4)] for d in (1, 2, 3)]
def both_cores(*pairs):
    arrays = [a for pair in pairs for a in pair]
    specs = [pl.BlockSpec((1, *a.shape[1:]), lambda i: (i, 0, 0, 0, 0)) for a in arrays]
    shape = (4, 4, sum(keep.shape[2] for keep, _ in pairs), 16, D)
    size = math.prod(shape) * 2
    return pl.pallas_call(
        add_kernel,
        grid=(4,),
        out_shape=jax.ShapeDtypeStruct(shape, BF),
        in_specs=specs,
        out_specs=pl.BlockSpec((1, *shape[1:]), lambda i: (i, 0, 0, 0, 0)),
        compiler_params=pltpu.CompilerParams(vmem_limit_bytes=VMEM_BYTES),
        cost_estimate=pl.CostEstimate(flops=size, bytes_accessed=3 * size, transcendentals=0),
    )(*arrays)


def by_seq(value):
    return [value] + [lax.ppermute(value, "seq", p) for p in BY_SEQ]


def update(early, late, heads, units, state):
    whole = [pl.BlockSpec(memory_space=pltpu.VMEM)] * 10
    parts = [pl.BlockSpec((1, *a.shape[1:]), lambda layer: (layer, 0, 0)) for a in state]
    return pl.pallas_call(
        update_kernel,
        grid=(LAYERS,),
        out_shape=[jax.ShapeDtypeStruct(a.shape, F32) for a in state],
        in_specs=whole + parts,
        out_specs=parts,
        compiler_params=pltpu.CompilerParams(vmem_limit_bytes=VMEM_BYTES),
        cost_estimate=pl.CostEstimate(flops=8 * 10**9, bytes_accessed=8 * 10**6, transcendentals=0),
    )(*early, *late, heads, units, *state)


def adamw(weight, first, second, grad, rate, decay):
    first = 0.9 * first + 0.1 * grad
    second = 0.999 * second + 0.001 * grad * grad
    first_hat = first / (1.0 - 0.9**STEP)
    second_hat = second / (1.0 - 0.999**STEP)
    return (first, second, weight - rate * (first_hat / (jnp.sqrt(second_hat) + 1e-08) + decay * weight))


def hidden_order(vector):
    return vector.reshape(32, 4, 16).transpose(1, 0, 2).reshape(HIDDEN)


def split_small(vector):
    pieces = [vector[i * D : (i + 1) * D][None] for i in range(8)]
    return pieces + [hidden_order(vector[8 * D :])[None]]


def score_table(table, hot):
    rows = lax.dot_general(table, hot, (((0,), (0,)), ((), ())), precision=highest, preferred_element_type=F32)
    rows = rows.reshape(HEADS, AREA, AREA) * log2e
    rows = jnp.pad(rows, ((0, 0), (0, 0), (0, SLOT - AREA)))
    rows = jnp.pad(rows, ((0, 0), (0, SLOT - AREA), (0, 0)), constant_values=padded_score)
    return jnp.concatenate([rows, rows], 2).reshape(HEADS * SLOT, 128)


def allowed_pairs(region):
    win = region.reshape(4, WIN, 4, WIN).transpose(0, 2, 1, 3).reshape(16, AREA)
    win = jnp.pad(win, ((0, 0), (0, SLOT - AREA)))
    same = win[:, :, None] == win[:, None, :]
    same = same | (jnp.arange(SLOT) >= AREA)[None, :, None]
    same = same.reshape(PAIRS, 2, SLOT, SLOT).transpose(0, 2, 1, 3).reshape(PAIRS, SLOT, 128)
    return same.astype(F32)


def local(
    images,
    out_grad,
    region_ids,
    rel_index,
    qkv_weight,
    qkv_first,
    qkv_second,
    proj_weight,
    proj_first,
    proj_second,
    expand_weight,
    expand_first,
    expand_second,
    contract_weight,
    contract_first,
    contract_second,
    small_params,
    small_first,
    small_second,
    bias_table,
    table_first,
    table_second,
):
    plain, plain_back, ahead, back, take_first, take_last = (jnp.asarray(a, BF) for a in placements())
    heads, units = (jnp.asarray(a, BF) for a in column_orders())
    img = lax.axis_index("img")
    x = lax.axis_index("col") * 2 + img // 2 % 2
    coords = jnp.stack([img // 4, x, img % 2]).astype(jnp.int32)
    matrices = (qkv_weight, proj_weight, expand_weight, contract_weight, heads, units)
    one, two = call(pack_kernel, [((4, 6, 16, D), BF), ((6, 16, D), BF)], matrices, us=3)

    def along_z(value):
        return [value] + [lax.ppermute(value, "img", from_z(d)) for d in (1, 2, 3)]

    def along_x(value):
        return [value] + [lax.ppermute(value, ("img", "col"), from_x(d)) for d in (1, 2, 3)]

    one0 = lax.all_to_all(one, ("img", "col"), 0, 0, tiled=True, axis_index_groups=ALONG_X)
    two0 = along_z(two)
    x0 = images.reshape(CELLS, D)
    g_out = out_grad.reshape(CELLS, D)
    by_key = jnp.pad(rel_index.T, ((0, 1), (0, SLOT - AREA)), constant_values=-1)
    by_key = jnp.concatenate([by_key, by_key], 1).reshape(25, 256)
    keys_hot = (jnp.arange(REL, dtype=jnp.int32)[:, None] == rel_index.T.reshape(1, AREA * AREA)).astype(F32)
    tables = [score_table(bias_table[layer], keys_hot) for layer in range(LAYERS)]
    region = lax.dynamic_slice_in_dim(region_ids, lax.axis_index("seq") * SIDE, SIDE, 0)
    mask = allowed_pairs(region)
    small = [split_small(small_params[layer]) for layer in range(LAYERS)]
    zero = jnp.zeros((1, D), F32)
    qkv_bias = [jnp.concatenate([s[2], zero, s[3]], 1) for s in small]

    by_columns = [columns(b) for b in range(4)]
    qkv_shape = ((PADDED, 3 * D), BF)
    attn_shape = ((PAIRS // 2, GROUPS, 256, 128), BF)
    slab_shapes = [((SLAB, D), BF), ((SLAB, D), BF), ((CORNER, D), BF)]
    cells16, cells32 = ((CELLS, D), BF), ((CELLS, D), F32)
    padded16 = ((PADDED, D), BF)
    wide16 = ((CELLS, HIDDEN), BF)

    copies = pltpu.SemaphoreType.DMA((32,))
    w_shapes = [((3, 32, 16, D), BF), ((9, 32, 16, D), BF)]
    g1, b1, _, _, bp, g2, b2, bo, bh = small[0]
    (hp0,) = call(enter_kernel, [padded16], (x0, g1, b1, plain), us=4)
    (two0,) = call(stack_kernel, [((4, 6, 16, D), BF)], two0, after=(hp0,))
    one0, two0 = along_z(one0), along_x(two0)
    one0 = one0 + [from_core(v) for v in one0]
    two0 = two0 + [from_core(v) for v in two0]
    half16 = ((PADDED // 2, D), BF)
    wq0, qkv0, attn0, attn0b, ctx0 = call(
        functools.partial(attend_kernel, False),
        [w_shapes[0], qkv_shape, attn_shape, attn_shape, cells16],
        (hp0, qkv_bias[0], tables[0], plain_back),
        [pltpu.VMEM(*padded16), copies],
        one0,
        coords,
        us=18,
        late=dict.fromkeys((0, 2, 3)),
        early=(0, 1, 2, 3),
    )
    spread, rest = call(
        pack_next_kernel, [((16, 3, 16, D), BF), ((9, 16, D), BF)], matrices, us=3, after=(ctx0,)
    )
    lines = lax.all_to_all(spread, ("img", "col"), 0, 0, tiled=True, axis_index_groups=OVER_XZ)
    one1 = [lines, from_core(lines)]
    wm0, mid0, h20, hidden0, slope0, x1, h1, *slabs = call(
        forward_kernel,
        [w_shapes[1], cells32, cells16, wide16, wide16, cells32, cells16, *slab_shapes],
        (x0, ctx0, bp, g2, b2, bo, bh, small[1][0], small[1][1], take_first),
        [pltpu.SemaphoreType.DMA((64,))],
        one0 + two0,
        coords,
        us=15,
        after=(spread, rest),
        late=dict.fromkeys((1, 0, 9)),
        early=(0, 1, 2, 3, 4, 5, 6),
    )
    (lines,) = call(stack_spread_kernel, [((4, 4, 9, 16, D), BF)], along_x(rest), us=2, after=(h1,))
    two1 = scattered_z(lines).reshape(16, 9, 16, D)
    g1, b1, _, _, bp, g2, b2, bo, bh = small[1]
    slabs = to_neighbours(slabs, True)
    wq1, hp1, qkv1, attn1, attn1b, ctxp1, *slabs = call(
        functools.partial(attend_kernel, True),
        [w_shapes[0], padded16, qkv_shape, attn_shape, attn_shape, padded16, *slab_shapes],
        (h1, *slabs, ahead, qkv_bias[1], tables[1], mask, take_last),
        [copies],
        one1,
        coords,
        us=18,
        after=(by_key,),
        late=dict.fromkeys((4, 0, 6, 7, 8)),
        early=(0, 1, 2, 3, 4, 5),
    )
    (two1,) = held((two1,), (hp1,))
    two1 = [two1, from_core(two1)]
    slabs = to_neighbours(slabs, False)
    out, dmid1, sums1, dbh1, dctx1, *slabs, keep, send = call(
        turn_kernel,
        [cells16, cells32, ((4, D), F32), ((1, HIDDEN), F32), cells16, *slab_shapes, *[((4, 4, 9, 16, D), BF)] * 2],
        (x1, ctxp1, *slabs, back, bp, g2, b2, bo, bh, g_out, take_first),
        [pltpu.VMEM(*a) for a in (w_shapes[1], cells16, cells32, cells16, wide16, wide16, wide16, cells16)] + [copies],
        two1,
        coords,
        us=34,
        late=dict.fromkeys((5, 1, 0, 11, 12)),
        early=(0, 1, 4, 8, 9),
    )
    slabs = to_neighbours(slabs, True)
    part_m1 = both_cores((keep, from_core(send)))
    dqkv1, dqb1, table1, dhp1, *slabs = call(
        attend_back_kernel,
        [qkv_shape, ((3, D), F32), ((HEADS, 256), F32), padded16, *slab_shapes],
        (dctx1, *slabs, ahead, qkv1, attn1, attn1b, wq1, take_last, by_key),
        [pltpu.VMEM((PADDED, D), BF), pltpu.VMEM((HEADS * SLOT, 128), F32)],
        us=20,
        after=(part_m1,),
        late=dict.fromkeys((4, 0, 5, 6, 7, 8, 9)),
        early=(0, 3),
    )
    slabs = to_neighbours(slabs, False)
    keep, send = call(
        grads_heads_kernel,
        [((4, 4, 3, 16, D), BF)] * 2,
        (hp1, dqkv1),
        place=coords,
        us=4,
        late={0: None, 1: by_columns[:3]},
        early=(0, 1),
    )
    pair_q1 = (keep, from_core(send))
    half_m1, *sent = call(sum_split_kernel, [((9, 16, D), BF)] * 4, (scattered_z(part_m1),), place=coords, us=2)
    grad1, dpre0, keep, send, dbo0, dbh0, norm1 = call(
        back_first_kernel,
        [cells32, wide16, *[((4, 4, 8, 16, D), BF)] * 2, ((1, D), F32), ((1, HIDDEN), F32), ((2, D), F32)],
        (dmid1, dhp1, *slabs, back, x1, small[1][0], hidden0, slope0, h20, wm0),
        [pltpu.VMEM((CELLS, D), BF)],
        place=coords,
        us=16,
        after=(half_m1, pair_q1[0]),
        late={5: None, 1: None, 6: None, 0: None, 11: [slice(5, 9)], 9: by_columns, 8: by_columns, 10: None},
        early=(0, 1, 2, 3),
    )
    got = [lax.ppermute(v, ("img", "col"), from_x(4 - d)) for d, v in zip((1, 2, 3), sent)]
    grad_m1 = sum((v.astype(F32) for v in got), half_m1.astype(F32)).astype(BF)
    dmid0, dwp0, sums0, dctxp0 = call(
        middle_first_kernel,
        [cells32, ((D, D), BF), ((3, D), F32), padded16],
        (grad1, dpre0, mid0, ctx0, wm0, small[0][5], plain),
        [pltpu.VMEM((CELLS, D), BF)],
        us=8,
        after=(grad_m1,),
        late={4: (0, 5), 1: by_columns, 2: None, 0: None, 3: None, 6: None},
        early=(0, 1),
    )
    part_0 = both_cores((keep, from_core(send)), pair_q1)
    grads_m1 = by_seq(grad_m1)
    half_0 = scattered_z(part_0)
    *keep_send, input_grad, sums = call(
        attend_back_end_kernel,
        [*[((4, 4, 4, 16, D), BF)] * 2, cells32, ((40, D), F32)],
        (dctxp0, qkv0, attn0, attn0b, hp0, dwp0, by_key, wq0, plain_back, x0, dmid0, small[0][0])
        + (norm1, dqb1, sums1, dbh1, table1, sums0, dbo0, dbh0),
        [pltpu.VMEM(*qkv_shape), pltpu.VMEM((HEADS * SLOT, 128), F32), pltpu.VMEM(*padded16)],
        place=coords,
        us=26,
        late=dict.fromkeys((0, 1, 2, 3, 4, 5, 7, 8, 9, 10)),
        early=(0, 1, 2),
        after=(part_0, *grads_m1),
    )
    other, more = from_core(keep_send[1]), from_core(sums)
    near, mine, *sent = call(
        to_xz_kernel,
        [((16, 5, 16, D), BF)] + [((11, 16, D), BF)] * 4,
        (keep_send[0], other, half_0, sums, more),
        place=coords,
        us=5,
    )
    near = lax.all_to_all(near, ("img", "col"), 0, 0, tiled=True, axis_index_groups=OVER_XZ)
    pieces = [mine] + [lax.ppermute(v, ("img", "col"), from_x(4 - d)) for d, v in zip((1, 2, 3), sent)]
    late, smalls = call(to_seq_kernel, [((15, 16, D), BF), ((64, 16, 128), F32)], (near, *pieces), us=3)
    late = by_seq(late)
    smalls = lax.all_to_all(smalls, ("img", "col", "seq"), 0, 0, tiled=True, axis_index_groups=OVER_CHIPS)

    state = (
        (qkv_weight, qkv_first, qkv_second),
        (proj_weight, proj_first, proj_second),
        (expand_weight, expand_first, expand_second),
        (contract_weight, contract_first, contract_second),
    )
    flat_state = [a for three in state for a in three]
    swap = functools.partial(jnp.transpose, axes=(0, 2, 1))
    small = (small_params, small_first, small_second, swap(bias_table), swap(table_first), swap(table_second))
    done = update(grads_m1, late, heads, units, flat_state)
    last = call(
        update_small_kernel,
        [(a.shape, F32) for a in small] + [((LAYERS, D), F32)],
        (smalls, units, *small),
        [pltpu.VMEM((48, D), F32)],
        us=3,
    )
    return (
        out.reshape(images.shape),
        input_grad.reshape(images.shape),
        *done,
        *last[:3],
        *(swap(a) for a in last[3:6]),
        last[6],
    )


def solution(mesh):
    cells = P("img", "seq", "col", None)
    matrix = P(None, ("img", "col"), None)
    in_specs = (cells, cells, P(None, "col"), P(), *([matrix] * 12), *([P()] * 6))
    out_specs = (cells, cells, *([matrix] * 12), *([P()] * 7))
    return jax.shard_map(local, mesh=mesh, in_specs=in_specs, out_specs=out_specs, check_vma=False)
```

```python
import functools
import math

import jax
import jax.numpy as jnp
import numpy as np
from jax import lax
from jax.experimental import pallas as pl
from jax.experimental.pallas import tpu as pltpu
from jax.sharding import PartitionSpec as P

D = 512
HEADS = 16
HEAD_DIM = 32
WIN = 7
SHIFT = 3
LAYERS = 2
STEP = 10
REL = 169
SIDE = 28
CELLS = SIDE * SIDE
AREA = WIN * WIN
SLOT = 64
PADDED = 16 * SLOT
PAIRS = 8
GROUPS = 4
SLAB = 96
CORNER = 16
HALO = 2 * SLAB + CORNER
HIDDEN = 4 * D

BF = jnp.bfloat16
F32 = jnp.float32
epsilon = 1e-05
log2e = math.log2(math.e)
masked_score = -1000000000.0 * log2e
padded_score = -1e30
highest = lax.Precision.HIGHEST
VMEM_BYTES = 58 * 2**20


def padded_row(r, c):
    return ((r // WIN) * 4 + c // WIN) * SLOT + (r % WIN) * WIN + c % WIN


def ahead_source(r, c):
    r, c = r + SHIFT, c + SHIFT
    if r < SIDE and c < SIDE:
        return r * SIDE + c
    if c < SIDE:
        return CELLS + (r - SIDE) * SIDE + c
    if r < SIDE:
        return CELLS + SLAB + r * SHIFT + c - SIDE
    return CELLS + 2 * SLAB + (r - SIDE) * SHIFT + c - SIDE


def back_source(r, c):
    if r >= SHIFT and c >= SHIFT:
        return padded_row(r - SHIFT, c - SHIFT)
    if c >= SHIFT:
        return PADDED + r * SIDE + c - SHIFT
    if r >= SHIFT:
        return PADDED + SLAB + (r - SHIFT) * SHIFT + c
    return PADDED + 2 * SLAB + r * SHIFT + c


def placements():
    plain = np.zeros((PADDED, CELLS), np.float32)
    ahead = np.zeros((PADDED, CELLS + HALO), np.float32)
    back = np.zeros((CELLS, PADDED + HALO), np.float32)
    take_first = np.zeros((HALO, CELLS), np.float32)
    take_last = np.zeros((HALO, PADDED), np.float32)
    for r in range(SIDE):
        for c in range(SIDE):
            plain[padded_row(r, c), r * SIDE + c] = 1
            ahead[padded_row(r, c), ahead_source(r, c)] = 1
            back[r * SIDE + c, back_source(r, c)] = 1
    edge = SIDE - SHIFT
    for a in range(SHIFT):
        for b in range(SIDE):
            take_first[a * SIDE + b, a * SIDE + b] = 1
            take_first[SLAB + b * SHIFT + a, b * SIDE + a] = 1
            take_last[a * SIDE + b, padded_row(edge + a, b)] = 1
            take_last[SLAB + b * SHIFT + a, padded_row(b, edge + a)] = 1
        for b in range(SHIFT):
            take_first[2 * SLAB + a * SHIFT + b, a * SIDE + b] = 1
            take_last[2 * SLAB + a * SHIFT + b, padded_row(edge + a, edge + b)] = 1
    return (plain, plain.T.copy(), ahead, back, take_first, take_last)


def column_orders():
    heads = np.zeros((384, 384), np.float32)
    units = np.zeros((512, 512), np.float32)
    for n in range(4):
        for part in range(3):
            for d in range(HEAD_DIM):
                heads[n * 96 + part * 32 + d, part * 128 + n * 32 + d] = 1
    for r in range(8):
        for b in range(4):
            for i in range(16):
                units[r * 64 + b * 16 + i, b * 128 + r * 16 + i] = 1
    return heads, units


def dot(a, b):
    return lax.dot_general(a, b, (((1,), (0,)), ((), ())), preferred_element_type=F32)


def dot_nt(a, b):
    return lax.dot_general(a, b, (((1,), (1,)), ((), ())), preferred_element_type=F32)


def dot_tn(a, b):
    return lax.dot_general(a, b, (((0,), (0,)), ((), ())), preferred_element_type=F32)


def normalized(x):
    centred = x - jnp.mean(x, -1, keepdims=True)
    inverse = lax.rsqrt(jnp.mean(centred * centred, -1, keepdims=True) + epsilon)
    return centred * inverse, inverse


def norm_back(grad, x, gain):
    hat, inverse = normalized(x)
    grad_hat = grad * gain
    grad_x = inverse * (
        grad_hat
        - jnp.mean(grad_hat, -1, keepdims=True)
        - hat * jnp.mean(grad_hat * hat, -1, keepdims=True)
    )
    return grad_x, jnp.sum(grad * hat, 0, keepdims=True), jnp.sum(grad, 0, keepdims=True)


def gelu_both(u):
    a = jnp.abs(u)
    t = 1.0 / (1.0 + (0.3275911 * 0.5**0.5) * a)
    e = jnp.exp2((-0.5 * log2e) * u * u)
    poly = t * (
        0.5 * 0.254829592
        + t * (0.5 * -0.284496736 + t * (0.5 * 1.421413741 + t * (0.5 * -1.453152027 + t * (0.5 * 1.061405429))))
    )
    tail = poly * e
    phi = jnp.where(u >= 0, 1.0 - tail, tail)
    return u * phi, phi + u * e * (1.0 / math.sqrt(2 * math.pi))


def head_rows(pair):
    lane = lax.broadcasted_iota(jnp.int32, pair.shape, 1) % 128 // HEAD_DIM
    zero = jnp.zeros_like(pair)
    return jnp.concatenate([jnp.where(lane == h, pair, zero) for h in range(4)], 0)


def head_fold(rows):
    lane = lax.broadcasted_iota(jnp.int32, (SLOT, 256), 1) % 128 // HEAD_DIM
    out = rows[:SLOT]
    for h in range(1, 4):
        out = jnp.where(lane == h, rows[h * SLOT : (h + 1) * SLOT], out)
    return out


def side_by_side(ref, start, lane):
    return jnp.concatenate(
        [ref[pl.ds(start, SLOT), lane : lane + 128], ref[pl.ds(start + SLOT, SLOT), lane : lane + 128]], 1
    )


def block_diagonal(pair):
    lane = lax.broadcasted_iota(jnp.int32, pair.shape, 1)
    zero = jnp.zeros_like(pair)
    return jnp.concatenate([jnp.where(lane < 128, pair, zero), jnp.where(lane >= 128, pair, zero)], 0)


def store_diagonal(ref, start, lane, rows):
    ref[pl.ds(start, SLOT), lane : lane + 128] = rows[:SLOT, :128].astype(ref.dtype)
    ref[pl.ds(start + SLOT, SLOT), lane : lane + 128] = rows[SLOT:, 128:].astype(ref.dtype)


class Moves:
    def __init__(self, sems):
        self.loads, self.stores, self.started, self.sems = {}, {}, [], sems

    def load(self, pairs, buffer):
        at = len(self.started)
        for source, target in pairs:
            copy = pltpu.make_async_copy(source, target, self.sems.at[len(self.started)])
            copy.start()
            self.started.append(copy)
        self.loads[id(buffer)] = range(at, len(self.started))

    def need(self, *refs, part=None):
        for ref in refs:
            places = self.loads.get(id(ref), ())
            for at in places if part is None else places[part : part + 1]:
                if self.started[at] is not None:
                    self.started[at].wait()
                    self.started[at] = None

    def ship(self, ref, at=()):
        if id(ref) in self.stores:
            copy = pltpu.make_async_copy(
                ref.at[at] if at else ref,
                self.stores[id(ref)].at[at] if at else self.stores[id(ref)],
                self.sems.at[len(self.started)],
            )
            copy.start()
            self.started.append(copy)

    def finish(self):
        for copy in self.started:
            if copy is not None:
                copy.wait()


def columns(b):
    return (slice(None), slice(b * D, (b + 1) * D))


def of_blocks(b):
    return (slice(None), slice(None), b)


def call(body, outs, args, scratch=(), pieces=(), place=None, us=1, after=(), late=None, early=()):
    shapes = [jax.ShapeDtypeStruct(s, d) for s, d in outs]
    late = late or {}
    lead = [] if place is None else [place]
    anywhere, inside = pl.BlockSpec(memory_space=pl.ANY), pl.BlockSpec(memory_space=pltpu.VMEM)
    specs = [anywhere] * len(after) + [pl.BlockSpec(memory_space=pltpu.SMEM)] * len(lead) + [anywhere] * len(pieces)
    specs += [anywhere if i in late else inside for i in range(len(args))]
    buffers = []
    for i, parts in late.items():
        rows = parts[1:] if isinstance(parts, tuple) else args[i].shape[:1]
        buffers.append(pltpu.VMEM((*rows, *args[i].shape[1:]), args[i].dtype))
    buffers += [pltpu.VMEM(*outs[i]) for i in early]
    moving = bool(buffers)
    if moving:
        buffers.append(pltpu.SemaphoreType.DMA((96,)))

    def whole(*refs):
        refs = refs[len(after) :]
        first, n_in = len(lead) + len(pieces), len(lead) + len(pieces) + len(args)
        ins, results = list(refs[:n_in]), list(refs[n_in : n_in + len(outs)])
        rest = refs[n_in + len(outs) :]
        if not moving:
            body(*refs)
            return
        own, buffer = rest[: len(scratch)], rest[len(scratch) :]
        moves = Moves(buffer[-1])
        for (i, parts), target in zip(late.items(), buffer):
            source = ins[first + i]
            if parts is None:
                pairs = [(source, target)]
            elif isinstance(parts, tuple):
                pairs = [(source.at[pl.ds(*parts)], target)]
            else:
                pairs = [(source.at[part], target.at[part]) for part in parts]
            moves.load(pairs, target)
            ins[first + i] = target
        for i, source in zip(early, buffer[len(late) :]):
            moves.stores[id(source)] = results[i]
            results[i] = source
        body(moves, *ins, *results, *own)
        moves.finish()

    return pl.pallas_call(
        whole,
        out_shape=shapes,
        in_specs=specs,
        out_specs=[anywhere if i in early else inside for i in range(len(outs))],
        scratch_shapes=list(scratch) + buffers,
        compiler_params=pltpu.CompilerParams(vmem_limit_bytes=VMEM_BYTES),
        cost_estimate=pl.CostEstimate(flops=us * 3 * 10**9, bytes_accessed=us * 10**6, transcendentals=0),
    )(*after, *lead, *pieces, *args)


def held(arrays, after):
    anywhere = pl.BlockSpec(memory_space=pl.ANY)
    return pl.pallas_call(
        lambda *refs: None,
        out_shape=[jax.ShapeDtypeStruct(a.shape, a.dtype) for a in arrays],
        in_specs=[anywhere] * (len(arrays) + len(after)),
        out_specs=[anywhere] * len(arrays),
        input_output_aliases={i: i for i in range(len(arrays))},
    )(*arrays, *after)


def owner_of(z, x, core):
    return z * 8 + (x % 2) * 4 + core * 2 + x // 2


def assembly(coords_ref, sets, w_ref, sems):
    z, x, core = coords_ref[0], coords_ref[1], coords_ref[2]
    copies = []
    for pieces, far, (low, count), first in sets:
        for k, piece in enumerate(pieces):
            from_core = core if k < len(pieces) // 2 else 1 - core
            for i in range(piece.shape[0]):
                if far == "zx":
                    owner = owner_of(i // 4, i % 4, from_core)
                elif far == "z":
                    owner = owner_of(i // 4, lax.rem(x + i % 4, 4), from_core)
                elif far == "by z":
                    owner = owner_of(lax.rem(z + k % 4, 4), i, from_core)
                else:
                    owner = owner_of(lax.rem(z + i, 4), lax.rem(x + k % 4, 4), from_core)
                source, target = piece.at[i, pl.ds(low, count)], w_ref.at[pl.ds(first, count), owner]
                copies.append(pltpu.make_async_copy(source, target, sems.at[len(copies)]))
    for c in copies:
        c.start()
    return copies


def block(ref, b):
    return ref[b].reshape(D, D)


def block_lanes(ref, b, lanes):
    return ref[b, :, :, lanes].reshape(D, lanes.stop - lanes.start)


def block_rows(ref, b, half):
    return ref[b, half * 16 : half * 16 + 16].reshape(256, D)


def store_grad(place_ref, keep_ref, send_ref, b, half, rows):
    first = place_ref[2] == 0
    rows = rows.astype(BF)
    for zz in range(2):
        for x in range(4):
            base = (zz * 8 + (x % 2) * 4 + x // 2) * 16
            one, two = rows[base : base + 16], rows[base + 32 : base + 48]
            keep_ref[half * 2 + zz, x, b] = jnp.where(first, one, two)
            send_ref[half * 2 + zz, x, b] = jnp.where(first, two, one)


def pack_blocks(layer, qkv_ref, proj_ref, expand_ref, contract_ref, heads_ref, units_ref, store):
    every = slice(None)
    store(3, every, proj_ref[layer].astype(BF))
    for b in range(4):
        store(8 + b, every, contract_ref[layer, 16 * b : 16 * b + 16, :].astype(BF))
    for g in range(GROUPS):
        lanes = slice(128 * g, 128 * g + 128)
        part = dot(qkv_ref[layer, :, 384 * g : 384 * g + 384].astype(BF), heads_ref[...]).astype(BF)
        for s in range(3):
            store(s, lanes, part[:, 128 * s : 128 * s + 128])
        part = dot(expand_ref[layer, :, 512 * g : 512 * g + 512].astype(BF), units_ref[...]).astype(BF)
        for b in range(4):
            store(4 + b, lanes, part[:, 128 * b : 128 * b + 128])


def pack_kernel(*refs):
    one_ref, two_ref = refs[6:]

    def store(b, lanes, value):
        if b < 6:
            for i in range(4):
                one_ref[i, b, :, lanes] = value
        else:
            two_ref[b - 6, :, lanes] = value

    pack_blocks(0, *refs[:6], store)


def pack_next_kernel(*refs):
    spread_ref, rest_ref = refs[6:]

    def store(b, lanes, value):
        if b < 3:
            for i in range(16):
                spread_ref[i, b, :, lanes] = value
        else:
            rest_ref[b - 3, :, lanes] = value

    pack_blocks(1, *refs[:6], store)


def stack_kernel(*refs):
    refs[5][...] = refs[0][...]
    for k in range(4):
        refs[6][k] = refs[1 + k][...]


def stack_spread_kernel(*refs):
    for k in range(4):
        for x in range(4):
            refs[4][x, k] = refs[k][...]


def enter_kernel(x_ref, gain_ref, bias_ref, place_ref, hp_ref):
    hat, _ = normalized(x_ref[...].astype(F32))
    h = (hat * gain_ref[...] + bias_ref[...]).astype(BF)
    hp_ref[...] = dot(place_ref[...], h).astype(BF)


def attend_pairs(qkv_ref, first, table_ref, mask_ref, attn_ref, into_ref):
    def one_pair(p, carry):
        start = pl.multiple_of(first + p * 128, 128)
        for g in range(GROUPS):
            lane = g * 128
            keys = head_rows(side_by_side(qkv_ref, start, D + lane))
            queries = block_diagonal(side_by_side(qkv_ref, start, lane))
            scores = dot_nt(keys, queries) * (HEAD_DIM**-0.5 * log2e) + table_ref[g * 256 : (g + 1) * 256, :]
            scores = scores.reshape(4, SLOT, 128)
            if mask_ref is not None:
                scores = jnp.where(mask_ref[p][None] > 0, scores, masked_score)
            scores = jnp.exp2(scores - jnp.max(scores, 1, keepdims=True))
            scores = scores * (1.0 / jnp.sum(scores, 1, keepdims=True))
            attn = scores.reshape(256, 128).astype(BF)
            attn_ref[p, g] = attn
            values = head_rows(side_by_side(qkv_ref, start, 2 * D + lane))
            store_diagonal(into_ref, pl.multiple_of(p * 128, 128), lane, dot_tn(attn, values))
        return carry

    lax.fori_loop(0, PAIRS // 2, one_pair, 0, unroll=4)


def attend_kernel(shifted, moves, *refs):
    count = 2 if shifted else 8
    coords_ref, pieces, refs = refs[0], refs[1 : count + 1], refs[count + 1 :]
    if shifted:
        h_ref, rows_ref, cols_ref, corner_ref, place_ref, bias_ref, table_ref, mask_ref, take_ref = refs[:9]
        w_ref, hp_ref, qkv_ref, one_ref, two_ref, ctxp_ref, rows_out, cols_out, corner_out, sems = refs[9:]
        copies = assembly(coords_ref, [(pieces, "zx", (0, 3), 0)], w_ref, sems)
        moves.need(place_ref, h_ref)
        place = place_ref[...]
        hp = dot(place[:, :CELLS], h_ref[...])
        slabs = jnp.concatenate([rows_ref[...], cols_ref[...], corner_ref[...]], 0)
        hp_ref[...] = (hp + dot(place[:, CELLS:], slabs)).astype(BF)
        moves.ship(hp_ref)
    else:
        hp_ref, bias_ref, table_ref, place_ref = refs[:4]
        w_ref, qkv_ref, one_ref, two_ref, ctx_ref, ctxp_ref, sems = refs[4:]
        mask_ref = None
        copies = assembly(coords_ref, [(pieces, "by z", (0, 3), 0)], w_ref, sems)
        moves.need(hp_ref)
    for c in copies:
        c.wait()
    moves.ship(w_ref)
    for s in range(3):
        for half in range(2):
            lanes = slice(half * 256, half * 256 + 256)
            wide = slice(s * D + half * 256, s * D + half * 256 + 256)
            qkv_ref[:, wide] = (dot(hp_ref[...], block_lanes(w_ref, s, lanes)) + bias_ref[:, wide]).astype(BF)
        moves.ship(qkv_ref, columns(s))
    upper = PADDED // 2
    masks = (None, None) if mask_ref is None else (mask_ref.at[:4], mask_ref.at[4:])
    moves.need(table_ref)
    if shifted:
        moves.need(mask_ref)
    attend_pairs(qkv_ref, 0, table_ref, masks[0], one_ref, ctxp_ref.at[:upper])
    moves.ship(one_ref)
    attend_pairs(qkv_ref, upper, table_ref, masks[1], two_ref, ctxp_ref.at[upper:])
    moves.ship(two_ref)
    if shifted:
        moves.ship(ctxp_ref)
        moves.need(take_ref)
        sent = dot(take_ref[...], ctxp_ref[...]).astype(BF)
        rows_out[...] = sent[:SLAB]
        cols_out[...] = sent[SLAB : 2 * SLAB]
        corner_out[...] = sent[2 * SLAB :]
    else:
        moves.need(place_ref)
        ctx_ref[...] = dot(place_ref[...], ctxp_ref[...]).astype(BF)


def feed_forward(moves, x_ref, ctx_ref, w_ref, vectors, mid_ref, h2_ref, hidden_ref, slope_ref):
    bp_ref, g2_ref, b2_ref, bo_ref, bh_ref = vectors
    mid_ref[...] = x_ref[...].astype(F32) + dot(ctx_ref[...], block(w_ref, 0)) + bp_ref[...]
    moves.ship(mid_ref)
    hat, _ = normalized(mid_ref[...])
    h2_ref[...] = (hat * g2_ref[...] + b2_ref[...]).astype(BF)
    moves.ship(h2_ref)
    for b in range(4):
        for half in range(2):
            lanes = slice(half * 256, half * 256 + 256)
            wide = slice(b * D + half * 256, b * D + half * 256 + 256)
            pre = dot(h2_ref[...], block_lanes(w_ref, 1 + b, lanes)) + bh_ref[:, wide]
            hidden, slope = gelu_both(pre)
            hidden_ref[:, wide] = hidden.astype(BF)
            slope_ref[:, wide] = slope.astype(BF)
        moves.ship(hidden_ref, columns(b))
        moves.ship(slope_ref, columns(b))
    out = mid_ref[...] + bo_ref[...]
    for b in range(4):
        out = out + dot(hidden_ref[:, b * D : (b + 1) * D], block(w_ref, 5 + b))
    return out


def forward_kernel(moves, *refs):
    coords_ref, ones, twos, refs = refs[0], refs[1:9], refs[9:17], refs[17:]
    x_ref, ctx_ref, *vectors = refs[:7]
    g1_ref, b1_ref, take_ref, w_ref, *kept = refs[7:15]
    out_ref, h_ref, rows_out, cols_out, corner_out, sems = refs[15:]
    copies = assembly(coords_ref, [(ones, "by z", (3, 3), 0), (twos, "by x", (0, 6), 3)], w_ref, sems)
    moves.need(ctx_ref)
    for c in copies:
        c.wait()
    moves.ship(w_ref)
    moves.need(x_ref)
    out = feed_forward(moves, x_ref, ctx_ref, w_ref, vectors, *kept)
    out_ref[...] = out
    moves.ship(out_ref)
    hat, _ = normalized(out)
    h_ref[...] = (hat * g1_ref[...] + b1_ref[...]).astype(BF)
    moves.ship(h_ref)
    moves.need(take_ref)
    sent = dot(take_ref[...], h_ref[...]).astype(BF)
    rows_out[...] = sent[:SLAB]
    cols_out[...] = sent[SLAB : 2 * SLAB]
    corner_out[...] = sent[2 * SLAB :]


def hidden_back_pass(moves, gm_ref, slope_ref, w_ref, dpre_ref, dbh_ref):
    moves.need(w_ref, part=0)
    for b in range(4):
        moves.need(slope_ref, part=b)
        for half in range(2):
            wide = slice(b * D + half * 256, b * D + half * 256 + 256)
            dpre = dot_nt(gm_ref[...], block_rows(w_ref, 5 + b, half)) * slope_ref[:, wide].astype(F32)
            dpre = dpre.astype(BF)
            dpre_ref[:, wide] = dpre
            dbh_ref[:, wide] = jnp.sum(dpre.astype(F32), 0, keepdims=True)
        moves.ship(dpre_ref, columns(b))


def middle_back_pass(moves, grad_ref, dpre_ref, w_ref, mid_ref, g2_ref, dmid_ref, go_ref, small_ref):
    moves.need(w_ref)
    moves.need(dpre_ref, part=0)
    dh2 = dot_nt(dpre_ref[:, :D], block(w_ref, 1))
    for b in range(1, 4):
        moves.need(dpre_ref, part=b)
        dh2 = dh2 + dot_nt(dpre_ref[:, b * D : (b + 1) * D], block(w_ref, 1 + b))
    moves.need(mid_ref, grad_ref)
    dx, dg2, db2 = norm_back(dh2, mid_ref[...], g2_ref[...])
    small_ref[1:2, :] = dg2
    small_ref[2:3, :] = db2
    dmid_ref[...] = grad_ref[...].astype(F32) + dx
    moves.ship(dmid_ref)
    go_ref[...] = dmid_ref[...].astype(BF)
    moves.ship(go_ref)
    small_ref[0:1, :] = jnp.sum(go_ref[...].astype(F32), 0, keepdims=True)


def turn_kernel(moves, *refs):
    coords_ref, pieces, refs = refs[0], refs[1:3], refs[3:]
    x_ref, ctxp_ref, rows_ref, cols_ref, corner_ref, place_ref, *vectors = refs[:11]
    g_ref, take_ref, out_ref, dmid_ref, small_ref, dbh_ref, dctx_ref, rows_out, cols_out, corner_out = refs[11:21]
    keep_ref, send_ref, w_ref, ctx_ref, mid_ref, h2_ref, hidden_ref, slope_ref, dpre_ref, go_ref, sems = refs[21:]
    copies = assembly(coords_ref, [(pieces, "z", (0, 9), 0)], w_ref, sems)
    moves.need(place_ref, ctxp_ref)
    place = place_ref[...]
    slabs = jnp.concatenate([rows_ref[...], cols_ref[...], corner_ref[...]], 0)
    ctx_ref[...] = (dot(place[:, :PADDED], ctxp_ref[...]) + dot(place[:, PADDED:], slabs)).astype(BF)
    for c in copies:
        c.wait()
    moves.need(x_ref)
    out = feed_forward(moves, x_ref, ctx_ref, w_ref, vectors, mid_ref, h2_ref, hidden_ref, slope_ref)
    out_ref[...] = out.astype(BF)
    moves.ship(out_ref)
    moves.need(g_ref)
    small_ref[3:4, :] = jnp.sum(g_ref[...].astype(F32), 0, keepdims=True)
    hidden_back_pass(moves, g_ref, slope_ref, w_ref, dpre_ref, dbh_ref)
    middle_back_pass(moves, g_ref, dpre_ref, w_ref, mid_ref, vectors[1], dmid_ref, go_ref, small_ref)
    dctx_ref[...] = dot_nt(go_ref[...], block(w_ref, 0)).astype(BF)
    moves.ship(dctx_ref)
    moves.need(take_ref)
    sent = dot(take_ref[...], dctx_ref[...]).astype(BF)
    rows_out[...] = sent[:SLAB]
    cols_out[...] = sent[SLAB : 2 * SLAB]
    corner_out[...] = sent[2 * SLAB :]
    hidden_grads(moves, coords_ref, 1, g_ref, hidden_ref, h2_ref, dpre_ref, keep_ref, send_ref)
    for half in range(2):
        rows = slice(half * 256, half * 256 + 256)
        store_grad(coords_ref, keep_ref, send_ref, 0, half, dot_tn(ctx_ref[:, rows], go_ref[...]))
    moves.ship(keep_ref, of_blocks(0))
    moves.ship(send_ref, of_blocks(0))


def hidden_grads(moves, coords_ref, first, gm_ref, hidden_ref, h2_ref, dpre_ref, keep_ref, send_ref):
    for b in range(4):
        moves.need(hidden_ref, part=b)
        for half in range(2):
            wide = slice(b * D + half * 256, b * D + half * 256 + 256)
            grad_c = dot_tn(hidden_ref[:, wide], gm_ref[...])
            store_grad(coords_ref, keep_ref, send_ref, first + 4 + b, half, grad_c)
        moves.ship(keep_ref, of_blocks(first + 4 + b))
        moves.ship(send_ref, of_blocks(first + 4 + b))
    moves.need(h2_ref, dpre_ref)
    for b in range(4):
        for half in range(2):
            rows = slice(half * 256, half * 256 + 256)
            grad_e = dot_tn(h2_ref[:, rows], dpre_ref[:, b * D : (b + 1) * D])
            store_grad(coords_ref, keep_ref, send_ref, first + b, half, grad_e)
        moves.ship(keep_ref, of_blocks(first + b))
        moves.ship(send_ref, of_blocks(first + b))


def back_first_kernel(moves, *refs):
    coords_ref, dmid1_ref, dhp_ref, rows_ref, cols_ref, corner_ref, back_ref, x1_ref, g1_ref = refs[:9]
    hidden_ref, slope_ref, h2_ref, w_ref = refs[9:13]
    grad_ref, dpre_ref, keep_ref, send_ref, dbo_ref, dbh_ref, above_ref, gm_ref = refs[13:]
    moves.need(back_ref, dhp_ref)
    back = back_ref[...]
    slabs = jnp.concatenate([rows_ref[...], cols_ref[...], corner_ref[...]], 0)
    dh = dot(back[:, :PADDED], dhp_ref[...]) + dot(back[:, PADDED:], slabs)
    moves.need(x1_ref)
    dx, dg1, db1 = norm_back(dh, x1_ref[...], g1_ref[...])
    above_ref[0:1, :] = dg1
    above_ref[1:2, :] = db1
    moves.need(dmid1_ref)
    grad = dmid1_ref[...] + dx
    grad_ref[...] = grad
    moves.ship(grad_ref)
    gm_ref[...] = grad.astype(BF)
    dbo_ref[...] = jnp.sum(gm_ref[...].astype(F32), 0, keepdims=True)
    hidden_back_pass(moves, gm_ref, slope_ref, w_ref, dpre_ref, dbh_ref)
    hidden_grads(moves, coords_ref, 0, gm_ref, hidden_ref, h2_ref, dpre_ref, keep_ref, send_ref)


def middle_first_kernel(moves, grad_ref, dpre_ref, mid_ref, ctx_ref, w_ref, g2_ref, place_ref, *outs):
    dmid_ref, dwp_ref, small_ref, dctxp_ref, go_ref = outs
    middle_back_pass(moves, grad_ref, dpre_ref, w_ref, mid_ref, g2_ref, dmid_ref, go_ref, small_ref)
    moves.need(ctx_ref)
    for half in range(2):
        rows = slice(half * 256, half * 256 + 256)
        dwp_ref[rows, :] = dot_tn(ctx_ref[:, rows], go_ref[...]).astype(BF)
    moves.ship(dwp_ref)
    dctx = dot_nt(go_ref[...], block(w_ref, 0)).astype(BF)
    moves.need(place_ref)
    dctxp_ref[...] = dot(place_ref[...], dctx).astype(BF)


def attend_back_pairs(first, qkv_ref, attn_ref, dctxp_ref, dqkv_ref, dtable_ref):
    if first == 0:
        dtable_ref[...] = jnp.zeros_like(dtable_ref)
    scale = HEAD_DIM**-0.5

    def one_pair(p, carry):
        start = pl.multiple_of(first + p * 128, 128)
        for g in range(GROUPS):
            lane = g * 128
            attn = attn_ref[p, g]
            keys = head_rows(side_by_side(qkv_ref, start, D + lane))
            values = head_rows(side_by_side(qkv_ref, start, 2 * D + lane))
            queries = block_diagonal(side_by_side(qkv_ref, start, lane))
            grads = block_diagonal(side_by_side(dctxp_ref, start, lane))
            probs = attn.astype(F32).reshape(4, SLOT, 128)
            dprobs = dot_nt(values, grads).reshape(4, SLOT, 128)
            dscores = probs * (dprobs - jnp.sum(probs * dprobs, 1, keepdims=True))
            dscores = dscores.reshape(256, 128).astype(BF)
            dtable_ref[g * 256 : (g + 1) * 256, :] += dscores.astype(F32)
            store_diagonal(dqkv_ref, start, lane, dot_tn(dscores, keys) * scale)
            dkeys = (head_fold(dot(dscores, queries)) * scale).astype(BF)
            dqkv_ref[pl.ds(start, SLOT), D + lane : D + lane + 128] = dkeys[:, :128]
            dqkv_ref[pl.ds(start + SLOT, SLOT), D + lane : D + lane + 128] = dkeys[:, 128:]
            dvalues = head_fold(dot(attn, grads)).astype(BF)
            dqkv_ref[pl.ds(start, SLOT), 2 * D + lane : 2 * D + lane + 128] = dvalues[:, :128]
            dqkv_ref[pl.ds(start + SLOT, SLOT), 2 * D + lane : 2 * D + lane + 128] = dvalues[:, 128:]
        return carry

    lax.fori_loop(0, PAIRS // 2, one_pair, 0, unroll=4)


def table_sum(dtable_ref, by_key_ref, out_ref):
    total = jnp.zeros((2 * HEADS, 256), F32)
    row = lax.broadcasted_iota(jnp.int32, (256, 256), 0)
    for c in range(25):
        hot = jnp.where(row == by_key_ref[c : c + 1, :], 1.0, 0.0).astype(BF)
        keys = [dtable_ref[pl.ds(2 * c + k, HEADS, stride=SLOT), :] for k in range(2)]
        rows = jnp.concatenate(keys, 1)
        high = rows.astype(BF)
        low = (rows - high.astype(F32)).astype(BF)
        total = total + dot_nt(jnp.concatenate([high, low], 0), hot)
    out_ref[...] = total[:HEADS] + total[HEADS:]


def attend_back_kernel(moves, *refs):
    dctx_ref, rows_ref, cols_ref, corner_ref, place_ref, qkv_ref, one_ref, two_ref, w_ref, take_ref, key_ref = refs[:11]
    dqkv_ref, dbias_ref, table_ref, dhp_ref, rows_out, cols_out, corner_out, dctxp_ref, dtable_ref = refs[11:]
    moves.need(place_ref, dctx_ref)
    place = place_ref[...]
    slabs = jnp.concatenate([rows_ref[...], cols_ref[...], corner_ref[...]], 0)
    dctxp_ref[...] = (dot(place[:, :CELLS], dctx_ref[...]) + dot(place[:, CELLS:], slabs)).astype(BF)
    moves.need(qkv_ref, one_ref)
    attend_back_pairs(0, qkv_ref, one_ref, dctxp_ref, dqkv_ref, dtable_ref)
    moves.need(two_ref)
    attend_back_pairs(PADDED // 2, qkv_ref, two_ref, dctxp_ref, dqkv_ref, dtable_ref)
    moves.ship(dqkv_ref)
    moves.need(w_ref)
    table_sum(dtable_ref, key_ref, table_ref)
    for s in range(3):
        dbias_ref[s : s + 1, :] = jnp.sum(dqkv_ref[:, s * D : (s + 1) * D].astype(F32), 0, keepdims=True)
    dhp = dot_nt(dqkv_ref[:, :D], block(w_ref, 0))
    for s in range(1, 3):
        dhp = dhp + dot_nt(dqkv_ref[:, s * D : (s + 1) * D], block(w_ref, s))
    dhp_ref[...] = dhp.astype(BF)
    moves.ship(dhp_ref)
    moves.need(take_ref)
    sent = dot(take_ref[...], dhp_ref[...]).astype(BF)
    rows_out[...] = sent[:SLAB]
    cols_out[...] = sent[SLAB : 2 * SLAB]
    corner_out[...] = sent[2 * SLAB :]


def grads_heads_kernel(moves, coords_ref, hp_ref, dqkv_ref, keep_ref, send_ref):
    moves.need(hp_ref)
    for s in range(3):
        moves.need(dqkv_ref, part=s)
        for half in range(2):
            rows = slice(half * 256, half * 256 + 256)
            grad_w = dot_tn(hp_ref[:, rows], dqkv_ref[:, s * D : (s + 1) * D])
            store_grad(coords_ref, keep_ref, send_ref, s, half, grad_w)
        moves.ship(keep_ref, of_blocks(s))
        moves.ship(send_ref, of_blocks(s))


def attend_back_end_kernel(moves, *refs):
    coords_ref, dctxp_ref, qkv_ref, one_ref, two_ref, hp_ref, dwp_ref, key_ref, w_ref, place_ref = refs[:10]
    x_ref, dmid_ref, g1_ref, norm1, dqb1, sums1, dbh1, table1, sums0, dbo0, dbh0 = refs[10:21]
    keep_ref, send_ref, out_ref, sums_ref, dqkv_ref, dtable_ref, dhp_ref = refs[21:]
    moves.need(dctxp_ref, qkv_ref, one_ref)
    attend_back_pairs(0, qkv_ref, one_ref, dctxp_ref, dqkv_ref, dtable_ref)
    moves.need(two_ref)
    attend_back_pairs(PADDED // 2, qkv_ref, two_ref, dctxp_ref, dqkv_ref, dtable_ref)
    moves.need(hp_ref)
    dqb = []
    for s in range(3):
        wide = slice(s * D, (s + 1) * D)
        dqb.append(jnp.sum(dqkv_ref[:, wide].astype(F32), 0, keepdims=True))
        for half in range(2):
            rows = slice(half * 256, half * 256 + 256)
            grad_w = dot_tn(hp_ref[:, rows], dqkv_ref[:, wide])
            store_grad(coords_ref, keep_ref, send_ref, s, half, grad_w)
    moves.need(dwp_ref)
    for half in range(2):
        store_grad(coords_ref, keep_ref, send_ref, 3, half, dwp_ref[half * 256 : half * 256 + 256, :])
    moves.ship(keep_ref)
    moves.ship(send_ref)
    moves.need(w_ref)
    dhp = dot_nt(dqkv_ref[:, :D], block(w_ref, 0))
    for s in range(1, 3):
        dhp = dhp + dot_nt(dqkv_ref[:, s * D : (s + 1) * D], block(w_ref, s))
    dhp_ref[...] = dhp.astype(BF)
    moves.need(place_ref, x_ref, dmid_ref)
    dh = dot(place_ref[...], dhp_ref[...])
    dx, dg1, db1 = norm_back(dh, x_ref[...].astype(F32), g1_ref[...])
    out_ref[...] = dmid_ref[...] + dx
    moves.ship(out_ref)
    for at, norm, query, value, sums, dbo, dbh in (
        (0, (dg1, db1), dqb[0], dqb[2], sums0, dbo0[...], dbh0),
        (12, (norm1[0:1, :], norm1[1:2, :]), dqb1[0:1, :], dqb1[2:3, :], sums1, sums1[3:4, :], dbh1),
    ):
        rows = [*norm, query, value, sums[0:1, :], sums[1:2, :], sums[2:3, :], dbo]
        rows += [dbh[:, D * b : D * b + D] for b in range(4)]
        for i, row in enumerate(rows):
            sums_ref[at + i : at + i + 1, :] = row
    table_sum(dtable_ref, key_ref, sums_ref.at[24:40, 0:256])
    sums_ref[24:40, 256:512] = table1[...]


def add_kernel(*refs):
    out_ref, at = refs[-1], 0
    for i in range(0, len(refs) - 1, 2):
        n = refs[i].shape[2]
        total = refs[i][...].astype(F32) + refs[i + 1][...].astype(F32)
        out_ref[:, :, at : at + n] = total.astype(BF)
        at += n


def sum_split_kernel(coords_ref, parts_ref, *outs):
    for d, out in enumerate(outs):
        target = lax.rem(coords_ref[1] + d, 4)
        total = parts_ref[0, target].astype(F32)
        for k in range(1, 4):
            total = total + parts_ref[k, target].astype(F32)
        out[...] = total.astype(BF)


def to_xz_kernel(coords_ref, keep_ref, other_ref, parts_ref, sums_ref, more_ref, near_ref, *outs):
    smalls = jnp.concatenate([sums_ref[...] + more_ref[...], jnp.zeros((8, D), F32)], 0)
    high = smalls.astype(BF).astype(F32)
    low = smalls - high
    for z in range(4):
        for x in range(4):
            total = keep_ref[z, x].astype(F32) + other_ref[z, x].astype(F32)
            near_ref[4 * z + x, 0:4] = total.astype(BF)
            at = 3 * (4 * z + x)
            rows = [high[at : at + 3], low[at : at + 3], jnp.zeros((10, D), F32)]
            near_ref[4 * z + x, 4] = jnp.concatenate(rows, 0).astype(BF)
    for d, out in enumerate(outs):
        target = lax.rem(coords_ref[1] + d, 4)
        total = parts_ref[0, target].astype(F32)
        for k in range(1, 4):
            total = total + parts_ref[k, target].astype(F32)
        out[...] = total.astype(BF)


def to_seq_kernel(near_ref, *refs):
    pieces, late_ref = refs[:4], refs[4]
    total = near_ref[0].astype(F32)
    for i in range(1, 16):
        total = total + near_ref[i].astype(F32)
    late_ref[0:4] = total[0:4].astype(BF)
    rows = total[4, 0:3] + total[4, 3:6]
    high = rows.astype(BF).astype(F32)
    late_ref[15] = jnp.concatenate([high, rows - high, jnp.zeros((10, D), F32)], 0).astype(BF)
    total = pieces[0][...].astype(F32)
    for piece in pieces[1:]:
        total = total + piece[...].astype(F32)
    late_ref[4:15] = total.astype(BF)


def to_plane_kernel(*refs):
    pieces, out_ref = [ref[15].astype(F32) for ref in refs[:4]], refs[4]
    first, second, third, fourth = (piece[0:3] + piece[3:6] for piece in pieces)
    total = (first + second) + (third + fourth)
    rows = [total[r : r + 1, 128 * q : 128 * q + 128] for r in range(3) for q in range(4)]
    rows = jnp.concatenate(rows + [jnp.zeros((4, 128), F32)], 0)
    for i in range(16):
        out_ref[i] = rows


def four(refs, b):
    return (refs[0][b].astype(F32) + refs[1][b].astype(F32)) + (refs[2][b].astype(F32) + refs[3][b].astype(F32))


def reorder(values, order):
    n = values.shape[0]
    high = values.astype(BF)
    rest = values - high.astype(F32)
    low = rest.astype(BF)
    last = (rest - low.astype(F32)).astype(BF)
    rows = dot_nt(jnp.concatenate([high, low, last], 0), order)
    return rows[:n] + rows[n : 2 * n] + rows[2 * n :]


def step_into(at, grad, old, new, rate, decay):
    weight, first, second = (ref[at] for ref in old)
    for ref, value in zip(new, adamw(weight, first, second, grad, rate, decay)):
        ref[at] = value


def update_small_kernel(*refs):
    smalls_ref, units_ref, small, table = refs[0], refs[1], refs[2:5], refs[5:8]
    new_small, new_table, bias_ref, sums_ref = refs[8:11], refs[11:14], refs[14], refs[15]
    for i in range(16):
        part = smalls_ref[i]
        for k in range(12):
            sums_ref[3 * i + k // 4 : 3 * i + k // 4 + 1, k % 4 * 128 : k % 4 * 128 + 128] = part[k : k + 1]
    for layer in range(LAYERS):
        rows = [sums_ref[12 * layer + i : 12 * layer + i + 1, :] for i in range(12)]
        bias_ref[layer : layer + 1, :] = rows[7]
        parts = [
            jnp.concatenate([rows[8 + b][:, 128 * g : 128 * g + 128] for b in range(4)], 1) for g in range(GROUPS)
        ]
        units = reorder(jnp.concatenate(parts + [jnp.zeros((12, D), F32)], 0), units_ref[...])
        for i, grad in enumerate(rows[:8] + [units[g : g + 1] for g in range(GROUPS)]):
            at = (slice(layer, layer + 1), slice(D * i, D * i + D))
            step_into(at, grad, small, new_small, 0.3, 0.0)
        step_into((layer,), sums_ref[24:40, 256 * layer : 256 * layer + REL], table, new_table, 0.6, 0.0)


def update_kernel(*refs):
    early, late, heads_ref, units_ref, refs = refs[:4], refs[4:8], refs[8], refs[9], refs[10:]
    old = [refs[3 * i : 3 * i + 3] for i in range(4)]
    new = [refs[12 + 3 * i : 15 + 3 * i] for i in range(4)]

    def layer_step(heads, head_at, rest, rest_at):
        step_into((0,), four(rest, rest_at), old[1], new[1], 0.1, 0.05)
        for b in range(4):
            step_into((0, slice(16 * b, 16 * b + 16)), four(rest, rest_at + 5 + b), old[3], new[3], 0.03, 0.05)
        for n, wide, order_ref, i, pieces, at in (
            (3, 384, heads_ref, 0, heads, head_at),
            (4, 512, units_ref, 2, rest, rest_at + 1),
        ):
            grads = [four(pieces, at + b) for b in range(n)]
            for g in range(GROUPS):
                part = jnp.concatenate([v[:, 128 * g : 128 * g + 128] for v in grads], 1)
                lanes = (0, slice(None), slice(wide * g, wide * g + wide))
                step_into(lanes, reorder(part, order_ref[...]), old[i], new[i], 0.03, 0.05)

    @pl.when(pl.program_id(0) == 0)
    def _():
        layer_step(late, 0, late, 3)

    @pl.when(pl.program_id(0) == 1)
    def _():
        layer_step(late, 12, early, 0)


def to_neighbours(slabs, ahead):
    step = -1 if ahead else 1
    along = [(i, (i + step) % 4) for i in range(4)]
    over = [(0, 1), (1, 0)]
    both = [(i * 2 + c, ((i + step) % 4) * 2 + 1 - c) for i in range(4) for c in range(2)]
    rows, cols, corner = slabs
    return (
        lax.ppermute(rows, "seq", along),
        lax.ppermute(cols, "col", over),
        lax.ppermute(corner, ("seq", "col"), both),
    )


def flat(z, x, core):
    return (z * 4 + (x % 2) * 2 + core) * 2 + x // 2


ALONG_X = [[flat(z, x, core) for x in range(4)] for z in range(4) for core in range(2)]
OVER_XZ = [[flat(z, x, core) for z in range(4) for x in range(4)] for core in range(2)]
OTHER_CORE = [(i, i ^ 1) for i in range(16)]


def from_z(distance):
    return [(((z + distance) % 4) * 4 + k, z * 4 + k) for z in range(4) for k in range(4)]


def from_x(distance):
    return [(flat(z, (x + distance) % 4, c), flat(z, x, c)) for z in range(4) for x in range(4) for c in range(2)]


ALONG_Z = [[z * 4 + k for z in range(4)] for k in range(4)]


def scattered_z(value):
    return lax.all_to_all(value, "img", 0, 0, tiled=True, axis_index_groups=ALONG_Z)


def from_core(value):
    return lax.ppermute(value, "img", OTHER_CORE)


BY_SEQ = [[(i, i ^ d) for i in range(4)] for d in (1, 2, 3)]
BY_Z = [[(z * 4 + k, (z ^ d) * 4 + k) for z in range(4) for k in range(4)] for d in (1, 2, 3)]
def both_cores(*pairs):
    arrays = [a for pair in pairs for a in pair]
    specs = [pl.BlockSpec((1, *a.shape[1:]), lambda i: (i, 0, 0, 0, 0)) for a in arrays]
    shape = (4, 4, sum(keep.shape[2] for keep, _ in pairs), 16, D)
    size = math.prod(shape) * 2
    return pl.pallas_call(
        add_kernel,
        grid=(4,),
        out_shape=jax.ShapeDtypeStruct(shape, BF),
        in_specs=specs,
        out_specs=pl.BlockSpec((1, *shape[1:]), lambda i: (i, 0, 0, 0, 0)),
        compiler_params=pltpu.CompilerParams(vmem_limit_bytes=VMEM_BYTES),
        cost_estimate=pl.CostEstimate(flops=size, bytes_accessed=3 * size, transcendentals=0),
    )(*arrays)


def by_seq(value):
    return [value] + [lax.ppermute(value, "seq", p) for p in BY_SEQ]


def update(early, late, heads, units, state):
    whole = [pl.BlockSpec(memory_space=pltpu.VMEM)] * 10
    parts = [pl.BlockSpec((1, *a.shape[1:]), lambda layer: (layer, 0, 0)) for a in state]
    return pl.pallas_call(
        update_kernel,
        grid=(LAYERS,),
        out_shape=[jax.ShapeDtypeStruct(a.shape, F32) for a in state],
        in_specs=whole + parts,
        out_specs=parts,
        compiler_params=pltpu.CompilerParams(vmem_limit_bytes=VMEM_BYTES),
        cost_estimate=pl.CostEstimate(flops=8 * 10**9, bytes_accessed=8 * 10**6, transcendentals=0),
    )(*early, *late, heads, units, *state)


def adamw(weight, first, second, grad, rate, decay):
    first = 0.9 * first + 0.1 * grad
    second = 0.999 * second + 0.001 * grad * grad
    first_hat = first / (1.0 - 0.9**STEP)
    second_hat = second / (1.0 - 0.999**STEP)
    return (first, second, weight - rate * (first_hat / (jnp.sqrt(second_hat) + 1e-08) + decay * weight))


def hidden_order(vector):
    return vector.reshape(32, 4, 16).transpose(1, 0, 2).reshape(HIDDEN)


def split_small(vector):
    pieces = [vector[i * D : (i + 1) * D][None] for i in range(8)]
    return pieces + [hidden_order(vector[8 * D :])[None]]


def score_table(table, hot):
    rows = lax.dot_general(table, hot, (((0,), (0,)), ((), ())), precision=highest, preferred_element_type=F32)
    rows = rows.reshape(HEADS, AREA, AREA) * log2e
    rows = jnp.pad(rows, ((0, 0), (0, 0), (0, SLOT - AREA)))
    rows = jnp.pad(rows, ((0, 0), (0, SLOT - AREA), (0, 0)), constant_values=padded_score)
    return jnp.concatenate([rows, rows], 2).reshape(HEADS * SLOT, 128)


def allowed_pairs(region):
    win = region.reshape(4, WIN, 4, WIN).transpose(0, 2, 1, 3).reshape(16, AREA)
    win = jnp.pad(win, ((0, 0), (0, SLOT - AREA)))
    same = win[:, :, None] == win[:, None, :]
    same = same | (jnp.arange(SLOT) >= AREA)[None, :, None]
    same = same.reshape(PAIRS, 2, SLOT, SLOT).transpose(0, 2, 1, 3).reshape(PAIRS, SLOT, 128)
    return same.astype(F32)


def local(
    images,
    out_grad,
    region_ids,
    rel_index,
    qkv_weight,
    qkv_first,
    qkv_second,
    proj_weight,
    proj_first,
    proj_second,
    expand_weight,
    expand_first,
    expand_second,
    contract_weight,
    contract_first,
    contract_second,
    small_params,
    small_first,
    small_second,
    bias_table,
    table_first,
    table_second,
):
    plain, plain_back, ahead, back, take_first, take_last = (jnp.asarray(a, BF) for a in placements())
    heads, units = (jnp.asarray(a, BF) for a in column_orders())
    img = lax.axis_index("img")
    x = lax.axis_index("col") * 2 + img // 2 % 2
    coords = jnp.stack([img // 4, x, img % 2]).astype(jnp.int32)
    matrices = (qkv_weight, proj_weight, expand_weight, contract_weight, heads, units)
    one, two = call(pack_kernel, [((4, 6, 16, D), BF), ((6, 16, D), BF)], matrices, us=3)

    def along_z(value):
        return [value] + [lax.ppermute(value, "img", from_z(d)) for d in (1, 2, 3)]

    def along_x(value):
        return [value] + [lax.ppermute(value, ("img", "col"), from_x(d)) for d in (1, 2, 3)]

    one0 = lax.all_to_all(one, ("img", "col"), 0, 0, tiled=True, axis_index_groups=ALONG_X)
    two0 = along_z(two)
    x0 = images.reshape(CELLS, D)
    g_out = out_grad.reshape(CELLS, D)
    by_key = jnp.pad(rel_index.T, ((0, 1), (0, SLOT - AREA)), constant_values=-1)
    by_key = jnp.concatenate([by_key, by_key], 1).reshape(25, 256)
    keys_hot = (jnp.arange(REL, dtype=jnp.int32)[:, None] == rel_index.T.reshape(1, AREA * AREA)).astype(F32)
    tables = [score_table(bias_table[layer], keys_hot) for layer in range(LAYERS)]
    region = lax.dynamic_slice_in_dim(region_ids, lax.axis_index("seq") * SIDE, SIDE, 0)
    mask = allowed_pairs(region)
    small = [split_small(small_params[layer]) for layer in range(LAYERS)]
    zero = jnp.zeros((1, D), F32)
    qkv_bias = [jnp.concatenate([s[2], zero, s[3]], 1) for s in small]

    by_columns = [columns(b) for b in range(4)]
    qkv_shape = ((PADDED, 3 * D), BF)
    attn_shape = ((PAIRS // 2, GROUPS, 256, 128), BF)
    slab_shapes = [((SLAB, D), BF), ((SLAB, D), BF), ((CORNER, D), BF)]
    cells16, cells32 = ((CELLS, D), BF), ((CELLS, D), F32)
    padded16 = ((PADDED, D), BF)
    wide16 = ((CELLS, HIDDEN), BF)

    copies = pltpu.SemaphoreType.DMA((32,))
    w_shapes = [((3, 32, 16, D), BF), ((9, 32, 16, D), BF)]
    g1, b1, _, _, bp, g2, b2, bo, bh = small[0]
    (hp0,) = call(enter_kernel, [padded16], (x0, g1, b1, plain), us=4)
    one0, two0 = call(stack_kernel, [((4, 6, 16, D), BF)] * 2, (one0, *two0), after=(hp0,))
    one0, two0 = along_z(one0), along_x(two0)
    one0 = one0 + [from_core(v) for v in one0]
    two0 = two0 + [from_core(v) for v in two0]
    half16 = ((PADDED // 2, D), BF)
    wq0, qkv0, attn0, attn0b, ctx0 = call(
        functools.partial(attend_kernel, False),
        [w_shapes[0], qkv_shape, attn_shape, attn_shape, cells16],
        (hp0, qkv_bias[0], tables[0], plain_back),
        [pltpu.VMEM(*padded16), copies],
        one0,
        coords,
        us=18,
        after=(mask, tables[1], by_key, *two0[1:4]),
        late=dict.fromkeys((0, 2, 3)),
        early=(0, 1, 2, 3),
    )
    spread, rest = call(
        pack_next_kernel, [((16, 3, 16, D), BF), ((9, 16, D), BF)], matrices, us=3, after=(ctx0,)
    )
    lines = lax.all_to_all(spread, ("img", "col"), 0, 0, tiled=True, axis_index_groups=OVER_XZ)
    one1 = lines
    (lines,) = call(stack_spread_kernel, [((4, 4, 9, 16, D), BF)], along_x(rest), us=2)
    wm0, mid0, h20, hidden0, slope0, x1, h1, *slabs = call(
        forward_kernel,
        [w_shapes[1], cells32, cells16, wide16, wide16, cells32, cells16, *slab_shapes],
        (x0, ctx0, bp, g2, b2, bo, bh, small[1][0], small[1][1], take_first),
        [pltpu.SemaphoreType.DMA((64,))],
        one0 + two0,
        coords,
        us=15,
        after=(spread, lines),
        late=dict.fromkeys((1, 0, 9)),
        early=(0, 1, 2, 3, 4, 5, 6),
    )
    two1 = scattered_z(lines).reshape(16, 9, 16, D)
    g1, b1, _, _, bp, g2, b2, bo, bh = small[1]
    (one1,) = held((one1,), (h1,))
    one1 = [one1, from_core(one1)]
    slabs = to_neighbours(slabs, True)
    wq1, hp1, qkv1, attn1, attn1b, ctxp1, *slabs = call(
        functools.partial(attend_kernel, True),
        [w_shapes[0], padded16, qkv_shape, attn_shape, attn_shape, padded16, *slab_shapes],
        (h1, *slabs, ahead, qkv_bias[1], tables[1], mask, take_last),
        [copies],
        one1,
        coords,
        us=18,
        after=(by_key,),
        late=dict.fromkeys((4, 0, 6, 7, 8)),
        early=(0, 1, 2, 3, 4, 5),
    )
    (two1,) = held((two1,), (hp1,))
    two1 = [two1, from_core(two1)]
    slabs = to_neighbours(slabs, False)
    out, dmid1, sums1, dbh1, dctx1, *slabs, keep, send = call(
        turn_kernel,
        [cells16, cells32, ((4, D), F32), ((1, HIDDEN), F32), cells16, *slab_shapes, *[((4, 4, 9, 16, D), BF)] * 2],
        (x1, ctxp1, *slabs, back, bp, g2, b2, bo, bh, g_out, take_first),
        [pltpu.VMEM(*a) for a in (w_shapes[1], cells16, cells32, cells16, wide16, wide16, wide16, cells16)] + [copies],
        two1,
        coords,
        us=34,
        late=dict.fromkeys((5, 1, 0, 11, 12)),
        early=(0, 1, 4, 8, 9),
    )
    slabs = to_neighbours(slabs, True)
    part_m1 = both_cores((keep, from_core(send)))
    dqkv1, dqb1, table1, dhp1, *slabs = call(
        attend_back_kernel,
        [qkv_shape, ((3, D), F32), ((HEADS, 256), F32), padded16, *slab_shapes],
        (dctx1, *slabs, ahead, qkv1, attn1, attn1b, wq1, take_last, by_key),
        [pltpu.VMEM((PADDED, D), BF), pltpu.VMEM((HEADS * SLOT, 128), F32)],
        us=20,
        after=(part_m1,),
        late=dict.fromkeys((4, 0, 5, 6, 7, 8, 9)),
        early=(0, 3),
    )
    slabs = to_neighbours(slabs, False)
    keep, send = call(
        grads_heads_kernel,
        [((4, 4, 3, 16, D), BF)] * 2,
        (hp1, dqkv1),
        place=coords,
        us=4,
        late={0: None, 1: by_columns[:3]},
        early=(0, 1),
    )
    pair_q1 = (keep, from_core(send))
    half_m1, *sent = call(sum_split_kernel, [((9, 16, D), BF)] * 4, (scattered_z(part_m1),), place=coords, us=2)
    grad1, dpre0, keep, send, dbo0, dbh0, norm1 = call(
        back_first_kernel,
        [cells32, wide16, *[((4, 4, 8, 16, D), BF)] * 2, ((1, D), F32), ((1, HIDDEN), F32), ((2, D), F32)],
        (dmid1, dhp1, *slabs, back, x1, small[1][0], hidden0, slope0, h20, wm0),
        [pltpu.VMEM((CELLS, D), BF)],
        place=coords,
        us=16,
        after=(half_m1, pair_q1[0]),
        late={5: None, 1: None, 6: None, 0: None, 11: [slice(5, 9)], 9: by_columns, 8: by_columns, 10: None},
        early=(0, 1, 2, 3),
    )
    got = [lax.ppermute(v, ("img", "col"), from_x(4 - d)) for d, v in zip((1, 2, 3), sent)]
    grad_m1 = sum((v.astype(F32) for v in got), half_m1.astype(F32)).astype(BF)
    dmid0, dwp0, sums0, dctxp0 = call(
        middle_first_kernel,
        [cells32, ((D, D), BF), ((3, D), F32), padded16],
        (grad1, dpre0, mid0, ctx0, wm0, small[0][5], plain),
        [pltpu.VMEM((CELLS, D), BF)],
        us=8,
        after=(grad_m1,),
        late={4: (0, 5), 1: by_columns, 2: None, 0: None, 3: None, 6: None},
        early=(0, 1),
    )
    part_0 = both_cores((keep, from_core(send)), pair_q1)
    grads_m1 = by_seq(grad_m1)
    half_0 = scattered_z(part_0)
    *keep_send, input_grad, sums = call(
        attend_back_end_kernel,
        [*[((4, 4, 4, 16, D), BF)] * 2, cells32, ((40, D), F32)],
        (dctxp0, qkv0, attn0, attn0b, hp0, dwp0, by_key, wq0, plain_back, x0, dmid0, small[0][0])
        + (norm1, dqb1, sums1, dbh1, table1, sums0, dbo0, dbh0),
        [pltpu.VMEM(*qkv_shape), pltpu.VMEM((HEADS * SLOT, 128), F32), pltpu.VMEM(*padded16)],
        place=coords,
        us=26,
        late=dict.fromkeys((0, 1, 2, 3, 4, 5, 7, 8, 9, 10)),
        early=(0, 1, 2),
        after=(part_0, *grads_m1),
    )
    other, more = from_core(keep_send[1]), from_core(sums)
    near, mine, *sent = call(
        to_xz_kernel,
        [((16, 5, 16, D), BF)] + [((11, 16, D), BF)] * 4,
        (keep_send[0], other, half_0, sums, more),
        place=coords,
        us=5,
    )
    near = lax.all_to_all(near, ("img", "col"), 0, 0, tiled=True, axis_index_groups=OVER_XZ)
    pieces = [mine] + [lax.ppermute(v, ("img", "col"), from_x(4 - d)) for d, v in zip((1, 2, 3), sent)]
    (late,) = call(to_seq_kernel, [((16, 16, D), BF)], (near, *pieces), us=3)
    late = by_seq(late)
    (smalls,) = call(to_plane_kernel, [((16, 16, 128), F32)], late, us=1)
    smalls = lax.all_to_all(smalls, ("img", "col"), 0, 0, tiled=True, axis_index_groups=OVER_XZ)

    state = (
        (qkv_weight, qkv_first, qkv_second),
        (proj_weight, proj_first, proj_second),
        (expand_weight, expand_first, expand_second),
        (contract_weight, contract_first, contract_second),
    )
    flat_state = [a for three in state for a in three]
    swap = functools.partial(jnp.transpose, axes=(0, 2, 1))
    small = (small_params, small_first, small_second, swap(bias_table), swap(table_first), swap(table_second))
    done = update(grads_m1, late, heads, units, flat_state)
    last = call(
        update_small_kernel,
        [(a.shape, F32) for a in small] + [((LAYERS, D), F32)],
        (smalls, units, *small),
        [pltpu.VMEM((48, D), F32)],
        us=3,
    )
    return (
        out.reshape(images.shape),
        input_grad.reshape(images.shape),
        *done,
        *last[:3],
        *(swap(a) for a in last[3:6]),
        last[6],
    )


def solution(mesh):
    cells = P("img", "seq", "col", None)
    matrix = P(None, ("img", "col"), None)
    in_specs = (cells, cells, P(None, "col"), P(), *([matrix] * 12), *([P()] * 6))
    out_specs = (cells, cells, *([matrix] * 12), *([P()] * 7))
    return jax.shard_map(local, mesh=mesh, in_specs=in_specs, out_specs=out_specs, check_vma=False)
```

```python
import functools
import math

import jax
import jax.numpy as jnp
import numpy as np
from jax import lax
from jax.experimental import pallas as pl
from jax.experimental.pallas import tpu as pltpu
from jax.sharding import PartitionSpec as P

D = 512
HEADS = 16
HEAD_DIM = 32
WIN = 7
SHIFT = 3
LAYERS = 2
STEP = 10
REL = 169
SIDE = 28
CELLS = SIDE * SIDE
AREA = WIN * WIN
SLOT = 64
PADDED = 16 * SLOT
PAIRS = 8
GROUPS = 4
SLAB = 96
CORNER = 16
HALO = 2 * SLAB + CORNER
HIDDEN = 4 * D

BF = jnp.bfloat16
F32 = jnp.float32
epsilon = 1e-05
log2e = math.log2(math.e)
masked_score = -1000000000.0 * log2e
padded_score = -1e30
highest = lax.Precision.HIGHEST
VMEM_BYTES = 58 * 2**20


def padded_row(r, c):
    return ((r // WIN) * 4 + c // WIN) * SLOT + (r % WIN) * WIN + c % WIN


def ahead_source(r, c):
    r, c = r + SHIFT, c + SHIFT
    if r < SIDE and c < SIDE:
        return r * SIDE + c
    if c < SIDE:
        return CELLS + (r - SIDE) * SIDE + c
    if r < SIDE:
        return CELLS + SLAB + r * SHIFT + c - SIDE
    return CELLS + 2 * SLAB + (r - SIDE) * SHIFT + c - SIDE


def back_source(r, c):
    if r >= SHIFT and c >= SHIFT:
        return padded_row(r - SHIFT, c - SHIFT)
    if c >= SHIFT:
        return PADDED + r * SIDE + c - SHIFT
    if r >= SHIFT:
        return PADDED + SLAB + (r - SHIFT) * SHIFT + c
    return PADDED + 2 * SLAB + r * SHIFT + c


def placements():
    plain = np.zeros((PADDED, CELLS), np.float32)
    ahead = np.zeros((PADDED, CELLS + HALO), np.float32)
    back = np.zeros((CELLS, PADDED + HALO), np.float32)
    take_first = np.zeros((HALO, CELLS), np.float32)
    take_last = np.zeros((HALO, PADDED), np.float32)
    for r in range(SIDE):
        for c in range(SIDE):
            plain[padded_row(r, c), r * SIDE + c] = 1
            ahead[padded_row(r, c), ahead_source(r, c)] = 1
            back[r * SIDE + c, back_source(r, c)] = 1
    edge = SIDE - SHIFT
    for a in range(SHIFT):
        for b in range(SIDE):
            take_first[a * SIDE + b, a * SIDE + b] = 1
            take_first[SLAB + b * SHIFT + a, b * SIDE + a] = 1
            take_last[a * SIDE + b, padded_row(edge + a, b)] = 1
            take_last[SLAB + b * SHIFT + a, padded_row(b, edge + a)] = 1
        for b in range(SHIFT):
            take_first[2 * SLAB + a * SHIFT + b, a * SIDE + b] = 1
            take_last[2 * SLAB + a * SHIFT + b, padded_row(edge + a, edge + b)] = 1
    return (plain, plain.T.copy(), ahead, back, take_first, take_last)


def column_orders():
    heads = np.zeros((384, 384), np.float32)
    units = np.zeros((512, 512), np.float32)
    for n in range(4):
        for part in range(3):
            for d in range(HEAD_DIM):
                heads[n * 96 + part * 32 + d, part * 128 + n * 32 + d] = 1
    for r in range(8):
        for b in range(4):
            for i in range(16):
                units[r * 64 + b * 16 + i, b * 128 + r * 16 + i] = 1
    return heads, units


def dot(a, b):
    return lax.dot_general(a, b, (((1,), (0,)), ((), ())), preferred_element_type=F32)


def dot_nt(a, b):
    return lax.dot_general(a, b, (((1,), (1,)), ((), ())), preferred_element_type=F32)


def dot_tn(a, b):
    return lax.dot_general(a, b, (((0,), (0,)), ((), ())), preferred_element_type=F32)


def normalized(x):
    centred = x - jnp.mean(x, -1, keepdims=True)
    inverse = lax.rsqrt(jnp.mean(centred * centred, -1, keepdims=True) + epsilon)
    return centred * inverse, inverse


def norm_back(grad, x, gain):
    hat, inverse = normalized(x)
    grad_hat = grad * gain
    grad_x = inverse * (
        grad_hat
        - jnp.mean(grad_hat, -1, keepdims=True)
        - hat * jnp.mean(grad_hat * hat, -1, keepdims=True)
    )
    return grad_x, jnp.sum(grad * hat, 0, keepdims=True), jnp.sum(grad, 0, keepdims=True)


def gelu_both(u):
    a = jnp.abs(u)
    t = 1.0 / (1.0 + (0.3275911 * 0.5**0.5) * a)
    e = jnp.exp2((-0.5 * log2e) * u * u)
    poly = t * (
        0.5 * 0.254829592
        + t * (0.5 * -0.284496736 + t * (0.5 * 1.421413741 + t * (0.5 * -1.453152027 + t * (0.5 * 1.061405429))))
    )
    tail = poly * e
    phi = jnp.where(u >= 0, 1.0 - tail, tail)
    return u * phi, phi + u * e * (1.0 / math.sqrt(2 * math.pi))


def head_rows(pair):
    lane = lax.broadcasted_iota(jnp.int32, pair.shape, 1) % 128 // HEAD_DIM
    zero = jnp.zeros_like(pair)
    return jnp.concatenate([jnp.where(lane == h, pair, zero) for h in range(4)], 0)


def head_fold(rows):
    lane = lax.broadcasted_iota(jnp.int32, (SLOT, 256), 1) % 128 // HEAD_DIM
    out = rows[:SLOT]
    for h in range(1, 4):
        out = jnp.where(lane == h, rows[h * SLOT : (h + 1) * SLOT], out)
    return out


def side_by_side(ref, start, lane):
    return jnp.concatenate(
        [ref[pl.ds(start, SLOT), lane : lane + 128], ref[pl.ds(start + SLOT, SLOT), lane : lane + 128]], 1
    )


def block_diagonal(pair):
    lane = lax.broadcasted_iota(jnp.int32, pair.shape, 1)
    zero = jnp.zeros_like(pair)
    return jnp.concatenate([jnp.where(lane < 128, pair, zero), jnp.where(lane >= 128, pair, zero)], 0)


def store_diagonal(ref, start, lane, rows):
    ref[pl.ds(start, SLOT), lane : lane + 128] = rows[:SLOT, :128].astype(ref.dtype)
    ref[pl.ds(start + SLOT, SLOT), lane : lane + 128] = rows[SLOT:, 128:].astype(ref.dtype)


class Moves:
    def __init__(self, sems):
        self.loads, self.stores, self.started, self.sems = {}, {}, [], sems

    def load(self, pairs, buffer):
        at = len(self.started)
        for source, target in pairs:
            copy = pltpu.make_async_copy(source, target, self.sems.at[len(self.started)])
            copy.start()
            self.started.append(copy)
        self.loads[id(buffer)] = range(at, len(self.started))

    def need(self, *refs, part=None):
        for ref in refs:
            places = self.loads.get(id(ref), ())
            for at in places if part is None else places[part : part + 1]:
                if self.started[at] is not None:
                    self.started[at].wait()
                    self.started[at] = None

    def ship(self, ref, at=()):
        if id(ref) in self.stores:
            copy = pltpu.make_async_copy(
                ref.at[at] if at else ref,
                self.stores[id(ref)].at[at] if at else self.stores[id(ref)],
                self.sems.at[len(self.started)],
            )
            copy.start()
            self.started.append(copy)

    def finish(self):
        for copy in self.started:
            if copy is not None:
                copy.wait()


def columns(b):
    return (slice(None), slice(b * D, (b + 1) * D))


def of_blocks(b):
    return (slice(None), slice(None), b)


def call(body, outs, args, scratch=(), pieces=(), place=None, us=1, after=(), late=None, early=()):
    shapes = [jax.ShapeDtypeStruct(s, d) for s, d in outs]
    late = late or {}
    lead = [] if place is None else [place]
    anywhere, inside = pl.BlockSpec(memory_space=pl.ANY), pl.BlockSpec(memory_space=pltpu.VMEM)
    specs = [anywhere] * len(after) + [pl.BlockSpec(memory_space=pltpu.SMEM)] * len(lead) + [anywhere] * len(pieces)
    specs += [anywhere if i in late else inside for i in range(len(args))]
    buffers = []
    for i, parts in late.items():
        rows = parts[1:] if isinstance(parts, tuple) else args[i].shape[:1]
        buffers.append(pltpu.VMEM((*rows, *args[i].shape[1:]), args[i].dtype))
    buffers += [pltpu.VMEM(*outs[i]) for i in early]
    moving = bool(buffers)
    if moving:
        buffers.append(pltpu.SemaphoreType.DMA((96,)))

    def whole(*refs):
        refs = refs[len(after) :]
        first, n_in = len(lead) + len(pieces), len(lead) + len(pieces) + len(args)
        ins, results = list(refs[:n_in]), list(refs[n_in : n_in + len(outs)])
        rest = refs[n_in + len(outs) :]
        if not moving:
            body(*refs)
            return
        own, buffer = rest[: len(scratch)], rest[len(scratch) :]
        moves = Moves(buffer[-1])
        for (i, parts), target in zip(late.items(), buffer):
            source = ins[first + i]
            if parts is None:
                pairs = [(source, target)]
            elif isinstance(parts, tuple):
                pairs = [(source.at[pl.ds(*parts)], target)]
            else:
                pairs = [(source.at[part], target.at[part]) for part in parts]
            moves.load(pairs, target)
            ins[first + i] = target
        for i, source in zip(early, buffer[len(late) :]):
            moves.stores[id(source)] = results[i]
            results[i] = source
        body(moves, *ins, *results, *own)
        moves.finish()

    return pl.pallas_call(
        whole,
        out_shape=shapes,
        in_specs=specs,
        out_specs=[anywhere if i in early else inside for i in range(len(outs))],
        scratch_shapes=list(scratch) + buffers,
        compiler_params=pltpu.CompilerParams(vmem_limit_bytes=VMEM_BYTES),
        cost_estimate=pl.CostEstimate(flops=us * 3 * 10**9, bytes_accessed=us * 10**6, transcendentals=0),
    )(*after, *lead, *pieces, *args)


def held(arrays, after):
    anywhere = pl.BlockSpec(memory_space=pl.ANY)
    return pl.pallas_call(
        lambda *refs: None,
        out_shape=[jax.ShapeDtypeStruct(a.shape, a.dtype) for a in arrays],
        in_specs=[anywhere] * (len(arrays) + len(after)),
        out_specs=[anywhere] * len(arrays),
        input_output_aliases={i: i for i in range(len(arrays))},
    )(*arrays, *after)


def owner_of(z, x, core):
    return z * 8 + (x % 2) * 4 + core * 2 + x // 2


def assembly(coords_ref, sets, w_ref, sems):
    z, x, core = coords_ref[0], coords_ref[1], coords_ref[2]
    copies = []
    for pieces, far, (low, count), first in sets:
        for k, piece in enumerate(pieces):
            from_core = core if k < len(pieces) // 2 else 1 - core
            for i in range(piece.shape[0]):
                if far == "zx":
                    owner = owner_of(i // 4, i % 4, from_core)
                elif far == "z":
                    owner = owner_of(i // 4, lax.rem(x + i % 4, 4), from_core)
                elif far == "by z":
                    owner = owner_of(lax.rem(z + k % 4, 4), i, from_core)
                else:
                    owner = owner_of(lax.rem(z + i, 4), lax.rem(x + k % 4, 4), from_core)
                source, target = piece.at[i, pl.ds(low, count)], w_ref.at[pl.ds(first, count), owner]
                copies.append(pltpu.make_async_copy(source, target, sems.at[len(copies)]))
    for c in copies:
        c.start()
    return copies


def block(ref, b):
    return ref[b].reshape(D, D)


def block_lanes(ref, b, lanes):
    return ref[b, :, :, lanes].reshape(D, lanes.stop - lanes.start)


def block_rows(ref, b, half):
    return ref[b, half * 16 : half * 16 + 16].reshape(256, D)


def store_grad(place_ref, keep_ref, send_ref, b, half, rows):
    first = place_ref[2] == 0
    rows = rows.astype(BF)
    for zz in range(2):
        for x in range(4):
            base = (zz * 8 + (x % 2) * 4 + x // 2) * 16
            one, two = rows[base : base + 16], rows[base + 32 : base + 48]
            keep_ref[half * 2 + zz, x, b] = jnp.where(first, one, two)
            send_ref[half * 2 + zz, x, b] = jnp.where(first, two, one)


def pack_blocks(layer, qkv_ref, proj_ref, expand_ref, contract_ref, heads_ref, units_ref, store):
    every = slice(None)
    store(3, every, proj_ref[layer].astype(BF))
    for b in range(4):
        store(8 + b, every, contract_ref[layer, 16 * b : 16 * b + 16, :].astype(BF))
    for g in range(GROUPS):
        lanes = slice(128 * g, 128 * g + 128)
        part = dot(qkv_ref[layer, :, 384 * g : 384 * g + 384].astype(BF), heads_ref[...]).astype(BF)
        for s in range(3):
            store(s, lanes, part[:, 128 * s : 128 * s + 128])
        part = dot(expand_ref[layer, :, 512 * g : 512 * g + 512].astype(BF), units_ref[...]).astype(BF)
        for b in range(4):
            store(4 + b, lanes, part[:, 128 * b : 128 * b + 128])


def pack_kernel(*refs):
    one_ref, two_ref = refs[6:]

    def store(b, lanes, value):
        if b < 6:
            for i in range(4):
                one_ref[i, b, :, lanes] = value
        else:
            two_ref[b - 6, :, lanes] = value

    pack_blocks(0, *refs[:6], store)


def pack_next_kernel(*refs):
    spread_ref, rest_ref = refs[6:]

    def store(b, lanes, value):
        if b < 3:
            for i in range(16):
                spread_ref[i, b, :, lanes] = value
        else:
            rest_ref[b - 3, :, lanes] = value

    pack_blocks(1, *refs[:6], store)


def stack_kernel(*refs):
    for k in range(4):
        refs[4][k] = refs[k][...]


def stack_spread_kernel(*refs):
    for k in range(4):
        for x in range(4):
            refs[4][x, k] = refs[k][...]


def enter_kernel(x_ref, gain_ref, bias_ref, place_ref, hp_ref):
    hat, _ = normalized(x_ref[...].astype(F32))
    h = (hat * gain_ref[...] + bias_ref[...]).astype(BF)
    hp_ref[...] = dot(place_ref[...], h).astype(BF)


def attend_pairs(qkv_ref, first, table_ref, mask_ref, attn_ref, into_ref):
    def one_pair(p, carry):
        start = pl.multiple_of(first + p * 128, 128)
        for g in range(GROUPS):
            lane = g * 128
            keys = head_rows(side_by_side(qkv_ref, start, D + lane))
            queries = block_diagonal(side_by_side(qkv_ref, start, lane))
            scores = dot_nt(keys, queries) * (HEAD_DIM**-0.5 * log2e) + table_ref[g * 256 : (g + 1) * 256, :]
            scores = scores.reshape(4, SLOT, 128)
            if mask_ref is not None:
                scores = jnp.where(mask_ref[p][None] > 0, scores, masked_score)
            scores = jnp.exp2(scores - jnp.max(scores, 1, keepdims=True))
            scores = scores * (1.0 / jnp.sum(scores, 1, keepdims=True))
            attn = scores.reshape(256, 128).astype(BF)
            attn_ref[p, g] = attn
            values = head_rows(side_by_side(qkv_ref, start, 2 * D + lane))
            store_diagonal(into_ref, pl.multiple_of(p * 128, 128), lane, dot_tn(attn, values))
        return carry

    lax.fori_loop(0, PAIRS // 2, one_pair, 0, unroll=4)


def attend_kernel(shifted, moves, *refs):
    count = 2 if shifted else 8
    coords_ref, pieces, refs = refs[0], refs[1 : count + 1], refs[count + 1 :]
    if shifted:
        h_ref, rows_ref, cols_ref, corner_ref, place_ref, bias_ref, table_ref, mask_ref, take_ref = refs[:9]
        w_ref, hp_ref, qkv_ref, one_ref, two_ref, ctxp_ref, rows_out, cols_out, corner_out, sems = refs[9:]
        copies = assembly(coords_ref, [(pieces, "zx", (0, 3), 0)], w_ref, sems)
        moves.need(place_ref, h_ref)
        place = place_ref[...]
        hp = dot(place[:, :CELLS], h_ref[...])
        slabs = jnp.concatenate([rows_ref[...], cols_ref[...], corner_ref[...]], 0)
        hp_ref[...] = (hp + dot(place[:, CELLS:], slabs)).astype(BF)
        moves.ship(hp_ref)
    else:
        hp_ref, bias_ref, table_ref, place_ref = refs[:4]
        w_ref, qkv_ref, one_ref, two_ref, ctx_ref, ctxp_ref, sems = refs[4:]
        mask_ref = None
        copies = assembly(coords_ref, [(pieces, "by z", (0, 3), 0)], w_ref, sems)
        moves.need(hp_ref)
    for c in copies:
        c.wait()
    moves.ship(w_ref)
    for s in range(3):
        for half in range(2):
            lanes = slice(half * 256, half * 256 + 256)
            wide = slice(s * D + half * 256, s * D + half * 256 + 256)
            qkv_ref[:, wide] = (dot(hp_ref[...], block_lanes(w_ref, s, lanes)) + bias_ref[:, wide]).astype(BF)
        moves.ship(qkv_ref, columns(s))
    upper = PADDED // 2
    masks = (None, None) if mask_ref is None else (mask_ref.at[:4], mask_ref.at[4:])
    moves.need(table_ref)
    if shifted:
        moves.need(mask_ref)
    attend_pairs(qkv_ref, 0, table_ref, masks[0], one_ref, ctxp_ref.at[:upper])
    moves.ship(one_ref)
    attend_pairs(qkv_ref, upper, table_ref, masks[1], two_ref, ctxp_ref.at[upper:])
    moves.ship(two_ref)
    if shifted:
        moves.ship(ctxp_ref)
        moves.need(take_ref)
        sent = dot(take_ref[...], ctxp_ref[...]).astype(BF)
        rows_out[...] = sent[:SLAB]
        cols_out[...] = sent[SLAB : 2 * SLAB]
        corner_out[...] = sent[2 * SLAB :]
    else:
        moves.need(place_ref)
        ctx_ref[...] = dot(place_ref[...], ctxp_ref[...]).astype(BF)


def feed_forward(moves, x_ref, ctx_ref, w_ref, vectors, mid_ref, h2_ref, hidden_ref, slope_ref):
    bp_ref, g2_ref, b2_ref, bo_ref, bh_ref = vectors
    mid_ref[...] = x_ref[...].astype(F32) + dot(ctx_ref[...], block(w_ref, 0)) + bp_ref[...]
    moves.ship(mid_ref)
    hat, _ = normalized(mid_ref[...])
    h2_ref[...] = (hat * g2_ref[...] + b2_ref[...]).astype(BF)
    moves.ship(h2_ref)
    for b in range(4):
        for half in range(2):
            lanes = slice(half * 256, half * 256 + 256)
            wide = slice(b * D + half * 256, b * D + half * 256 + 256)
            pre = dot(h2_ref[...], block_lanes(w_ref, 1 + b, lanes)) + bh_ref[:, wide]
            hidden, slope = gelu_both(pre)
            hidden_ref[:, wide] = hidden.astype(BF)
            slope_ref[:, wide] = slope.astype(BF)
        moves.ship(hidden_ref, columns(b))
        moves.ship(slope_ref, columns(b))
    out = mid_ref[...] + bo_ref[...]
    for b in range(4):
        out = out + dot(hidden_ref[:, b * D : (b + 1) * D], block(w_ref, 5 + b))
    return out


def forward_kernel(moves, *refs):
    coords_ref, ones, twos, refs = refs[0], refs[1:9], refs[9:17], refs[17:]
    x_ref, ctx_ref, *vectors = refs[:7]
    g1_ref, b1_ref, take_ref, w_ref, *kept = refs[7:15]
    out_ref, h_ref, rows_out, cols_out, corner_out, sems = refs[15:]
    copies = assembly(coords_ref, [(ones, "by z", (3, 3), 0), (twos, "by x", (0, 6), 3)], w_ref, sems)
    moves.need(ctx_ref)
    for c in copies:
        c.wait()
    moves.ship(w_ref)
    moves.need(x_ref)
    out = feed_forward(moves, x_ref, ctx_ref, w_ref, vectors, *kept)
    out_ref[...] = out
    moves.ship(out_ref)
    hat, _ = normalized(out)
    h_ref[...] = (hat * g1_ref[...] + b1_ref[...]).astype(BF)
    moves.ship(h_ref)
    moves.need(take_ref)
    sent = dot(take_ref[...], h_ref[...]).astype(BF)
    rows_out[...] = sent[:SLAB]
    cols_out[...] = sent[SLAB : 2 * SLAB]
    corner_out[...] = sent[2 * SLAB :]


def hidden_back_pass(moves, gm_ref, slope_ref, w_ref, dpre_ref, dbh_ref):
    moves.need(w_ref, part=0)
    for b in range(4):
        moves.need(slope_ref, part=b)
        for half in range(2):
            wide = slice(b * D + half * 256, b * D + half * 256 + 256)
            dpre = dot_nt(gm_ref[...], block_rows(w_ref, 5 + b, half)) * slope_ref[:, wide].astype(F32)
            dpre = dpre.astype(BF)
            dpre_ref[:, wide] = dpre
            dbh_ref[:, wide] = jnp.sum(dpre.astype(F32), 0, keepdims=True)
        moves.ship(dpre_ref, columns(b))


def middle_back_pass(moves, grad_ref, dpre_ref, w_ref, mid_ref, g2_ref, dmid_ref, go_ref, small_ref):
    moves.need(w_ref)
    moves.need(dpre_ref, part=0)
    dh2 = dot_nt(dpre_ref[:, :D], block(w_ref, 1))
    for b in range(1, 4):
        moves.need(dpre_ref, part=b)
        dh2 = dh2 + dot_nt(dpre_ref[:, b * D : (b + 1) * D], block(w_ref, 1 + b))
    moves.need(mid_ref, grad_ref)
    dx, dg2, db2 = norm_back(dh2, mid_ref[...], g2_ref[...])
    small_ref[1:2, :] = dg2
    small_ref[2:3, :] = db2
    dmid_ref[...] = grad_ref[...].astype(F32) + dx
    moves.ship(dmid_ref)
    go_ref[...] = dmid_ref[...].astype(BF)
    moves.ship(go_ref)
    small_ref[0:1, :] = jnp.sum(go_ref[...].astype(F32), 0, keepdims=True)


def turn_kernel(moves, *refs):
    coords_ref, pieces, refs = refs[0], refs[1:3], refs[3:]
    x_ref, ctxp_ref, rows_ref, cols_ref, corner_ref, place_ref, *vectors = refs[:11]
    g_ref, take_ref, out_ref, dmid_ref, small_ref, dbh_ref, dctx_ref, rows_out, cols_out, corner_out = refs[11:21]
    keep_ref, send_ref, w_ref, ctx_ref, mid_ref, h2_ref, hidden_ref, slope_ref, dpre_ref, go_ref, sems = refs[21:]
    copies = assembly(coords_ref, [(pieces, "z", (0, 9), 0)], w_ref, sems)
    moves.need(place_ref, ctxp_ref)
    place = place_ref[...]
    slabs = jnp.concatenate([rows_ref[...], cols_ref[...], corner_ref[...]], 0)
    ctx_ref[...] = (dot(place[:, :PADDED], ctxp_ref[...]) + dot(place[:, PADDED:], slabs)).astype(BF)
    for c in copies:
        c.wait()
    moves.need(x_ref)
    out = feed_forward(moves, x_ref, ctx_ref, w_ref, vectors, mid_ref, h2_ref, hidden_ref, slope_ref)
    out_ref[...] = out.astype(BF)
    moves.ship(out_ref)
    moves.need(g_ref)
    small_ref[3:4, :] = jnp.sum(g_ref[...].astype(F32), 0, keepdims=True)
    hidden_back_pass(moves, g_ref, slope_ref, w_ref, dpre_ref, dbh_ref)
    middle_back_pass(moves, g_ref, dpre_ref, w_ref, mid_ref, vectors[1], dmid_ref, go_ref, small_ref)
    dctx_ref[...] = dot_nt(go_ref[...], block(w_ref, 0)).astype(BF)
    moves.ship(dctx_ref)
    moves.need(take_ref)
    sent = dot(take_ref[...], dctx_ref[...]).astype(BF)
    rows_out[...] = sent[:SLAB]
    cols_out[...] = sent[SLAB : 2 * SLAB]
    corner_out[...] = sent[2 * SLAB :]
    hidden_grads(moves, coords_ref, 1, g_ref, hidden_ref, h2_ref, dpre_ref, keep_ref, send_ref)
    for half in range(2):
        rows = slice(half * 256, half * 256 + 256)
        store_grad(coords_ref, keep_ref, send_ref, 0, half, dot_tn(ctx_ref[:, rows], go_ref[...]))
    moves.ship(keep_ref, of_blocks(0))
    moves.ship(send_ref, of_blocks(0))


def hidden_grads(moves, coords_ref, first, gm_ref, hidden_ref, h2_ref, dpre_ref, keep_ref, send_ref):
    for b in range(4):
        moves.need(hidden_ref, part=b)
        for half in range(2):
            wide = slice(b * D + half * 256, b * D + half * 256 + 256)
            grad_c = dot_tn(hidden_ref[:, wide], gm_ref[...])
            store_grad(coords_ref, keep_ref, send_ref, first + 4 + b, half, grad_c)
        moves.ship(keep_ref, of_blocks(first + 4 + b))
        moves.ship(send_ref, of_blocks(first + 4 + b))
    moves.need(h2_ref, dpre_ref)
    for b in range(4):
        for half in range(2):
            rows = slice(half * 256, half * 256 + 256)
            grad_e = dot_tn(h2_ref[:, rows], dpre_ref[:, b * D : (b + 1) * D])
            store_grad(coords_ref, keep_ref, send_ref, first + b, half, grad_e)
        moves.ship(keep_ref, of_blocks(first + b))
        moves.ship(send_ref, of_blocks(first + b))


def back_first_kernel(moves, *refs):
    coords_ref, dmid1_ref, dhp_ref, rows_ref, cols_ref, corner_ref, back_ref, x1_ref, g1_ref = refs[:9]
    hidden_ref, slope_ref, h2_ref, w_ref = refs[9:13]
    grad_ref, dpre_ref, keep_ref, send_ref, dbo_ref, dbh_ref, above_ref, gm_ref = refs[13:]
    moves.need(back_ref, dhp_ref)
    back = back_ref[...]
    slabs = jnp.concatenate([rows_ref[...], cols_ref[...], corner_ref[...]], 0)
    dh = dot(back[:, :PADDED], dhp_ref[...]) + dot(back[:, PADDED:], slabs)
    moves.need(x1_ref)
    dx, dg1, db1 = norm_back(dh, x1_ref[...], g1_ref[...])
    above_ref[0:1, :] = dg1
    above_ref[1:2, :] = db1
    moves.need(dmid1_ref)
    grad = dmid1_ref[...] + dx
    grad_ref[...] = grad
    moves.ship(grad_ref)
    gm_ref[...] = grad.astype(BF)
    dbo_ref[...] = jnp.sum(gm_ref[...].astype(F32), 0, keepdims=True)
    hidden_back_pass(moves, gm_ref, slope_ref, w_ref, dpre_ref, dbh_ref)
    hidden_grads(moves, coords_ref, 0, gm_ref, hidden_ref, h2_ref, dpre_ref, keep_ref, send_ref)


def middle_first_kernel(moves, grad_ref, dpre_ref, mid_ref, ctx_ref, w_ref, g2_ref, place_ref, *outs):
    dmid_ref, dwp_ref, small_ref, dctxp_ref, go_ref = outs
    middle_back_pass(moves, grad_ref, dpre_ref, w_ref, mid_ref, g2_ref, dmid_ref, go_ref, small_ref)
    moves.need(ctx_ref)
    for half in range(2):
        rows = slice(half * 256, half * 256 + 256)
        dwp_ref[rows, :] = dot_tn(ctx_ref[:, rows], go_ref[...]).astype(BF)
    moves.ship(dwp_ref)
    dctx = dot_nt(go_ref[...], block(w_ref, 0)).astype(BF)
    moves.need(place_ref)
    dctxp_ref[...] = dot(place_ref[...], dctx).astype(BF)


def attend_back_pairs(first, qkv_ref, attn_ref, dctxp_ref, dqkv_ref, dtable_ref):
    if first == 0:
        dtable_ref[...] = jnp.zeros_like(dtable_ref)
    scale = HEAD_DIM**-0.5

    def one_pair(p, carry):
        start = pl.multiple_of(first + p * 128, 128)
        for g in range(GROUPS):
            lane = g * 128
            attn = attn_ref[p, g]
            keys = head_rows(side_by_side(qkv_ref, start, D + lane))
            values = head_rows(side_by_side(qkv_ref, start, 2 * D + lane))
            queries = block_diagonal(side_by_side(qkv_ref, start, lane))
            grads = block_diagonal(side_by_side(dctxp_ref, start, lane))
            probs = attn.astype(F32).reshape(4, SLOT, 128)
            dprobs = dot_nt(values, grads).reshape(4, SLOT, 128)
            dscores = probs * (dprobs - jnp.sum(probs * dprobs, 1, keepdims=True))
            dscores = dscores.reshape(256, 128).astype(BF)
            dtable_ref[g * 256 : (g + 1) * 256, :] += dscores.astype(F32)
            store_diagonal(dqkv_ref, start, lane, dot_tn(dscores, keys) * scale)
            dkeys = (head_fold(dot(dscores, queries)) * scale).astype(BF)
            dqkv_ref[pl.ds(start, SLOT), D + lane : D + lane + 128] = dkeys[:, :128]
            dqkv_ref[pl.ds(start + SLOT, SLOT), D + lane : D + lane + 128] = dkeys[:, 128:]
            dvalues = head_fold(dot(attn, grads)).astype(BF)
            dqkv_ref[pl.ds(start, SLOT), 2 * D + lane : 2 * D + lane + 128] = dvalues[:, :128]
            dqkv_ref[pl.ds(start + SLOT, SLOT), 2 * D + lane : 2 * D + lane + 128] = dvalues[:, 128:]
        return carry

    lax.fori_loop(0, PAIRS // 2, one_pair, 0)


def table_sum(dtable_ref, by_key_ref, out_ref):
    total = jnp.zeros((2 * HEADS, 256), F32)
    row = lax.broadcasted_iota(jnp.int32, (256, 256), 0)
    for c in range(25):
        hot = jnp.where(row == by_key_ref[c : c + 1, :], 1.0, 0.0).astype(BF)
        keys = [dtable_ref[pl.ds(2 * c + k, HEADS, stride=SLOT), :] for k in range(2)]
        rows = jnp.concatenate(keys, 1)
        high = rows.astype(BF)
        low = (rows - high.astype(F32)).astype(BF)
        total = total + dot_nt(jnp.concatenate([high, low], 0), hot)
    out_ref[...] = total[:HEADS] + total[HEADS:]


def attend_back_kernel(moves, *refs):
    dctx_ref, rows_ref, cols_ref, corner_ref, place_ref, qkv_ref, one_ref, two_ref, w_ref, take_ref, key_ref = refs[:11]
    dqkv_ref, dbias_ref, table_ref, dhp_ref, rows_out, cols_out, corner_out, dctxp_ref, dtable_ref = refs[11:]
    moves.need(place_ref, dctx_ref)
    place = place_ref[...]
    slabs = jnp.concatenate([rows_ref[...], cols_ref[...], corner_ref[...]], 0)
    dctxp_ref[...] = (dot(place[:, :CELLS], dctx_ref[...]) + dot(place[:, CELLS:], slabs)).astype(BF)
    moves.need(qkv_ref, one_ref)
    attend_back_pairs(0, qkv_ref, one_ref, dctxp_ref, dqkv_ref, dtable_ref)
    moves.need(two_ref)
    attend_back_pairs(PADDED // 2, qkv_ref, two_ref, dctxp_ref, dqkv_ref, dtable_ref)
    moves.ship(dqkv_ref)
    moves.need(w_ref)
    table_sum(dtable_ref, key_ref, table_ref)
    for s in range(3):
        dbias_ref[s : s + 1, :] = jnp.sum(dqkv_ref[:, s * D : (s + 1) * D].astype(F32), 0, keepdims=True)
    dhp = dot_nt(dqkv_ref[:, :D], block(w_ref, 0))
    for s in range(1, 3):
        dhp = dhp + dot_nt(dqkv_ref[:, s * D : (s + 1) * D], block(w_ref, s))
    dhp_ref[...] = dhp.astype(BF)
    moves.ship(dhp_ref)
    moves.need(take_ref)
    sent = dot(take_ref[...], dhp_ref[...]).astype(BF)
    rows_out[...] = sent[:SLAB]
    cols_out[...] = sent[SLAB : 2 * SLAB]
    corner_out[...] = sent[2 * SLAB :]


def grads_heads_kernel(moves, coords_ref, hp_ref, dqkv_ref, keep_ref, send_ref):
    moves.need(hp_ref)
    for s in range(3):
        moves.need(dqkv_ref, part=s)
        for half in range(2):
            rows = slice(half * 256, half * 256 + 256)
            grad_w = dot_tn(hp_ref[:, rows], dqkv_ref[:, s * D : (s + 1) * D])
            store_grad(coords_ref, keep_ref, send_ref, s, half, grad_w)
        moves.ship(keep_ref, of_blocks(s))
        moves.ship(send_ref, of_blocks(s))


def attend_back_end_kernel(moves, *refs):
    coords_ref, dctxp_ref, qkv_ref, one_ref, two_ref, hp_ref, dwp_ref, key_ref, w_ref, place_ref = refs[:10]
    x_ref, dmid_ref, g1_ref, norm1, dqb1, sums1, dbh1, table1, sums0, dbo0, dbh0 = refs[10:21]
    keep_ref, send_ref, out_ref, sums_ref, dqkv_ref, dtable_ref, dhp_ref = refs[21:]
    moves.need(dctxp_ref, qkv_ref, one_ref)
    attend_back_pairs(0, qkv_ref, one_ref, dctxp_ref, dqkv_ref, dtable_ref)
    moves.need(two_ref)
    attend_back_pairs(PADDED // 2, qkv_ref, two_ref, dctxp_ref, dqkv_ref, dtable_ref)
    moves.need(hp_ref)
    dqb = []
    for s in range(3):
        wide = slice(s * D, (s + 1) * D)
        dqb.append(jnp.sum(dqkv_ref[:, wide].astype(F32), 0, keepdims=True))
        for half in range(2):
            rows = slice(half * 256, half * 256 + 256)
            grad_w = dot_tn(hp_ref[:, rows], dqkv_ref[:, wide])
            store_grad(coords_ref, keep_ref, send_ref, s, half, grad_w)
    moves.need(dwp_ref)
    for half in range(2):
        store_grad(coords_ref, keep_ref, send_ref, 3, half, dwp_ref[half * 256 : half * 256 + 256, :])
    moves.ship(keep_ref)
    moves.ship(send_ref)
    moves.need(w_ref)
    dhp = dot_nt(dqkv_ref[:, :D], block(w_ref, 0))
    for s in range(1, 3):
        dhp = dhp + dot_nt(dqkv_ref[:, s * D : (s + 1) * D], block(w_ref, s))
    dhp_ref[...] = dhp.astype(BF)
    moves.need(place_ref, x_ref, dmid_ref)
    dh = dot(place_ref[...], dhp_ref[...])
    dx, dg1, db1 = norm_back(dh, x_ref[...].astype(F32), g1_ref[...])
    out_ref[...] = dmid_ref[...] + dx
    moves.ship(out_ref)
    for at, norm, query, value, sums, dbo, dbh in (
        (0, (dg1, db1), dqb[0], dqb[2], sums0, dbo0[...], dbh0),
        (12, (norm1[0:1, :], norm1[1:2, :]), dqb1[0:1, :], dqb1[2:3, :], sums1, sums1[3:4, :], dbh1),
    ):
        rows = [*norm, query, value, sums[0:1, :], sums[1:2, :], sums[2:3, :], dbo]
        rows += [dbh[:, D * b : D * b + D] for b in range(4)]
        for i, row in enumerate(rows):
            sums_ref[at + i : at + i + 1, :] = row
    table_sum(dtable_ref, key_ref, sums_ref.at[24:40, 0:256])
    sums_ref[24:40, 256:512] = table1[...]


def add_kernel(*refs):
    out_ref, at = refs[-1], 0
    for i in range(0, len(refs) - 1, 2):
        n = refs[i].shape[2]
        total = refs[i][...].astype(F32) + refs[i + 1][...].astype(F32)
        out_ref[:, :, at : at + n] = total.astype(BF)
        at += n


def sum_split_kernel(coords_ref, parts_ref, *outs):
    for d, out in enumerate(outs):
        target = lax.rem(coords_ref[1] + d, 4)
        total = parts_ref[0, target].astype(F32)
        for k in range(1, 4):
            total = total + parts_ref[k, target].astype(F32)
        out[...] = total.astype(BF)


def to_xz_kernel(coords_ref, keep_ref, other_ref, parts_ref, sums_ref, more_ref, near_ref, *outs):
    smalls = jnp.concatenate([sums_ref[...] + more_ref[...], jnp.zeros((8, D), F32)], 0)
    high = smalls.astype(BF).astype(F32)
    low = smalls - high
    for z in range(4):
        for x in range(4):
            total = keep_ref[z, x].astype(F32) + other_ref[z, x].astype(F32)
            near_ref[4 * z + x, 0:4] = total.astype(BF)
            at = 3 * (4 * z + x)
            rows = [high[at : at + 3], low[at : at + 3], jnp.zeros((10, D), F32)]
            near_ref[4 * z + x, 4] = jnp.concatenate(rows, 0).astype(BF)
    for d, out in enumerate(outs):
        target = lax.rem(coords_ref[1] + d, 4)
        total = parts_ref[0, target].astype(F32)
        for k in range(1, 4):
            total = total + parts_ref[k, target].astype(F32)
        out[...] = total.astype(BF)


def to_seq_kernel(near_ref, *refs):
    pieces, late_ref, small_ref = refs[:4], refs[4], refs[5]
    total = near_ref[0].astype(F32)
    for i in range(1, 16):
        total = total + near_ref[i].astype(F32)
    late_ref[0:4] = total[0:4].astype(BF)
    rows = total[4, 0:3] + total[4, 3:6]
    rows = [rows[r : r + 1, 128 * q : 128 * q + 128] for r in range(3) for q in range(4)]
    rows = jnp.concatenate(rows + [jnp.zeros((4, 128), F32)], 0)
    for i in range(64):
        small_ref[i] = rows
    total = pieces[0][...].astype(F32)
    for piece in pieces[1:]:
        total = total + piece[...].astype(F32)
    late_ref[4:15] = total.astype(BF)


def four(refs, b):
    return (refs[0][b].astype(F32) + refs[1][b].astype(F32)) + (refs[2][b].astype(F32) + refs[3][b].astype(F32))


def reorder(values, order):
    n = values.shape[0]
    high = values.astype(BF)
    rest = values - high.astype(F32)
    low = rest.astype(BF)
    last = (rest - low.astype(F32)).astype(BF)
    rows = dot_nt(jnp.concatenate([high, low, last], 0), order)
    return rows[:n] + rows[n : 2 * n] + rows[2 * n :]


def step_into(at, grad, old, new, rate, decay):
    weight, first, second = (ref[at] for ref in old)
    for ref, value in zip(new, adamw(weight, first, second, grad, rate, decay)):
        ref[at] = value


def update_small_kernel(*refs):
    smalls_ref, units_ref, small, table = refs[0], refs[1], refs[2:5], refs[5:8]
    new_small, new_table, bias_ref, sums_ref = refs[8:11], refs[11:14], refs[14], refs[15]
    for i in range(16):
        part = (smalls_ref[4 * i] + smalls_ref[4 * i + 1]) + (smalls_ref[4 * i + 2] + smalls_ref[4 * i + 3])
        for k in range(12):
            sums_ref[3 * i + k // 4 : 3 * i + k // 4 + 1, k % 4 * 128 : k % 4 * 128 + 128] = part[k : k + 1]
    for layer in range(LAYERS):
        rows = [sums_ref[12 * layer + i : 12 * layer + i + 1, :] for i in range(12)]
        bias_ref[layer : layer + 1, :] = rows[7]
        parts = [
            jnp.concatenate([rows[8 + b][:, 128 * g : 128 * g + 128] for b in range(4)], 1) for g in range(GROUPS)
        ]
        units = reorder(jnp.concatenate(parts + [jnp.zeros((12, D), F32)], 0), units_ref[...])
        for i, grad in enumerate(rows[:8] + [units[g : g + 1] for g in range(GROUPS)]):
            at = (slice(layer, layer + 1), slice(D * i, D * i + D))
            step_into(at, grad, small, new_small, 0.3, 0.0)
        step_into((layer,), sums_ref[24:40, 256 * layer : 256 * layer + REL], table, new_table, 0.6, 0.0)


def reordered_steps(pieces, at, n, order_ref, old, new):
    wide = order_ref.shape[0]
    grads = [four(pieces, at + b) for b in range(n)]
    for g in range(GROUPS):
        part = jnp.concatenate([v[:, 128 * g : 128 * g + 128] for v in grads], 1)
        lanes = (0, slice(None), slice(wide * g, wide * g + wide))
        step_into(lanes, reorder(part, order_ref[...]), old, new, 0.03, 0.05)


def rest_steps(pieces, at, units_ref, old, new):
    step_into((0,), four(pieces, at), old[0:3], new[0:3], 0.1, 0.05)
    for b in range(4):
        step_into((0, slice(16 * b, 16 * b + 16)), four(pieces, at + 5 + b), old[6:9], new[6:9], 0.03, 0.05)
    reordered_steps(pieces, at + 1, 4, units_ref, old[3:6], new[3:6])


def update_early_kernel(*refs):
    rest_steps(refs[:4], 0, refs[4], refs[5:14], refs[14:])


def update_kernel(*refs):
    late, heads_ref, units_ref, old, new = refs[9:13], refs[13], refs[14], refs[15:27], refs[27:]

    @pl.when(pl.program_id(0) == 0)
    def _():
        reordered_steps(late, 0, 3, heads_ref, old[:3], new[:3])
        rest_steps(late, 3, units_ref, old[3:], new[3:])

    @pl.when(pl.program_id(0) == 1)
    def _():
        reordered_steps(late, 12, 3, heads_ref, old[:3], new[:3])


def to_neighbours(slabs, ahead):
    step = -1 if ahead else 1
    along = [(i, (i + step) % 4) for i in range(4)]
    over = [(0, 1), (1, 0)]
    both = [(i * 2 + c, ((i + step) % 4) * 2 + 1 - c) for i in range(4) for c in range(2)]
    rows, cols, corner = slabs
    return (
        lax.ppermute(rows, "seq", along),
        lax.ppermute(cols, "col", over),
        lax.ppermute(corner, ("seq", "col"), both),
    )


def flat(z, x, core):
    return (z * 4 + (x % 2) * 2 + core) * 2 + x // 2


ALONG_X = [[flat(z, x, core) for x in range(4)] for z in range(4) for core in range(2)]
OVER_XZ = [[flat(z, x, core) for z in range(4) for x in range(4)] for core in range(2)]
OVER_CHIPS = [[i * 4 + y for i in group for y in range(4)] for group in OVER_XZ]
OTHER_CORE = [(i, i ^ 1) for i in range(16)]


def from_z(distance):
    return [(((z + distance) % 4) * 4 + k, z * 4 + k) for z in range(4) for k in range(4)]


def from_x(distance):
    return [(flat(z, (x + distance) % 4, c), flat(z, x, c)) for z in range(4) for x in range(4) for c in range(2)]


ALONG_Z = [[z * 4 + k for z in range(4)] for k in range(4)]


def scattered_z(value):
    return lax.all_to_all(value, "img", 0, 0, tiled=True, axis_index_groups=ALONG_Z)


def from_core(value):
    return lax.ppermute(value, "img", OTHER_CORE)


BY_SEQ = [[(i, i ^ d) for i in range(4)] for d in (1, 2, 3)]
BY_Z = [[(z * 4 + k, (z ^ d) * 4 + k) for z in range(4) for k in range(4)] for d in (1, 2, 3)]
def both_cores(*pairs):
    arrays = [a for pair in pairs for a in pair]
    specs = [pl.BlockSpec((1, *a.shape[1:]), lambda i: (i, 0, 0, 0, 0)) for a in arrays]
    shape = (4, 4, sum(keep.shape[2] for keep, _ in pairs), 16, D)
    size = math.prod(shape) * 2
    return pl.pallas_call(
        add_kernel,
        grid=(4,),
        out_shape=jax.ShapeDtypeStruct(shape, BF),
        in_specs=specs,
        out_specs=pl.BlockSpec((1, *shape[1:]), lambda i: (i, 0, 0, 0, 0)),
        compiler_params=pltpu.CompilerParams(vmem_limit_bytes=VMEM_BYTES),
        cost_estimate=pl.CostEstimate(flops=size, bytes_accessed=3 * size, transcendentals=0),
    )(*arrays)


def by_seq(value):
    return [value] + [lax.ppermute(value, "seq", p) for p in BY_SEQ]


def update(early, late, heads, units, state):
    inside, anywhere = pl.BlockSpec(memory_space=pltpu.VMEM), pl.BlockSpec(memory_space=pl.ANY)
    rest = state[3:]
    second = [pl.BlockSpec((1, *a.shape[1:]), lambda _: (1, 0, 0)) for a in rest]
    first = [pl.BlockSpec((1, *a.shape[1:]), lambda _: (0, 0, 0)) for a in rest]
    both = [pl.BlockSpec((1, *a.shape[1:]), lambda layer: (layer, 0, 0)) for a in state[:3]]
    done = pl.pallas_call(
        update_early_kernel,
        grid=(1,),
        out_shape=[jax.ShapeDtypeStruct(a.shape, F32) for a in rest],
        in_specs=[inside] * 5 + second,
        out_specs=second,
        compiler_params=pltpu.CompilerParams(vmem_limit_bytes=VMEM_BYTES),
        cost_estimate=pl.CostEstimate(flops=4 * 10**9, bytes_accessed=4 * 10**6, transcendentals=0),
    )(*early, units, *rest)
    return pl.pallas_call(
        update_kernel,
        grid=(LAYERS,),
        out_shape=[jax.ShapeDtypeStruct(a.shape, F32) for a in state],
        in_specs=[anywhere] * 9 + [inside] * 6 + both + first,
        out_specs=both + first,
        input_output_aliases={i: 3 + i for i in range(9)},
        compiler_params=pltpu.CompilerParams(vmem_limit_bytes=VMEM_BYTES),
        cost_estimate=pl.CostEstimate(flops=8 * 10**9, bytes_accessed=8 * 10**6, transcendentals=0),
    )(*done, *late, heads, units, *state)


def adamw(weight, first, second, grad, rate, decay):
    first = 0.9 * first + 0.1 * grad
    second = 0.999 * second + 0.001 * grad * grad
    first_hat = first / (1.0 - 0.9**STEP)
    second_hat = second / (1.0 - 0.999**STEP)
    return (first, second, weight - rate * (first_hat / (jnp.sqrt(second_hat) + 1e-08) + decay * weight))


def hidden_order(vector):
    return vector.reshape(32, 4, 16).transpose(1, 0, 2).reshape(HIDDEN)


def split_small(vector):
    pieces = [vector[i * D : (i + 1) * D][None] for i in range(8)]
    return pieces + [hidden_order(vector[8 * D :])[None]]


def score_table(table, hot):
    rows = lax.dot_general(table, hot, (((0,), (0,)), ((), ())), precision=highest, preferred_element_type=F32)
    rows = rows.reshape(HEADS, AREA, AREA) * log2e
    rows = jnp.pad(rows, ((0, 0), (0, 0), (0, SLOT - AREA)))
    rows = jnp.pad(rows, ((0, 0), (0, SLOT - AREA), (0, 0)), constant_values=padded_score)
    return jnp.concatenate([rows, rows], 2).reshape(HEADS * SLOT, 128)


def allowed_pairs(region):
    win = region.reshape(4, WIN, 4, WIN).transpose(0, 2, 1, 3).reshape(16, AREA)
    win = jnp.pad(win, ((0, 0), (0, SLOT - AREA)))
    same = win[:, :, None] == win[:, None, :]
    same = same | (jnp.arange(SLOT) >= AREA)[None, :, None]
    same = same.reshape(PAIRS, 2, SLOT, SLOT).transpose(0, 2, 1, 3).reshape(PAIRS, SLOT, 128)
    return same.astype(F32)


def local(
    images,
    out_grad,
    region_ids,
    rel_index,
    qkv_weight,
    qkv_first,
    qkv_second,
    proj_weight,
    proj_first,
    proj_second,
    expand_weight,
    expand_first,
    expand_second,
    contract_weight,
    contract_first,
    contract_second,
    small_params,
    small_first,
    small_second,
    bias_table,
    table_first,
    table_second,
):
    plain, plain_back, ahead, back, take_first, take_last = (jnp.asarray(a, BF) for a in placements())
    heads, units = (jnp.asarray(a, BF) for a in column_orders())
    img = lax.axis_index("img")
    x = lax.axis_index("col") * 2 + img // 2 % 2
    coords = jnp.stack([img // 4, x, img % 2]).astype(jnp.int32)
    matrices = (qkv_weight, proj_weight, expand_weight, contract_weight, heads, units)
    one, two = call(pack_kernel, [((4, 6, 16, D), BF), ((6, 16, D), BF)], matrices, us=3)

    def along_z(value):
        return [value] + [lax.ppermute(value, "img", from_z(d)) for d in (1, 2, 3)]

    def along_x(value):
        return [value] + [lax.ppermute(value, ("img", "col"), from_x(d)) for d in (1, 2, 3)]

    one0 = lax.all_to_all(one, ("img", "col"), 0, 0, tiled=True, axis_index_groups=ALONG_X)
    two0 = along_z(two)
    x0 = images.reshape(CELLS, D)
    g_out = out_grad.reshape(CELLS, D)
    by_key = jnp.pad(rel_index.T, ((0, 1), (0, SLOT - AREA)), constant_values=-1)
    by_key = jnp.concatenate([by_key, by_key], 1).reshape(25, 256)
    keys_hot = (jnp.arange(REL, dtype=jnp.int32)[:, None] == rel_index.T.reshape(1, AREA * AREA)).astype(F32)
    tables = [score_table(bias_table[layer], keys_hot) for layer in range(LAYERS)]
    region = lax.dynamic_slice_in_dim(region_ids, lax.axis_index("seq") * SIDE, SIDE, 0)
    mask = allowed_pairs(region)
    small = [split_small(small_params[layer]) for layer in range(LAYERS)]
    zero = jnp.zeros((1, D), F32)
    qkv_bias = [jnp.concatenate([s[2], zero, s[3]], 1) for s in small]

    by_columns = [columns(b) for b in range(4)]
    qkv_shape = ((PADDED, 3 * D), BF)
    attn_shape = ((PAIRS // 2, GROUPS, 256, 128), BF)
    slab_shapes = [((SLAB, D), BF), ((SLAB, D), BF), ((CORNER, D), BF)]
    cells16, cells32 = ((CELLS, D), BF), ((CELLS, D), F32)
    padded16 = ((PADDED, D), BF)
    wide16 = ((CELLS, HIDDEN), BF)

    copies = pltpu.SemaphoreType.DMA((32,))
    w_shapes = [((3, 32, 16, D), BF), ((9, 32, 16, D), BF)]
    g1, b1, _, _, bp, g2, b2, bo, bh = small[0]
    (hp0,) = call(enter_kernel, [padded16], (x0, g1, b1, plain), us=4)
    (two0,) = call(stack_kernel, [((4, 6, 16, D), BF)], two0, after=(hp0,))
    one0, two0 = along_z(one0), along_x(two0)
    one0 = one0 + [from_core(v) for v in one0]
    two0 = two0 + [from_core(v) for v in two0]
    half16 = ((PADDED // 2, D), BF)
    wq0, qkv0, attn0, attn0b, ctx0 = call(
        functools.partial(attend_kernel, False),
        [w_shapes[0], qkv_shape, attn_shape, attn_shape, cells16],
        (hp0, qkv_bias[0], tables[0], plain_back),
        [pltpu.VMEM(*padded16), copies],
        one0,
        coords,
        us=18,
        late=dict.fromkeys((0, 2, 3)),
        early=(0, 1, 2, 3),
    )
    spread, rest = call(
        pack_next_kernel, [((16, 3, 16, D), BF), ((9, 16, D), BF)], matrices, us=3, after=(ctx0,)
    )
    lines = lax.all_to_all(spread, ("img", "col"), 0, 0, tiled=True, axis_index_groups=OVER_XZ)
    one1 = [lines, from_core(lines)]
    wm0, mid0, h20, hidden0, slope0, x1, h1, *slabs = call(
        forward_kernel,
        [w_shapes[1], cells32, cells16, wide16, wide16, cells32, cells16, *slab_shapes],
        (x0, ctx0, bp, g2, b2, bo, bh, small[1][0], small[1][1], take_first),
        [pltpu.SemaphoreType.DMA((64,))],
        one0 + two0,
        coords,
        us=15,
        after=(spread, rest),
        late=dict.fromkeys((1, 0, 9)),
        early=(0, 1, 2, 3, 4, 5, 6),
    )
    (lines,) = call(stack_spread_kernel, [((4, 4, 9, 16, D), BF)], along_x(rest), us=2, after=(h1,))
    two1 = scattered_z(lines).reshape(16, 9, 16, D)
    g1, b1, _, _, bp, g2, b2, bo, bh = small[1]
    slabs = to_neighbours(slabs, True)
    wq1, hp1, qkv1, attn1, attn1b, ctxp1, *slabs = call(
        functools.partial(attend_kernel, True),
        [w_shapes[0], padded16, qkv_shape, attn_shape, attn_shape, padded16, *slab_shapes],
        (h1, *slabs, ahead, qkv_bias[1], tables[1], mask, take_last),
        [copies],
        one1,
        coords,
        us=18,
        after=(by_key,),
        late=dict.fromkeys((4, 0, 6, 7, 8)),
        early=(0, 1, 2, 3, 4, 5),
    )
    (two1,) = held((two1,), (hp1,))
    two1 = [two1, from_core(two1)]
    slabs = to_neighbours(slabs, False)
    out, dmid1, sums1, dbh1, dctx1, *slabs, keep, send = call(
        turn_kernel,
        [cells16, cells32, ((4, D), F32), ((1, HIDDEN), F32), cells16, *slab_shapes, *[((4, 4, 9, 16, D), BF)] * 2],
        (x1, ctxp1, *slabs, back, bp, g2, b2, bo, bh, g_out, take_first),
        [pltpu.VMEM(*a) for a in (w_shapes[1], cells16, cells32, cells16, wide16, wide16, wide16, cells16)] + [copies],
        two1,
        coords,
        us=34,
        late=dict.fromkeys((5, 1, 0, 11, 12)),
        early=(0, 1, 4, 8, 9),
    )
    slabs = to_neighbours(slabs, True)
    part_m1 = both_cores((keep, from_core(send)))
    dqkv1, dqb1, table1, dhp1, *slabs = call(
        attend_back_kernel,
        [qkv_shape, ((3, D), F32), ((HEADS, 256), F32), padded16, *slab_shapes],
        (dctx1, *slabs, ahead, qkv1, attn1, attn1b, wq1, take_last, by_key),
        [pltpu.VMEM((PADDED, D), BF), pltpu.VMEM((HEADS * SLOT, 128), F32)],
        us=20,
        after=(part_m1,),
        late=dict.fromkeys((4, 0, 5, 6, 7, 8, 9)),
        early=(0, 3),
    )
    slabs = to_neighbours(slabs, False)
    keep, send = call(
        grads_heads_kernel,
        [((4, 4, 3, 16, D), BF)] * 2,
        (hp1, dqkv1),
        place=coords,
        us=4,
        late={0: None, 1: by_columns[:3]},
        early=(0, 1),
    )
    pair_q1 = (keep, from_core(send))
    half_m1, *sent = call(sum_split_kernel, [((9, 16, D), BF)] * 4, (scattered_z(part_m1),), place=coords, us=2)
    grad1, dpre0, keep, send, dbo0, dbh0, norm1 = call(
        back_first_kernel,
        [cells32, wide16, *[((4, 4, 8, 16, D), BF)] * 2, ((1, D), F32), ((1, HIDDEN), F32), ((2, D), F32)],
        (dmid1, dhp1, *slabs, back, x1, small[1][0], hidden0, slope0, h20, wm0),
        [pltpu.VMEM((CELLS, D), BF)],
        place=coords,
        us=16,
        after=(half_m1, pair_q1[0]),
        late={5: None, 1: None, 6: None, 0: None, 11: [slice(5, 9)], 9: by_columns, 8: by_columns, 10: None},
        early=(0, 1, 2, 3),
    )
    got = [lax.ppermute(v, ("img", "col"), from_x(4 - d)) for d, v in zip((1, 2, 3), sent)]
    grad_m1 = sum((v.astype(F32) for v in got), half_m1.astype(F32)).astype(BF)
    dmid0, dwp0, sums0, dctxp0 = call(
        middle_first_kernel,
        [cells32, ((D, D), BF), ((3, D), F32), padded16],
        (grad1, dpre0, mid0, ctx0, wm0, small[0][5], plain),
        [pltpu.VMEM((CELLS, D), BF)],
        us=8,
        after=(grad_m1,),
        late={4: (0, 5), 1: by_columns, 2: None, 0: None, 3: None, 6: None},
        early=(0, 1),
    )
    part_0 = both_cores((keep, from_core(send)), pair_q1)
    grads_m1 = by_seq(grad_m1)
    half_0 = scattered_z(part_0)
    *keep_send, input_grad, sums = call(
        attend_back_end_kernel,
        [*[((4, 4, 4, 16, D), BF)] * 2, cells32, ((40, D), F32)],
        (dctxp0, qkv0, attn0, attn0b, hp0, dwp0, by_key, wq0, plain_back, x0, dmid0, small[0][0])
        + (norm1, dqb1, sums1, dbh1, table1, sums0, dbo0, dbh0),
        [pltpu.VMEM(*qkv_shape), pltpu.VMEM((HEADS * SLOT, 128), F32), pltpu.VMEM(*padded16)],
        place=coords,
        us=26,
        late=dict.fromkeys((0, 1, 2, 3, 4, 5, 7, 8, 9, 10)),
        early=(0, 1, 2),
        after=(part_0, *grads_m1),
    )
    other, more = from_core(keep_send[1]), from_core(sums)
    near, mine, *sent = call(
        to_xz_kernel,
        [((16, 5, 16, D), BF)] + [((11, 16, D), BF)] * 4,
        (keep_send[0], other, half_0, sums, more),
        place=coords,
        us=5,
    )
    near = lax.all_to_all(near, ("img", "col"), 0, 0, tiled=True, axis_index_groups=OVER_XZ)
    pieces = [mine] + [lax.ppermute(v, ("img", "col"), from_x(4 - d)) for d, v in zip((1, 2, 3), sent)]
    late, smalls = call(to_seq_kernel, [((15, 16, D), BF), ((64, 16, 128), F32)], (near, *pieces), us=3)
    late = by_seq(late)
    smalls = lax.all_to_all(smalls, ("img", "col", "seq"), 0, 0, tiled=True, axis_index_groups=OVER_CHIPS)

    state = (
        (qkv_weight, qkv_first, qkv_second),
        (proj_weight, proj_first, proj_second),
        (expand_weight, expand_first, expand_second),
        (contract_weight, contract_first, contract_second),
    )
    flat_state = [a for three in state for a in three]
    swap = functools.partial(jnp.transpose, axes=(0, 2, 1))
    small = (small_params, small_first, small_second, swap(bias_table), swap(table_first), swap(table_second))
    done = update(grads_m1, late, heads, units, flat_state)
    last = call(
        update_small_kernel,
        [(a.shape, F32) for a in small] + [((LAYERS, D), F32)],
        (smalls, units, *small),
        [pltpu.VMEM((48, D), F32)],
        us=3,
    )
    return (
        out.reshape(images.shape),
        input_grad.reshape(images.shape),
        *done,
        *last[:3],
        *(swap(a) for a in last[3:6]),
        last[6],
    )


def solution(mesh):
    cells = P("img", "seq", "col", None)
    matrix = P(None, ("img", "col"), None)
    in_specs = (cells, cells, P(None, "col"), P(), *([matrix] * 12), *([P()] * 6))
    out_specs = (cells, cells, *([matrix] * 12), *([P()] * 7))
    return jax.shard_map(local, mesh=mesh, in_specs=in_specs, out_specs=out_specs, check_vma=False)
```
